512 devices in a mesh: row: 64 (over y, z_hi, x, core), col: 8 (over z_lo).
Axes of the slice: x: 4, y: 4, z: 16 (z_hi: 2, z_lo: 8; z = z_hi * 8 + z_lo), core: 2. Of those that a mesh axis runs over, the one named last changes fastest.
Arguments:
- queries: bfloat16 [8192, 8192], P('row'), may hold values from -18 to 18
- keys: bfloat16 [8192, 512], P(('row', 'col')), may hold values from -18 to 18
- values: bfloat16 [8192, 512], P(('row', 'col')), may hold values from -6 to 6
- order: int32 [8192], P(('row', 'col')), may hold values from 0 to 8191, as said below
Outputs:
- attended: bfloat16 [8192, 8192], P(('row', 'col'))
The draws below stay inside these ranges and needn't reach their ends.
Inputs may be any that keep to these rules, and one draw needn't show every extreme that they name: `order`: each device's 16 entries are consecutive increasing positions; every position of the sequence appears once.
All inputs are finite; a program needn't handle non-finite values.
Results may differ from the reference program's by a relative error of at most 0.03.
Values may be sent and summed in bfloat16 or wider, within the bound.
A program may use at most 64 MiB of HBM per device.

```python
import jax
import jax.numpy as jnp
from jax import lax

HD = 128
KVH = 4
GROUP = 16
TOK_DEV = 16
TOKENS = 8192
N_ROW = 64
N_COL = 8


def shared_directions(key):
    return jnp.clip(jax.random.normal(key, (TOKENS, KVH * HD), jnp.float32), -3.0, 3.0)


def draw_keys(key, part):
    directions = shared_directions(key)
    result = directions
    return result.astype(jnp.bfloat16)


def draw_queries(key, part):
    key = jax.random.fold_in(key, 2)
    result = 1.5 * jnp.clip(jax.random.normal(key, (TOKENS, KVH * GROUP * HD), jnp.float32), -4.0, 4.0)
    return result.astype(jnp.bfloat16)


def draw_order(key, part):
    key = jax.random.fold_in(key, 3)
    block_count = TOKENS // TOK_DEV
    shuffled = jax.random.permutation(key, block_count).astype(jnp.int32)
    tokens_index = jnp.arange(TOKENS, dtype=jnp.int32)
    return (shuffled[tokens_index // TOK_DEV] * TOK_DEV + tokens_index % TOK_DEV).astype(jnp.int32)


def level_of(own_key, dims, shards, least, top_value):
    level = 1.0
    for axis_at, shards_of in shards:
        heights = jax.random.uniform(jax.random.fold_in(jax.random.fold_in(own_key, 6), axis_at), (shards_of,), jnp.float32, least / len(shards), top_value / len(shards))
        level = level * jnp.repeat(jnp.exp(heights), dims[axis_at] // shards_of).reshape((-1,) + (1,) * (len(dims) - 1 - axis_at))
    return level


def gaussian(key, dims, scale, bound, pieces=(), kind=jnp.bfloat16):
    level = level_of(key, dims, pieces, -0.22, 0.18) if pieces else 1.0
    values = jax.random.normal(key, dims, jnp.float32) * scale * level
    return jnp.minimum(jnp.maximum(values, -bound), bound).astype(kind)


def setup_inputs(seed: int = 0) -> dict:
    streams_of = jax.random.split(jax.random.key(seed), 5)
    queries = draw_queries(jax.random.fold_in(streams_of[4], 71), 0)
    keys = draw_keys(jax.random.fold_in(streams_of[4], 71), 0)
    values = gaussian(streams_of[2], (TOKENS, KVH * HD), 1.5, 6.0, ((0, 512),))
    order = draw_order(jax.random.fold_in(streams_of[4], 71), 0)
    return dict(queries=queries, keys=keys, values=values, order=order)


def tile_part(query_block, query_pos, key_block, value_block, key_pos):
    score_scale = HD ** -0.5
    scores = jnp.einsum('qgrd,kgd->grqk', query_block.astype(jnp.float32), key_block.astype(jnp.float32)) * score_scale
    visible = key_pos[None, :] <= query_pos[:, None]
    scores = jnp.where(visible, scores, -1e30)
    largest = scores.max(-1)
    raised = jnp.where(visible, jnp.exp(scores - largest[..., None]), 0.0)
    denominator = raised.sum(-1)
    probs = lax.optimization_barrier(raised.astype(jnp.bfloat16)).astype(jnp.float32)
    numerator = jnp.einsum('grqk,kgd->qgrd', probs, value_block.astype(jnp.float32))
    has_key = largest > -1e29
    safe_total = jnp.where(has_key, denominator, 1.0)
    key_mask = jnp.transpose(has_key, (2, 0, 1))
    part = jnp.where(key_mask[..., None], numerator / jnp.transpose(safe_total, (2, 0, 1))[..., None], 0.0)
    log_total = jnp.where(key_mask, jnp.transpose(largest + jnp.log(safe_total), (2, 0, 1)), -1e30)
    return part.astype(jnp.bfloat16), log_total


def reference(queries, keys, values, order):
    query_blocks = queries.reshape(N_ROW, N_COL * TOK_DEV, KVH, GROUP, HD)
    key_groups = jnp.transpose(keys.reshape(N_ROW, N_COL, TOK_DEV, KVH, HD), (1, 0, 2, 3, 4)).reshape(N_COL, N_ROW * TOK_DEV, KVH, HD)
    value_groups = jnp.transpose(values.reshape(N_ROW, N_COL, TOK_DEV, KVH, HD), (1, 0, 2, 3, 4)).reshape(N_COL, N_ROW * TOK_DEV, KVH, HD)
    position_grid = order.reshape(N_ROW, N_COL, TOK_DEV)
    query_positions = position_grid.reshape(N_ROW, N_COL * TOK_DEV)
    key_positions = jnp.transpose(position_grid, (1, 0, 2)).reshape(N_COL, N_ROW * TOK_DEV)

    def row_block(inputs):
        query_block, query_pos = inputs
        parts, logs = lax.map(lambda group: tile_part(query_block, query_pos, group[0], group[1], group[2]), (key_groups, value_groups, key_positions))
        largest = logs.max(0)
        shares = jnp.exp(logs - largest)
        shares = shares / shares.sum(0)
        merged = jnp.sum(shares[..., None] * parts.astype(jnp.float32), axis=0)
        return merged.reshape(merged.shape[0], KVH * GROUP * HD).astype(jnp.bfloat16)

    attended = lax.map(row_block, (query_blocks, query_positions))
    return attended.reshape(TOKENS, KVH * GROUP * HD)
```

```python
import math

import jax
import jax.numpy as jnp
from jax import lax
from jax.experimental import pallas as pl
from jax.experimental.pallas import tpu as pltpu
from jax.sharding import PartitionSpec as P

HD = 128
KVH = 4
GROUP = 16
TOK = 16
NX, NY, NZ, NLO = 4, 4, 16, 8
QTOK = 64
WIDTH = GROUP * HD
BLOCK = 2 * NZ + 1
KEYS = 2 * NZ * TOK
BF = jnp.bfloat16
F32 = jnp.float32
MASKED = -1e30
RATE = math.log2(math.e) / math.sqrt(HD)

ORDER = [
    (0, 0), (1, 0), (3, 0), (0, 1), (0, 3), (2, 0), (1, 1), (1, 3),
    (3, 1), (3, 3), (0, 2), (2, 1), (2, 3), (1, 2), (3, 2), (2, 2),
]
SLOT = {place: index for index, place in enumerate(ORDER)}
STEP = {"A-": (1, 0), "A+": (-1, 0), "B-": (0, 1), "B+": (0, -1)}
FORWARD = {
    (0, 0): ["A-", "A+", "B-", "B+"],
    (1, 0): ["A-", "B-", "B+"],
    (3, 0): ["B-", "B+"],
    (2, 0): ["B-", "B+"],
    (0, 1): ["B-"],
    (1, 1): ["B-"],
    (2, 3): ["B+"],
    (3, 3): ["B+"],
}
ROUTES = []
for place in ORDER:
    for way in FORWARD.get(place, []):
        da, db = STEP[way]
        ROUTES.append((SLOT[place], way, SLOT[((place[0] + da) % 4, (place[1] + db) % 4)]))


def kernel(
    q_hbm, k_ref, v_ref, order_ref, out_ref,
    mine, theirs, stage, pos_own, pos_line, q_raw, q_t, k_aug, v_rows, v_t, acc, top, out_stage,
    q_sem, z_send, z_recv, p_send, p_recv, f_send, m_recv, c_send, t_recv, o_send, o_recv,
):
    row = lax.axis_index("row")
    col = lax.axis_index("col")
    core = row % 2
    x = (row // 2) % NX
    y = row // (4 * NX)
    z = ((row // (2 * NX)) % 2) * NLO + col
    head = col % KVH
    half = col // KVH

    def device(x_at, y_at, z_at, core_at):
        return (y_at * (4 * NX) + (z_at // NLO) * (2 * NX) + x_at * 2 + core_at, z_at % NLO)

    line = [None] + [device(x, y, (z + d) % NZ, core) for d in range(1, NZ)]
    plane = {}
    for way, (da, db) in STEP.items():
        sx = (1 - core) * da + core * db
        sy = core * da + (1 - core) * db
        plane[way] = device((x - sx + NX) % NX, (y - sy + NY) % NY, z, core)
    twin = device(x, y, z, 1 - core)

    q_copy = pltpu.make_async_copy(
        q_hbm.at[pl.ds(half * QTOK, QTOK), pl.ds(pl.multiple_of(head * WIDTH, WIDTH), WIDTH)],
        q_raw, q_sem,
    )
    q_copy.start()

    barrier = pltpu.get_barrier_semaphore()
    others = line[1:] + list(plane.values()) + [twin]
    for other in others:
        pl.semaphore_signal(barrier, inc=1, device_id=other, device_id_type=pl.DeviceIdType.MESH)

    for g in range(KVH):
        stage[g, 0] = k_ref[:, g * HD:(g + 1) * HD]
        stage[g, 1] = v_ref[:, g * HD:(g + 1) * HD]
    pos_own[...] = jnp.full((1, 128), order_ref[0], jnp.int32)

    pl.semaphore_wait(barrier, len(others))

    def remote(src, dst, send, recv, to):
        return pltpu.make_async_remote_copy(
            src_ref=src, dst_ref=dst, send_sem=send, recv_sem=recv,
            device_id=to, device_id_type=pl.DeviceIdType.MESH,
        )

    line_copies = []
    for n, d in enumerate([8, 7, 9, 6, 10, 5, 11, 4, 12, 3, 13, 2, 14, 1, 15]):
        at = NZ - d
        line_copies.append(remote(
            stage.at[(z + d) % KVH], mine.at[0, pl.ds(2 * at, 2)], z_send.at[n], z_recv, line[d]
        ))
        line_copies.append(remote(
            pos_own, pos_line.at[at], p_send.at[n], p_recv, line[d]
        ))
    for copy in line_copies:
        copy.start()
    mine[0, 0:2] = stage[head]
    pos_line[0] = pos_own[...]

    q_copy.wait()
    for cc in range(4):
        rows = jnp.concatenate(
            [q_raw[cc * TOK:(cc + 1) * TOK, g * HD:(g + 1) * HD] for g in range(GROUP)], axis=0
        )
        q_t[0:HD, cc * 256:(cc + 1) * 256] = rows.T
        token = lax.broadcasted_iota(jnp.int32, (HD, 256), 0)
        lane = lax.broadcasted_iota(jnp.int32, (HD, 256), 1)
        q_t[HD:, cc * 256:(cc + 1) * 256] = jnp.where(
            token == cc * TOK + lane % TOK, 1.0, 0.0
        ).astype(BF)
    v_t[HD:, :] = jnp.ones((TOK, KEYS), BF)
    acc[...] = jnp.zeros_like(acc)
    top[...] = jnp.full_like(top, MASKED)

    pltpu.make_async_copy(pos_line.at[pl.ds(1, NZ - 1)], pos_line.at[pl.ds(1, NZ - 1)], p_recv).wait()
    starts = jnp.concatenate([pos_line[d] for d in range(NZ)], axis=0)
    lane16 = lax.broadcasted_iota(jnp.int32, (TOK, 128), 1)
    mine[0, 2 * NZ] = jnp.where(lane16 < 64, starts // 128, starts % 128).astype(F32).astype(BF)
    lane1 = lax.broadcasted_iota(jnp.int32, (1, 128), 1)
    q_pos = jnp.zeros((1, 128), jnp.int32)
    for cc in range(4):
        q_pos = jnp.where(
            lane1 // TOK == cc, pos_line[(cc - head + NZ) % NZ] + lane1 % TOK, q_pos
        )
    q_pos = q_pos.astype(F32)

    pltpu.make_async_copy(
        mine.at[0, pl.ds(2, 2 * NZ - 2)], mine.at[0, pl.ds(2, 2 * NZ - 2)], z_recv
    ).wait()

    def route(n):
        slot, way, there = ROUTES[n]
        return remote(mine.at[slot], mine.at[there], f_send.at[n], m_recv.at[there], plane[way])

    def to_twin(slot):
        return remote(mine.at[slot], theirs.at[slot], c_send.at[slot], t_recv.at[slot], twin)

    for n in range(len(ROUTES)):
        if ROUTES[n][0] == 0:
            route(n).start()
    to_twin(0).start()

    def prepare(block, slot, base):
        word = block[slot, 2 * NZ].astype(F32)
        turned = pltpu.roll(word, 64, 1)
        start = jnp.where(lane16 < 64, word * 128.0 + turned, turned * 128.0 + word)
        offset = lax.broadcasted_iota(jnp.int32, (TOK, 128), 0).astype(F32)
        for d in range(NZ):
            at = slice(base + d * TOK, base + (d + 1) * TOK)
            k_aug[at, 0:HD] = block[slot, 2 * d]
            k_pos = start[d:d + 1, :] + offset
            k_aug[at, HD:] = jnp.where(k_pos <= q_pos, 0.0, MASKED).astype(BF)
            v_rows[at, :] = block[slot, 2 * d + 1]
        part = slice(base, base + NZ * TOK)
        v_t[0:HD, part] = v_rows[part, :].T

    def step(slot, carry):
        @pl.when(slot < 15)
        def _():
            later = mine.at[slot + 1]
            pltpu.make_async_copy(later, later, m_recv.at[slot + 1]).wait()
            for n in range(len(ROUTES)):
                if ROUTES[n][0] > 0:
                    @pl.when(slot + 1 == ROUTES[n][0])
                    def _():
                        route(n).start()
            to_twin(slot + 1).start()

        prepare(mine, slot, 0)
        pltpu.make_async_copy(theirs.at[slot], theirs.at[slot], t_recv.at[slot]).wait()
        prepare(theirs, slot, NZ * TOK)
        for cc in range(4):
            at = slice(cc * 256, (cc + 1) * 256)
            scores = jnp.dot(k_aug[...], q_t[:, at], preferred_element_type=F32)
            old = top[:, at]
            new = jnp.maximum(old, jnp.max(scores, axis=0, keepdims=True))
            probs = jnp.exp2((scores - new) * RATE).astype(BF)
            acc[:, at] = acc[:, at] * jnp.exp2((old - new) * RATE) + jnp.dot(
                v_t[...], probs, preferred_element_type=F32
            )
            top[:, at] = new
        return carry

    lax.fori_loop(0, 16, step, 0)

    for cc in range(4):
        at = slice(cc * 256, (cc + 1) * 256)
        done = (acc[0:HD, at] / acc[HD:HD + 1, at]).T.astype(BF)
        for g in range(GROUP):
            out_stage[cc, :, g * HD:(g + 1) * HD] = done[g * TOK:(g + 1) * TOK, :]
    columns = pl.ds(pl.multiple_of(head * WIDTH, WIDTH), WIDTH)
    out_copies = []
    for j in (2, 1, 3):
        cc = (head + j) % KVH
        to = device(x, y, (z // KVH) * KVH + cc, core)
        out_copies.append(remote(
            out_stage.at[cc], out_ref.at[:, columns], o_send.at[j], o_recv.at[j], to
        ))
    for copy in out_copies:
        copy.start()
    own = pltpu.make_async_copy(out_stage.at[head], out_ref.at[:, columns], o_send.at[0])
    own.start()
    own.wait()
    for j in (1, 2, 3):
        source = (head - j + KVH) % KVH
        place = out_ref.at[:, pl.ds(pl.multiple_of(source * WIDTH, WIDTH), WIDTH)]
        pltpu.make_async_copy(place, place, o_recv.at[j]).wait()
    for copy in out_copies:
        copy.wait_send()
    for copy in line_copies:
        copy.wait_send()
    for n in range(len(ROUTES)):
        route(n).wait_send()
    for slot in range(16):
        to_twin(slot).wait_send()


def shards(queries, keys, values, order):
    dma = pltpu.SemaphoreType.DMA
    return pl.pallas_call(
        kernel,
        out_shape=jax.ShapeDtypeStruct((TOK, KVH * WIDTH), BF),
        in_specs=[
            pl.BlockSpec(memory_space=pl.ANY),
            pl.BlockSpec(memory_space=pltpu.VMEM),
            pl.BlockSpec(memory_space=pltpu.VMEM),
            pl.BlockSpec(memory_space=pltpu.SMEM),
        ],
        out_specs=pl.BlockSpec(memory_space=pltpu.VMEM),
        scratch_shapes=[
            pltpu.VMEM((16, BLOCK, TOK, HD), BF),
            pltpu.VMEM((16, BLOCK, TOK, HD), BF),
            pltpu.VMEM((KVH, 2, TOK, HD), BF),
            pltpu.VMEM((1, 128), jnp.int32),
            pltpu.VMEM((NZ, 1, 128), jnp.int32),
            pltpu.VMEM((QTOK, WIDTH), BF),
            pltpu.VMEM((2 * HD, 1024), BF),
            pltpu.VMEM((KEYS, 2 * HD), BF),
            pltpu.VMEM((KEYS, HD), BF),
            pltpu.VMEM((HD + TOK, KEYS), BF),
            pltpu.VMEM((HD + TOK, 1024), F32),
            pltpu.VMEM((1, 1024), F32),
            pltpu.VMEM((4, TOK, WIDTH), BF),
            dma, dma((NZ - 1,)), dma, dma((NZ - 1,)), dma,
            dma((len(ROUTES),)), dma((16,)), dma((16,)), dma((16,)), dma((4,)), dma((4,)),
        ],
        compiler_params=pltpu.CompilerParams(
            collective_id=0, has_side_effects=True, vmem_limit_bytes=40 * 1024 * 1024
        ),
        cost_estimate=pl.CostEstimate(
            flops=4 * 1024 * 8192 * 128, bytes_accessed=1 << 20, transcendentals=1024 * 8192
        ),
    )(queries, keys, values, order)


def solution(mesh):
    return jax.shard_map(
        shards,
        mesh=mesh,
        in_specs=(
            P("row", None),
            P(("row", "col"), None),
            P(("row", "col"), None),
            P(("row", "col")),
        ),
        out_specs=P(("row", "col"), None),
        check_vma=False,
    )
```

```python
import math

import jax
import jax.numpy as jnp
from jax import lax
from jax.experimental import pallas as pl
from jax.experimental.pallas import tpu as pltpu
from jax.sharding import PartitionSpec as P

HD = 128
KVH = 4
GROUP = 16
TOK = 16
NX, NY, NZ, NLO = 4, 4, 16, 8
QTOK = 64
WIDTH = GROUP * HD
BLOCK = 2 * 2 * HD + TOK
KEYS = 2 * NZ * TOK
BF = jnp.bfloat16
F32 = jnp.float32
MASKED = -1e30
RATE = math.log2(math.e) / math.sqrt(HD)

ORDER = [
    (0, 0), (1, 0), (3, 0), (0, 1), (0, 3), (2, 0), (1, 1), (1, 3),
    (3, 1), (3, 3), (0, 2), (2, 1), (2, 3), (1, 2), (3, 2), (2, 2),
]
SLOT = {place: index for index, place in enumerate(ORDER)}
STEP = {"A-": (1, 0), "A+": (-1, 0), "B-": (0, 1), "B+": (0, -1)}
FORWARD = {
    (0, 0): ["A-", "A+", "B-", "B+"],
    (1, 0): ["A-", "B-", "B+"],
    (3, 0): ["B-", "B+"],
    (2, 0): ["B-", "B+"],
    (0, 1): ["B-"],
    (1, 1): ["B-"],
    (2, 3): ["B+"],
    (3, 3): ["B+"],
}
ROUTES = []
for place in ORDER:
    for way in FORWARD.get(place, []):
        da, db = STEP[way]
        ROUTES.append((SLOT[place], way, SLOT[((place[0] + da) % 4, (place[1] + db) % 4)]))


def kernel(
    q_hbm, k_hbm, v_hbm, order_hbm, out_ref,
    mine, theirs, stage, landed, order_own, pos_own, pos_line, q_raw, q_t,
    even, odd, peak_even, peak_odd, acc, top, out_stage,
    q_sem, kv_sem, order_sem,
    z_send, z_recv, p_send, p_recv, f_send, m_recv, c_send, t_recv, o_send, o_recv,
):
    row = lax.axis_index("row")
    col = lax.axis_index("col")
    core = row % 2
    x = (row // 2) % NX
    y = row // (4 * NX)
    z = ((row // (2 * NX)) % 2) * NLO + col
    head = col % KVH
    half = col // KVH

    order_copy = pltpu.make_async_copy(order_hbm, order_own, order_sem)
    order_copy.start()
    for g in range(KVH):
        columns = slice(g * HD, (g + 1) * HD)
        pltpu.make_async_copy(k_hbm.at[:, columns], stage.at[g, 0], kv_sem).start()
        pltpu.make_async_copy(v_hbm.at[:, columns], stage.at[g, 1], kv_sem).start()
    q_copy = pltpu.make_async_copy(
        q_hbm.at[pl.ds(half * QTOK, QTOK), pl.ds(pl.multiple_of(head * WIDTH, WIDTH), WIDTH)],
        q_raw, q_sem,
    )
    q_copy.start()

    def device(x_at, y_at, z_at, core_at):
        return (y_at * (4 * NX) + (z_at // NLO) * (2 * NX) + x_at * 2 + core_at, z_at % NLO)

    line = [None] + [device(x, y, (z + d) % NZ, core) for d in range(1, NZ)]
    plane = {}
    for way, (da, db) in STEP.items():
        sx = (1 - core) * da + core * db
        sy = core * da + (1 - core) * db
        plane[way] = device((x - sx + NX) % NX, (y - sy + NY) % NY, z, core)
    twin = device(x, y, z, 1 - core)

    barrier = pltpu.get_barrier_semaphore()
    others = line[1:] + list(plane.values()) + [twin]
    for other in others:
        pl.semaphore_signal(barrier, inc=1, device_id=other, device_id_type=pl.DeviceIdType.MESH)

    order_copy.wait()
    pos_own[...] = jnp.full((1, 128), order_own[0], jnp.int32)
    pltpu.make_async_copy(stage, stage, kv_sem).wait()
    pl.semaphore_wait(barrier, len(others))

    def remote(src, dst, send, recv, to):
        return pltpu.make_async_remote_copy(
            src_ref=src, dst_ref=dst, send_sem=send, recv_sem=recv,
            device_id=to, device_id_type=pl.DeviceIdType.MESH,
        )

    line_copies = []
    for n, d in enumerate([8, 7, 9, 6, 10, 5, 11, 4, 12, 3, 13, 2, 14, 1, 15]):
        at = NZ - d
        line_copies.append(remote(
            stage.at[(z + d) % KVH], landed.at[at], z_send.at[n], z_recv, line[d]
        ))
        line_copies.append(remote(
            pos_own, pos_line.at[at], p_send.at[n], p_recv, line[d]
        ))
    for copy in line_copies:
        copy.start()
    landed[0] = stage[head]
    pos_line[0] = pos_own[...]

    q_copy.wait()
    for cc in range(4):
        rows = jnp.concatenate(
            [q_raw[cc * TOK:(cc + 1) * TOK, g * HD:(g + 1) * HD] for g in range(GROUP)], axis=0
        )
        q_t[0:HD, cc * 256:(cc + 1) * 256] = rows.T
        token = lax.broadcasted_iota(jnp.int32, (HD, 256), 0)
        lane = lax.broadcasted_iota(jnp.int32, (HD, 256), 1)
        q_t[HD:, cc * 256:(cc + 1) * 256] = jnp.where(
            token == cc * TOK + lane % TOK, 1.0, 0.0
        ).astype(BF)
    acc[...] = jnp.zeros_like(acc)
    top[...] = jnp.full_like(top, MASKED)

    pltpu.make_async_copy(pos_line.at[pl.ds(1, NZ - 1)], pos_line.at[pl.ds(1, NZ - 1)], p_recv).wait()
    starts = jnp.concatenate([pos_line[d] for d in range(NZ)], axis=0)
    lane16 = lax.broadcasted_iota(jnp.int32, (TOK, 128), 1)
    mine[0, 4 * HD:] = jnp.where(lane16 < 64, starts // 128, starts % 128).astype(F32).astype(BF)
    lane1 = lax.broadcasted_iota(jnp.int32, (1, 128), 1)
    q_pos = jnp.zeros((1, 128), jnp.int32)
    for cc in range(4):
        q_pos = jnp.where(
            lane1 // TOK == cc, pos_line[(cc - head + NZ) % NZ] + lane1 % TOK, q_pos
        )
    q_pos = q_pos.astype(F32)

    rest = landed.at[pl.ds(1, NZ - 1)]
    pltpu.make_async_copy(rest, rest, z_recv).wait()
    for d in range(NZ):
        mine[0, d * TOK:(d + 1) * TOK] = landed[d, 0]
    for part in range(2):
        values = jnp.concatenate([landed[part * 8 + d, 1] for d in range(8)], axis=0)
        mine[0, (2 + part) * HD:(3 + part) * HD] = values.T

    def route(n):
        slot, way, there = ROUTES[n]
        return remote(mine.at[slot], mine.at[there], f_send.at[n], m_recv.at[there], plane[way])

    def to_twin(slot):
        return remote(mine.at[slot], theirs.at[slot], c_send.at[slot], t_recv.at[slot], twin)

    def wait_mine(slot):
        pltpu.make_async_copy(mine.at[slot], mine.at[slot], m_recv.at[slot]).wait()

    def wait_theirs(slot):
        pltpu.make_async_copy(theirs.at[slot], theirs.at[slot], t_recv.at[slot]).wait()

    def pass_on(slot):
        for n in range(len(ROUTES)):
            if isinstance(slot, int):
                if ROUTES[n][0] == slot:
                    route(n).start()
            elif ROUTES[n][0] > 1:
                @pl.when(slot == ROUTES[n][0])
                def _():
                    route(n).start()
        to_twin(slot).start()

    offset = lax.broadcasted_iota(jnp.int32, (TOK, 128), 0).astype(F32)

    def augmented(block, slot):
        word = block[slot, 4 * HD:].astype(F32)
        turned = pltpu.roll(word, 64, 1)
        start = jnp.where(lane16 < 64, word * 128.0 + turned, turned * 128.0 + word)
        bias = jnp.concatenate(
            [
                jnp.where(start[d:d + 1, :] + offset <= q_pos, 0.0, MASKED).astype(BF)
                for d in range(NZ)
            ],
            axis=0,
        )
        return jnp.concatenate([block[slot, 0:2 * HD], bias], axis=1)

    def keys_of(slot):
        return jnp.concatenate([augmented(mine, slot), augmented(theirs, slot)], axis=0)

    def values_of(slot):
        parts = [
            block[slot, at:at + HD] for block in (mine, theirs) for at in (2 * HD, 3 * HD)
        ]
        return jnp.concatenate(
            [jnp.concatenate(parts, axis=1), jnp.ones((TOK, KEYS), BF)], axis=0
        )

    def score(cc, keys, into, peak):
        scores = jnp.dot(keys, q_t[:, cc * 256:(cc + 1) * 256], preferred_element_type=F32)
        into[cc] = scores
        peak[cc] = jnp.max(scores, axis=0, keepdims=True)

    def absorb(cc, values, source, peak):
        old = top[cc]
        new = jnp.maximum(old, peak[cc])
        probs = jnp.exp2((source[cc] - new) * RATE).astype(BF)
        acc[cc] = acc[cc] * jnp.exp2((old - new) * RATE) + jnp.dot(
            values, probs, preferred_element_type=F32
        )
        top[cc] = new

    def step(slot, source, peak, into, into_peak):
        keys = keys_of(slot + 1)
        values = values_of(slot)
        for cc in range(4):
            score(cc, keys, into, into_peak)
            absorb(cc, values, source, peak)

    pass_on(0)
    wait_mine(1)
    pass_on(1)
    wait_theirs(0)
    keys = keys_of(0)
    for cc in range(4):
        score(cc, keys, even, peak_even)

    def pair(i, carry):
        slot = 2 * i
        wait_mine(slot + 2)
        pass_on(slot + 2)
        wait_theirs(slot + 1)
        step(slot, even, peak_even, odd, peak_odd)
        wait_mine(slot + 3)
        pass_on(slot + 3)
        wait_theirs(slot + 2)
        step(slot + 1, odd, peak_odd, even, peak_even)
        return carry

    lax.fori_loop(0, 7, pair, 0)
    wait_theirs(15)
    step(14, even, peak_even, odd, peak_odd)
    values = values_of(15)
    for cc in range(4):
        absorb(cc, values, odd, peak_odd)

    columns = pl.ds(pl.multiple_of(head * WIDTH, WIDTH), WIDTH)
    out_copies = []
    for j in (2, 1, 3, 0):
        cc = (head + j) % KVH
        done = (acc[cc, 0:HD] / acc[cc, HD:HD + 1]).T.astype(BF)
        for g in range(GROUP):
            out_stage[j, :, g * HD:(g + 1) * HD] = done[g * TOK:(g + 1) * TOK, :]
        if j == 0:
            out_copies.append(pltpu.make_async_copy(
                out_stage.at[j], out_ref.at[:, columns], o_send.at[j]
            ))
        else:
            to = device(x, y, (z // KVH) * KVH + cc, core)
            out_copies.append(remote(
                out_stage.at[j], out_ref.at[:, columns], o_send.at[j], o_recv.at[j], to
            ))
        out_copies[-1].start()
    for copy in line_copies:
        copy.wait_send()
    for n in range(len(ROUTES)):
        route(n).wait_send()
    for slot in range(16):
        to_twin(slot).wait_send()
    for j in (1, 2, 3):
        source = (head - j + KVH) % KVH
        place = out_ref.at[:, pl.ds(pl.multiple_of(source * WIDTH, WIDTH), WIDTH)]
        pltpu.make_async_copy(place, place, o_recv.at[j]).wait()
    for copy in out_copies[:3]:
        copy.wait_send()
    out_copies[3].wait()


def shards(queries, keys, values, order):
    dma = pltpu.SemaphoreType.DMA
    return pl.pallas_call(
        kernel,
        out_shape=jax.ShapeDtypeStruct((TOK, KVH * WIDTH), BF),
        in_specs=[pl.BlockSpec(memory_space=pl.ANY)] * 4,
        out_specs=pl.BlockSpec(memory_space=pltpu.VMEM),
        scratch_shapes=[
            pltpu.VMEM((16, BLOCK, HD), BF),
            pltpu.VMEM((16, BLOCK, HD), BF),
            pltpu.VMEM((KVH, 2, TOK, HD), BF),
            pltpu.VMEM((NZ, 2, TOK, HD), BF),
            pltpu.SMEM((TOK,), jnp.int32),
            pltpu.VMEM((1, 128), jnp.int32),
            pltpu.VMEM((NZ, 1, 128), jnp.int32),
            pltpu.VMEM((QTOK, WIDTH), BF),
            pltpu.VMEM((2 * HD, 1024), BF),
            pltpu.VMEM((4, KEYS, 256), F32),
            pltpu.VMEM((4, KEYS, 256), F32),
            pltpu.VMEM((4, 1, 256), F32),
            pltpu.VMEM((4, 1, 256), F32),
            pltpu.VMEM((4, HD + TOK, 256), F32),
            pltpu.VMEM((4, 1, 256), F32),
            pltpu.VMEM((4, TOK, WIDTH), BF),
            dma, dma, dma,
            dma((NZ - 1,)), dma, dma((NZ - 1,)), dma,
            dma((len(ROUTES),)), dma((16,)), dma((16,)), dma((16,)), dma((4,)), dma((4,)),
        ],
        compiler_params=pltpu.CompilerParams(
            collective_id=0, has_side_effects=True, vmem_limit_bytes=60 * 1024 * 1024
        ),
        cost_estimate=pl.CostEstimate(
            flops=4 * 1024 * 8192 * 128, bytes_accessed=1 << 20, transcendentals=1024 * 8192
        ),
    )(queries, keys, values, order)


def solution(mesh):
    return jax.shard_map(
        shards,
        mesh=mesh,
        in_specs=(
            P("row", None),
            P(("row", "col"), None),
            P(("row", "col"), None),
            P(("row", "col")),
        ),
        out_specs=P(("row", "col"), None),
        check_vma=False,
    )
```

```python
import math

import jax
import jax.numpy as jnp
from jax import lax
from jax.experimental import pallas as pl
from jax.experimental.pallas import tpu as pltpu
from jax.sharding import PartitionSpec as P

HD = 128
KVH = 4
GROUP = 16
TOK = 16
NX, NY, NZ, NLO = 4, 4, 16, 8
QTOK = 64
WIDTH = GROUP * HD
HALF = 8
BKEYS = HALF * TOK
BLOCK = BKEYS + HD + TOK
KEYS = 4 * BKEYS
BF = jnp.bfloat16
F32 = jnp.float32
MASKED = -1e30
RATE = math.log2(math.e) / math.sqrt(HD)

ORDER = [
    (0, 0, 0), (1, 0, 0), (3, 0, 0), (0, 1, 0), (0, 3, 0), (0, 0, 1), (2, 0, 0), (1, 1, 0),
    (3, 1, 0), (1, 3, 0), (3, 3, 0), (0, 2, 0), (1, 0, 1), (3, 0, 1), (0, 1, 1), (0, 3, 1),
    (2, 1, 0), (2, 3, 0), (2, 0, 1), (1, 1, 1), (3, 1, 1), (1, 3, 1), (3, 3, 1), (1, 2, 0),
    (3, 2, 0), (0, 2, 1), (2, 1, 1), (2, 3, 1), (1, 2, 1), (3, 2, 1), (2, 2, 0), (2, 2, 1),
]
BLOCKS = len(ORDER)
SLOT = {place: index for index, place in enumerate(ORDER)}
STEP = {"A-": (1, 0), "A+": (-1, 0), "B-": (0, 1), "B+": (0, -1)}


def onward(a, b, wave):
    ways = []
    if b == 0:
        if a == 0:
            ways += ["A-", "A+"]
        if (a, wave) == (1, 0):
            ways.append("A-")
        if (a, wave) == (3, 1):
            ways.append("A+")
        ways += ["B-", "B+"]
    if (b, wave) == (1, 0):
        ways.append("B-")
    if (b, wave) == (3, 1):
        ways.append("B+")
    return ways


ROUTES = []
for place in ORDER:
    for way in onward(*place):
        da, db = STEP[way]
        there = ((place[0] + da) % 4, (place[1] + db) % 4, place[2])
        ROUTES.append((SLOT[place], way, SLOT[there]))


def kernel(
    q_hbm, k_hbm, v_hbm, order_hbm, out_ref,
    mine, theirs, stage, landed, order_own, pos_own, pos_line, q_raw, q_t,
    even, odd, peak_even, peak_odd, acc, top, out_stage,
    q_sem, kv_sem, order_sem,
    z_send, z_recv, p_send, p_recv, f_send, m_recv, c_send, t_recv, o_send, o_recv,
):
    row = lax.axis_index("row")
    col = lax.axis_index("col")
    core = row % 2
    x = (row // 2) % NX
    y = row // (4 * NX)
    z = ((row // (2 * NX)) % 2) * NLO + col
    head = col % KVH
    half = col // KVH

    order_copy = pltpu.make_async_copy(order_hbm, order_own, order_sem)
    order_copy.start()
    for g in range(KVH):
        columns = slice(g * HD, (g + 1) * HD)
        pltpu.make_async_copy(k_hbm.at[:, columns], stage.at[g, 0], kv_sem).start()
        pltpu.make_async_copy(v_hbm.at[:, columns], stage.at[g, 1], kv_sem).start()
    q_copy = pltpu.make_async_copy(
        q_hbm.at[pl.ds(half * QTOK, QTOK), pl.ds(pl.multiple_of(head * WIDTH, WIDTH), WIDTH)],
        q_raw, q_sem,
    )
    q_copy.start()

    def device(x_at, y_at, z_at, core_at):
        return (y_at * (4 * NX) + (z_at // NLO) * (2 * NX) + x_at * 2 + core_at, z_at % NLO)

    line = [None] + [device(x, y, (z + d) % NZ, core) for d in range(1, NZ)]
    plane = {}
    for way, (da, db) in STEP.items():
        sx = (1 - core) * da + core * db
        sy = core * da + (1 - core) * db
        plane[way] = device((x - sx + NX) % NX, (y - sy + NY) % NY, z, core)
    twin = device(x, y, z, 1 - core)

    barrier = pltpu.get_barrier_semaphore()
    others = line[1:] + list(plane.values()) + [twin]
    for other in others:
        pl.semaphore_signal(barrier, inc=1, device_id=other, device_id_type=pl.DeviceIdType.MESH)

    order_copy.wait()
    pos_own[...] = jnp.full((1, 128), order_own[0], jnp.int32)
    pltpu.make_async_copy(stage, stage, kv_sem).wait()
    pl.semaphore_wait(barrier, len(others))

    def remote(src, dst, send, recv, to):
        return pltpu.make_async_remote_copy(
            src_ref=src, dst_ref=dst, send_sem=send, recv_sem=recv,
            device_id=to, device_id_type=pl.DeviceIdType.MESH,
        )

    line_copies = []
    for wave, ds in enumerate(([12, 13, 3, 14, 2, 15, 1], [8, 7, 9, 6, 10, 5, 11, 4])):
        for d in ds:
            at = wave * HALF + (NZ - d) % HALF
            line_copies.append(remote(
                stage.at[(z + d) % KVH], landed.at[at], z_send.at[d - 1], z_recv.at[wave], line[d]
            ))
            line_copies.append(remote(
                pos_own, pos_line.at[at], p_send.at[d - 1], p_recv.at[wave], line[d]
            ))
    for copy in line_copies:
        copy.start()
    landed[0] = stage[head]
    pos_line[0] = pos_own[...]

    q_copy.wait()
    for cc in range(4):
        rows = jnp.concatenate(
            [q_raw[cc * TOK:(cc + 1) * TOK, g * HD:(g + 1) * HD] for g in range(GROUP)], axis=0
        )
        q_t[0:HD, cc * 256:(cc + 1) * 256] = rows.T
        token = lax.broadcasted_iota(jnp.int32, (HD, 256), 0)
        lane = lax.broadcasted_iota(jnp.int32, (HD, 256), 1)
        q_t[HD:, cc * 256:(cc + 1) * 256] = jnp.where(
            token == cc * TOK + lane % TOK, 1.0, 0.0
        ).astype(BF)
    acc[...] = jnp.zeros_like(acc)
    top[...] = jnp.full_like(top, MASKED)

    lane16 = lax.broadcasted_iota(jnp.int32, (TOK, 128), 1)

    def collect(wave):
        first = 1 - wave
        got = pos_line.at[pl.ds(wave * HALF + first, HALF - first)]
        pltpu.make_async_copy(got, got, p_recv.at[wave]).wait()
        got = landed.at[pl.ds(wave * HALF + first, HALF - first)]
        pltpu.make_async_copy(got, got, z_recv.at[wave]).wait()
        slot = SLOT[(0, 0, wave)]
        places = [wave * HALF + d for d in range(HALF)]
        starts = jnp.concatenate([pos_line[d] for d in places * 2], axis=0)
        mine[slot, BKEYS + HD:] = jnp.where(
            lane16 < 64, starts // 128, starts % 128
        ).astype(F32).astype(BF)
        for d in range(HALF):
            mine[slot, d * TOK:(d + 1) * TOK] = landed[wave * HALF + d, 0]
        mine[slot, BKEYS:BKEYS + HD] = jnp.concatenate([landed[d, 1] for d in places], axis=0).T

    def route(n):
        slot, way, there = ROUTES[n]
        return remote(mine.at[slot], mine.at[there], f_send.at[n], m_recv.at[there], plane[way])

    def to_twin(slot):
        return remote(mine.at[slot], theirs.at[slot], c_send.at[slot], t_recv.at[slot], twin)

    def wait_mine(slot):
        pltpu.make_async_copy(mine.at[slot], mine.at[slot], m_recv.at[slot]).wait()

    def wait_theirs(slot):
        pltpu.make_async_copy(theirs.at[slot], theirs.at[slot], t_recv.at[slot]).wait()

    def pass_on(slot):
        for n in range(len(ROUTES)):
            if ROUTES[n][0] == slot:
                route(n).start()
        to_twin(slot).start()

    collect(0)
    pass_on(0)

    lane1 = lax.broadcasted_iota(jnp.int32, (1, 128), 1)
    q_pos = jnp.zeros((1, 128), jnp.int32)
    for cc in range(4):
        q_pos = jnp.where(
            lane1 // TOK == cc, pos_line[(cc - head + HALF) % HALF] + lane1 % TOK, q_pos
        )
    limit = (q_pos - lax.broadcasted_iota(jnp.int32, (TOK, 128), 0)).astype(F32)

    def augmented(block, slot):
        word = block[slot, BKEYS + HD:].astype(F32)
        turned = pltpu.roll(word, 64, 1)
        start = jnp.where(lane16 < 64, word * 128.0 + turned, turned * 128.0 + word)
        bias = jnp.concatenate(
            [jnp.where(start[d:d + 1, :] <= limit, 0.0, MASKED).astype(BF) for d in range(HALF)],
            axis=0,
        )
        return jnp.concatenate([block[slot, 0:BKEYS], bias], axis=1)

    def keys_of(s):
        return jnp.concatenate(
            [augmented(block, 2 * s + k) for block in (mine, theirs) for k in (0, 1)], axis=0
        )

    def values_of(s):
        parts = [block[2 * s + k, BKEYS:BKEYS + HD] for block in (mine, theirs) for k in (0, 1)]
        return jnp.concatenate(
            [jnp.concatenate(parts, axis=1), jnp.ones((TOK, KEYS), BF)], axis=0
        )

    def score(cc, keys, into, peak):
        scores = jnp.dot(keys, q_t[:, cc * 256:(cc + 1) * 256], preferred_element_type=F32)
        into[cc] = scores
        peak[cc] = jnp.max(scores, axis=0, keepdims=True)

    def absorb(cc, values, source, peak):
        old = top[cc]
        new = jnp.maximum(old, peak[cc])
        probs = jnp.exp2((source[cc] - new) * RATE).astype(BF)
        acc[cc] = acc[cc] * jnp.exp2((old - new) * RATE) + jnp.dot(
            values, probs, preferred_element_type=F32
        )
        top[cc] = new

    def step(s, source, peak, into, into_peak):
        keys = keys_of(s + 1)
        values = values_of(s)
        for cc in range(4):
            score(cc, keys, into, into_peak)
            absorb(cc, values, source, peak)

    wait_mine(1)
    pass_on(1)
    wait_theirs(0)
    wait_theirs(1)
    keys = keys_of(0)
    for cc in range(4):
        score(cc, keys, even, peak_even)
    for slot in (2, 3):
        wait_mine(slot)
        pass_on(slot)
    wait_theirs(2)
    wait_theirs(3)
    step(0, even, peak_even, odd, peak_odd)
    wait_mine(4)
    pass_on(4)
    collect(1)
    pass_on(5)

    def pair(i, carry):
        for k in range(2):
            s = 2 * i + 1 + k
            for v in range(7):
                first = 4 * v + 6 + 2 * k
                if first < BLOCKS:
                    @pl.when(i == v)
                    def _():
                        for slot in (first, first + 1):
                            wait_mine(slot)
                            pass_on(slot)
            wait_theirs(2 * s + 2)
            wait_theirs(2 * s + 3)
            if k == 0:
                step(s, odd, peak_odd, even, peak_even)
            else:
                step(s, even, peak_even, odd, peak_odd)
        return carry

    lax.fori_loop(0, 7, pair, 0)
    values = values_of(15)
    for cc in range(4):
        absorb(cc, values, odd, peak_odd)

    columns = pl.ds(pl.multiple_of(head * WIDTH, WIDTH), WIDTH)
    out_copies = []
    for j in (2, 1, 3, 0):
        cc = (head + j) % KVH
        done = (acc[cc, 0:HD] / acc[cc, HD:HD + 1]).T.astype(BF)
        for g in range(GROUP):
            out_stage[j, :, g * HD:(g + 1) * HD] = done[g * TOK:(g + 1) * TOK, :]
        if j == 0:
            out_copies.append(pltpu.make_async_copy(
                out_stage.at[j], out_ref.at[:, columns], o_send.at[j]
            ))
        else:
            to = device(x, y, (z // KVH) * KVH + cc, core)
            out_copies.append(remote(
                out_stage.at[j], out_ref.at[:, columns], o_send.at[j], o_recv.at[j], to
            ))
        out_copies[-1].start()
    for copy in line_copies:
        copy.wait_send()
    for n in range(len(ROUTES)):
        route(n).wait_send()
    for slot in range(BLOCKS):
        to_twin(slot).wait_send()
    for j in (1, 2, 3):
        source = (head - j + KVH) % KVH
        place = out_ref.at[:, pl.ds(pl.multiple_of(source * WIDTH, WIDTH), WIDTH)]
        pltpu.make_async_copy(place, place, o_recv.at[j]).wait()
    for copy in out_copies[:3]:
        copy.wait_send()
    out_copies[3].wait()


def shards(queries, keys, values, order):
    dma = pltpu.SemaphoreType.DMA
    return pl.pallas_call(
        kernel,
        out_shape=jax.ShapeDtypeStruct((TOK, KVH * WIDTH), BF),
        in_specs=[pl.BlockSpec(memory_space=pl.ANY)] * 4,
        out_specs=pl.BlockSpec(memory_space=pl.ANY),
        scratch_shapes=[
            pltpu.VMEM((BLOCKS, BLOCK, HD), BF),
            pltpu.VMEM((BLOCKS, BLOCK, HD), BF),
            pltpu.VMEM((KVH, 2, TOK, HD), BF),
            pltpu.VMEM((NZ, 2, TOK, HD), BF),
            pltpu.SMEM((TOK,), jnp.int32),
            pltpu.VMEM((1, 128), jnp.int32),
            pltpu.VMEM((NZ, 1, 128), jnp.int32),
            pltpu.VMEM((QTOK, WIDTH), BF),
            pltpu.VMEM((2 * HD, 1024), BF),
            pltpu.VMEM((4, KEYS, 256), F32),
            pltpu.VMEM((4, KEYS, 256), F32),
            pltpu.VMEM((4, 1, 256), F32),
            pltpu.VMEM((4, 1, 256), F32),
            pltpu.VMEM((4, HD + TOK, 256), F32),
            pltpu.VMEM((4, 1, 256), F32),
            pltpu.VMEM((4, TOK, WIDTH), BF),
            dma, dma, dma,
            dma((NZ - 1,)), dma((2,)), dma((NZ - 1,)), dma((2,)),
            dma((len(ROUTES),)), dma((BLOCKS,)), dma((BLOCKS,)), dma((BLOCKS,)),
            dma((4,)), dma((4,)),
        ],
        compiler_params=pltpu.CompilerParams(
            collective_id=0, has_side_effects=True, vmem_limit_bytes=60 * 1024 * 1024
        ),
        cost_estimate=pl.CostEstimate(
            flops=4 * 1024 * 8192 * 128, bytes_accessed=1 << 20, transcendentals=1024 * 8192
        ),
    )(queries, keys, values, order)


def solution(mesh):
    return jax.shard_map(
        shards,
        mesh=mesh,
        in_specs=(
            P("row", None),
            P(("row", "col"), None),
            P(("row", "col"), None),
            P(("row", "col")),
        ),
        out_specs=P(("row", "col"), None),
        check_vma=False,
    )
```

```python
import math

import jax
import jax.numpy as jnp
from jax import lax
from jax.experimental import pallas as pl
from jax.experimental.pallas import tpu as pltpu
from jax.sharding import PartitionSpec as P

HD = 128
KVH = 4
GROUP = 16
TOK = 16
NX, NY, NZ, NLO = 4, 4, 16, 8
QTOK = 64
WIDTH = GROUP * HD
HALF = 8
BKEYS = HALF * TOK
BLOCK = BKEYS + HD + TOK
KEYS = 4 * BKEYS
BF = jnp.bfloat16
F32 = jnp.float32
MASKED = -1e30
RATE = math.log2(math.e) / math.sqrt(HD)

ORDER = [
    (0, 0, 0), (1, 0, 0), (3, 0, 0), (0, 1, 0), (0, 3, 0), (0, 0, 1), (2, 0, 0), (1, 1, 0),
    (3, 1, 0), (1, 3, 0), (3, 3, 0), (0, 2, 0), (1, 0, 1), (3, 0, 1), (0, 1, 1), (0, 3, 1),
    (2, 1, 0), (2, 3, 0), (2, 0, 1), (1, 1, 1), (3, 1, 1), (1, 3, 1), (3, 3, 1), (1, 2, 0),
    (3, 2, 0), (0, 2, 1), (2, 1, 1), (2, 3, 1), (1, 2, 1), (3, 2, 1), (2, 2, 0), (2, 2, 1),
]
BLOCKS = len(ORDER)
SLOT = {place: index for index, place in enumerate(ORDER)}
STEP = {"A-": (1, 0), "A+": (-1, 0), "B-": (0, 1), "B+": (0, -1)}


def onward(a, b, wave):
    ways = []
    if b == 0:
        if a == 0:
            ways += ["A-", "A+"]
        if (a, wave) == (1, 0):
            ways.append("A-")
        if (a, wave) == (3, 1):
            ways.append("A+")
        ways += ["B-", "B+"]
    if (b, wave) == (1, 0):
        ways.append("B-")
    if (b, wave) == (3, 1):
        ways.append("B+")
    return ways


ROUTES = []
for place in ORDER:
    for way in onward(*place):
        da, db = STEP[way]
        there = ((place[0] + da) % 4, (place[1] + db) % 4, place[2])
        ROUTES.append((SLOT[place], way, SLOT[there]))


def place():
    row = lax.axis_index("row")
    col = lax.axis_index("col")
    return (row // 2) % NX, row // (4 * NX), ((row // (2 * NX)) % 2) * NLO + col, row % 2


def device(x, y, z, core):
    return (y * (4 * NX) + (z // NLO) * (2 * NX) + x * 2 + core, z % NLO)


def remote(src, dst, send, recv, to):
    return pltpu.make_async_remote_copy(
        src_ref=src, dst_ref=dst, send_sem=send, recv_sem=recv,
        device_id=to, device_id_type=pl.DeviceIdType.MESH,
    )


def greet(others):
    barrier = pltpu.get_barrier_semaphore()
    for other in others:
        pl.semaphore_signal(barrier, inc=1, device_id=other, device_id_type=pl.DeviceIdType.MESH)
    return barrier


def gather(
    k_hbm, v_hbm, order_hbm, mine, theirs, pos_line,
    stage, landed, order_own, pos_own, kv_sem, order_sem,
    z_send, z_recv, p_send, p_recv, f_send, m_recv, c_send, t_recv,
):
    x, y, z, core = place()
    head = z % KVH
    order_copy = pltpu.make_async_copy(order_hbm, order_own, order_sem)
    order_copy.start()
    for g in range(KVH):
        columns = slice(g * HD, (g + 1) * HD)
        pltpu.make_async_copy(k_hbm.at[:, columns], stage.at[g, 0], kv_sem).start()
        pltpu.make_async_copy(v_hbm.at[:, columns], stage.at[g, 1], kv_sem).start()

    line = [None] + [device(x, y, (z + d) % NZ, core) for d in range(1, NZ)]
    plane = {}
    for way, (da, db) in STEP.items():
        sx = (1 - core) * da + core * db
        sy = core * da + (1 - core) * db
        plane[way] = device((x - sx + NX) % NX, (y - sy + NY) % NY, z, core)
    twin = device(x, y, z, 1 - core)
    others = line[1:] + list(plane.values()) + [twin]
    barrier = greet(others)
    order_copy.wait()
    pos_own[...] = jnp.full((1, 128), order_own[0], jnp.int32)
    pltpu.make_async_copy(stage, stage, kv_sem).wait()
    pl.semaphore_wait(barrier, len(others))

    line_copies = []
    for wave, ds in enumerate(([12, 13, 3, 14, 2, 15, 1], [8, 7, 9, 6, 10, 5, 11, 4])):
        for d in ds:
            at = wave * HALF + (NZ - d) % HALF
            line_copies.append(remote(
                stage.at[(z + d) % KVH], landed.at[at], z_send.at[d - 1], z_recv.at[wave], line[d]
            ))
            line_copies.append(remote(
                pos_own, pos_line.at[at], p_send.at[d - 1], p_recv.at[wave], line[d]
            ))
    for copy in line_copies:
        copy.start()
    landed[0] = stage[head]
    pos_line[0] = pos_own[...]

    lane16 = lax.broadcasted_iota(jnp.int32, (TOK, 128), 1)

    def collect(wave):
        first = 1 - wave
        got = pos_line.at[pl.ds(wave * HALF + first, HALF - first)]
        pltpu.make_async_copy(got, got, p_recv.at[wave]).wait()
        got = landed.at[pl.ds(wave * HALF + first, HALF - first)]
        pltpu.make_async_copy(got, got, z_recv.at[wave]).wait()
        slot = SLOT[(0, 0, wave)]
        places = [wave * HALF + d for d in range(HALF)]
        starts = jnp.concatenate([pos_line[d] for d in places * 2], axis=0)
        mine[slot, BKEYS + HD:] = jnp.where(
            lane16 < 64, starts // 128, starts % 128
        ).astype(F32).astype(BF)
        for d in range(HALF):
            mine[slot, d * TOK:(d + 1) * TOK] = landed[wave * HALF + d, 0]
        mine[slot, BKEYS:BKEYS + HD] = jnp.concatenate([landed[d, 1] for d in places], axis=0).T

    def route(n):
        slot, way, there = ROUTES[n]
        return remote(mine.at[slot], mine.at[there], f_send.at[n], m_recv.at[there], plane[way])

    def to_twin(slot):
        return remote(mine.at[slot], theirs.at[slot], c_send.at[slot], t_recv.at[slot], twin)

    def wait_mine(slot):
        pltpu.make_async_copy(mine.at[slot], mine.at[slot], m_recv.at[slot]).wait()

    def wait_theirs(slot):
        pltpu.make_async_copy(theirs.at[slot], theirs.at[slot], t_recv.at[slot]).wait()

    def pass_on(slot):
        for n in range(len(ROUTES)):
            if ROUTES[n][0] == slot:
                route(n).start()
        to_twin(slot).start()

    collect(0)
    pass_on(0)
    for slot in range(1, BLOCKS):
        if slot == SLOT[(0, 0, 1)]:
            collect(1)
        else:
            wait_mine(slot)
        pass_on(slot)
    for slot in range(BLOCKS):
        wait_theirs(slot)
    for copy in line_copies:
        copy.wait_send()
    for n in range(len(ROUTES)):
        route(n).wait_send()
    for slot in range(BLOCKS):
        to_twin(slot).wait_send()


def attention(
    q_hbm, mine, theirs, pos_line, out_stage,
    q_raw, q_t, even, odd, peak_even, peak_odd, acc, top, q_sem,
):
    x, y, z, core = place()
    head = z % KVH
    half = (z // KVH) % 2
    q_copy = pltpu.make_async_copy(
        q_hbm.at[pl.ds(half * QTOK, QTOK), pl.ds(pl.multiple_of(head * WIDTH, WIDTH), WIDTH)],
        q_raw, q_sem,
    )
    q_copy.start()
    q_copy.wait()
    for cc in range(4):
        rows = jnp.concatenate(
            [q_raw[cc * TOK:(cc + 1) * TOK, g * HD:(g + 1) * HD] for g in range(GROUP)], axis=0
        )
        q_t[0:HD, cc * 256:(cc + 1) * 256] = rows.T
        token = lax.broadcasted_iota(jnp.int32, (HD, 256), 0)
        lane = lax.broadcasted_iota(jnp.int32, (HD, 256), 1)
        q_t[HD:, cc * 256:(cc + 1) * 256] = jnp.where(
            token == cc * TOK + lane % TOK, 1.0, 0.0
        ).astype(BF)
    acc[...] = jnp.zeros_like(acc)
    top[...] = jnp.full_like(top, MASKED)

    lane16 = lax.broadcasted_iota(jnp.int32, (TOK, 128), 1)
    lane1 = lax.broadcasted_iota(jnp.int32, (1, 128), 1)
    q_pos = jnp.zeros((1, 128), jnp.int32)
    for cc in range(4):
        q_pos = jnp.where(
            lane1 // TOK == cc, pos_line[(cc - head + HALF) % HALF] + lane1 % TOK, q_pos
        )
    limit = (q_pos - lax.broadcasted_iota(jnp.int32, (TOK, 128), 0)).astype(F32)

    def augmented(block, slot):
        word = block[slot, BKEYS + HD:].astype(F32)
        turned = pltpu.roll(word, 64, 1)
        start = jnp.where(lane16 < 64, word * 128.0 + turned, turned * 128.0 + word)
        bias = jnp.concatenate(
            [jnp.where(start[d:d + 1, :] <= limit, 0.0, MASKED).astype(BF) for d in range(HALF)],
            axis=0,
        )
        return jnp.concatenate([block[slot, 0:BKEYS], bias], axis=1)

    def keys_of(s):
        return jnp.concatenate(
            [augmented(block, 2 * s + k) for block in (mine, theirs) for k in (0, 1)], axis=0
        )

    def values_of(s):
        parts = [block[2 * s + k, BKEYS:BKEYS + HD] for block in (mine, theirs) for k in (0, 1)]
        return jnp.concatenate(
            [jnp.concatenate(parts, axis=1), jnp.ones((TOK, KEYS), BF)], axis=0
        )

    def score(cc, keys, into, peak):
        scores = jnp.dot(keys, q_t[:, cc * 256:(cc + 1) * 256], preferred_element_type=F32)
        into[cc] = scores
        peak[cc] = jnp.max(scores, axis=0, keepdims=True)

    def absorb(cc, values, source, peak):
        old = top[cc]
        new = jnp.maximum(old, peak[cc])
        probs = jnp.exp2((source[cc] - new) * RATE).astype(BF)
        acc[cc] = acc[cc] * jnp.exp2((old - new) * RATE) + jnp.dot(
            values, probs, preferred_element_type=F32
        )
        top[cc] = new

    def step(s, source, peak, into, into_peak):
        keys = keys_of(s + 1)
        values = values_of(s)
        for cc in range(4):
            score(cc, keys, into, into_peak)
            absorb(cc, values, source, peak)

    keys = keys_of(0)
    for cc in range(4):
        score(cc, keys, even, peak_even)

    def pair(i, carry):
        step(2 * i, even, peak_even, odd, peak_odd)
        step(2 * i + 1, odd, peak_odd, even, peak_even)
        return carry

    lax.fori_loop(0, 7, pair, 0)
    step(14, even, peak_even, odd, peak_odd)
    values = values_of(15)
    for cc in range(4):
        absorb(cc, values, odd, peak_odd)
    for cc in range(4):
        done = (acc[cc, 0:HD] / acc[cc, HD:HD + 1]).T.astype(BF)
        for g in range(GROUP):
            out_stage[cc, :, g * HD:(g + 1) * HD] = done[g * TOK:(g + 1) * TOK, :]


def deliver(pieces, out_ref, o_send, o_recv):
    x, y, z, core = place()
    head = z % KVH
    targets = [device(x, y, (z // KVH) * KVH + (head + j) % KVH, core) for j in (1, 2, 3)]
    barrier = greet(targets)
    pl.semaphore_wait(barrier, len(targets))
    columns = pl.ds(pl.multiple_of(head * WIDTH, WIDTH), WIDTH)
    own = pltpu.make_async_copy(pieces.at[head], out_ref.at[:, columns], o_send.at[0])
    copies = [
        remote(
            pieces.at[(head + j) % KVH], out_ref.at[:, columns],
            o_send.at[j], o_recv.at[j], targets[j - 1],
        )
        for j in (2, 1, 3)
    ]
    for copy in copies:
        copy.start()
    own.start()
    own.wait()
    for j in (1, 2, 3):
        source = (head - j + KVH) % KVH
        there = out_ref.at[:, pl.ds(pl.multiple_of(source * WIDTH, WIDTH), WIDTH)]
        pltpu.make_async_copy(there, there, o_recv.at[j]).wait()
    for copy in copies:
        copy.wait_send()


def shards(queries, keys, values, order):
    dma = pltpu.SemaphoreType.DMA
    any_space = pl.BlockSpec(memory_space=pl.ANY)
    vmem = pl.BlockSpec(memory_space=pltpu.VMEM)
    blocks = jax.ShapeDtypeStruct((BLOCKS, BLOCK, HD), BF)
    mine, theirs, pos_line = pl.pallas_call(
        gather,
        out_shape=(blocks, blocks, jax.ShapeDtypeStruct((NZ, 1, 128), jnp.int32)),
        in_specs=[any_space] * 3,
        out_specs=[vmem] * 3,
        scratch_shapes=[
            pltpu.VMEM((KVH, 2, TOK, HD), BF),
            pltpu.VMEM((NZ, 2, TOK, HD), BF),
            pltpu.SMEM((TOK,), jnp.int32),
            pltpu.VMEM((1, 128), jnp.int32),
            dma, dma,
            dma((NZ - 1,)), dma((2,)), dma((NZ - 1,)), dma((2,)),
            dma((len(ROUTES),)), dma((BLOCKS,)), dma((BLOCKS,)), dma((BLOCKS,)),
        ],
        compiler_params=pltpu.CompilerParams(
            collective_id=0, has_side_effects=True, vmem_limit_bytes=40 * 1024 * 1024
        ),
    )(keys, values, order)
    pieces = pl.pallas_call(
        attention,
        out_shape=jax.ShapeDtypeStruct((4, TOK, WIDTH), BF),
        in_specs=[any_space, vmem, vmem, vmem],
        out_specs=vmem,
        scratch_shapes=[
            pltpu.VMEM((QTOK, WIDTH), BF),
            pltpu.VMEM((2 * HD, 1024), BF),
            pltpu.VMEM((4, KEYS, 256), F32),
            pltpu.VMEM((4, KEYS, 256), F32),
            pltpu.VMEM((4, 1, 256), F32),
            pltpu.VMEM((4, 1, 256), F32),
            pltpu.VMEM((4, HD + TOK, 256), F32),
            pltpu.VMEM((4, 1, 256), F32),
            dma,
        ],
        compiler_params=pltpu.CompilerParams(vmem_limit_bytes=40 * 1024 * 1024),
        cost_estimate=pl.CostEstimate(
            flops=4 * 1024 * 8192 * 128, bytes_accessed=5 << 20, transcendentals=1024 * 8192
        ),
    )(queries, mine, theirs, pos_line)
    return pl.pallas_call(
        deliver,
        out_shape=jax.ShapeDtypeStruct((TOK, KVH * WIDTH), BF),
        in_specs=[vmem],
        out_specs=vmem,
        scratch_shapes=[dma((4,)), dma((4,))],
        compiler_params=pltpu.CompilerParams(
            collective_id=1, has_side_effects=True, vmem_limit_bytes=40 * 1024 * 1024
        ),
    )(pieces)


def solution(mesh):
    return jax.shard_map(
        shards,
        mesh=mesh,
        in_specs=(
            P("row", None),
            P(("row", "col"), None),
            P(("row", "col"), None),
            P(("row", "col")),
        ),
        out_specs=P(("row", "col"), None),
        check_vma=False,
    )
```

```python
import math

import jax
import jax.numpy as jnp
from jax import lax
from jax.experimental import pallas as pl
from jax.experimental.pallas import tpu as pltpu
from jax.sharding import PartitionSpec as P

HD = 128
KVH = 4
GROUP = 16
TOK = 16
NX, NY, NZ, NLO = 4, 4, 16, 8
QTOK = 64
WIDTH = GROUP * HD
HALF = 8
BKEYS = HALF * TOK
BLOCK = BKEYS + HD + TOK
KEYS = 2 * BKEYS
ROWS = 8
BF = jnp.bfloat16
F32 = jnp.float32
MASKED = -1e30
RATE = math.log2(math.e) / math.sqrt(HD)

ORDER = [
    (0, 0, 0), (1, 0, 0), (0, 3, 0), (0, 1, 0), (3, 0, 0), (0, 0, 1), (2, 0, 0), (0, 2, 0),
    (1, 3, 0), (1, 1, 0), (3, 0, 1), (3, 1, 0), (2, 3, 0), (1, 0, 1), (3, 3, 0), (0, 3, 1),
    (2, 0, 1), (1, 2, 0), (2, 1, 0), (3, 3, 1), (1, 3, 1), (2, 3, 1), (0, 1, 1), (0, 2, 1),
    (3, 2, 0), (3, 2, 1), (2, 1, 1), (3, 1, 1), (2, 2, 0), (1, 1, 1), (1, 2, 1), (2, 2, 1),
]
BLOCKS = len(ORDER)
SLOT = {place: index for index, place in enumerate(ORDER)}
STEP = {"A-": (1, 0), "A+": (-1, 0), "B-": (0, 1), "B+": (0, -1)}


def onward(a, b, wave):
    ways = []
    if b == 0:
        if a == 0:
            ways += ["A-", "A+"]
        if (a, wave) == (1, 0):
            ways.append("A-")
        if (a, wave) == (3, 1):
            ways.append("A+")
        ways += ["B-", "B+"]
    if (b, wave) == (1, 0):
        ways.append("B-")
    if (b, wave) == (3, 1):
        ways.append("B+")
    return ways


ROUTES = []
for place in ORDER:
    for way in onward(*place):
        da, db = STEP[way]
        there = ((place[0] + da) % 4, (place[1] + db) % 4, place[2])
        ROUTES.append((SLOT[place], way, SLOT[there]))


def kernel(
    q_hbm, k_hbm, v_hbm, order_hbm, out_ref,
    mine, stage, landed, order_own, pos_own, pos_line, q_raw, q_pos, q_t,
    even, odd, peak_even, peak_odd, acc, top, half_send, half_recv, stat_send, stat_recv, out_stage,
    q_sem, kv_sem, order_sem,
    z_send, z_recv, p_send, p_recv, f_send, m_recv, t_send, t_recv, h_send, h_recv, o_send, o_recv,
):
    row = lax.axis_index("row")
    col = lax.axis_index("col")
    core = row % 2
    x = (row // 2) % NX
    y = row // (4 * NX)
    z = ((row // (2 * NX)) % 2) * NLO + col
    head = col % KVH
    half = col // KVH

    order_copy = pltpu.make_async_copy(order_hbm, order_own, order_sem)
    order_copy.start()
    for g in range(KVH):
        columns = slice(g * HD, (g + 1) * HD)
        pltpu.make_async_copy(k_hbm.at[:, columns], stage.at[g, 0], kv_sem).start()
        pltpu.make_async_copy(v_hbm.at[:, columns], stage.at[g, 1], kv_sem).start()
    q_copy = pltpu.make_async_copy(
        q_hbm.at[pl.ds(half * QTOK, QTOK), pl.ds(pl.multiple_of(head * WIDTH, WIDTH), WIDTH)],
        q_raw.at[0], q_sem,
    )
    q_copy.start()

    def device(x_at, y_at, z_at, core_at):
        return (y_at * (4 * NX) + (z_at // NLO) * (2 * NX) + x_at * 2 + core_at, z_at % NLO)

    line = [None] + [device(x, y, (z + d) % NZ, core) for d in range(1, NZ)]
    plane = {}
    for way, (da, db) in STEP.items():
        sx = (1 - core) * da + core * db
        sy = core * da + (1 - core) * db
        plane[way] = device((x - sx + NX) % NX, (y - sy + NY) % NY, z, core)
    twin = device(x, y, z, 1 - core)

    barrier = pltpu.get_barrier_semaphore()
    others = line[1:] + list(plane.values()) + [twin]
    for other in others:
        pl.semaphore_signal(barrier, inc=1, device_id=other, device_id_type=pl.DeviceIdType.MESH)

    order_copy.wait()
    pos_own[...] = jnp.full((1, 128), order_own[0], jnp.int32)
    pltpu.make_async_copy(stage, stage, kv_sem).wait()
    pl.semaphore_wait(barrier, len(others))

    def remote(src, dst, send, recv, to):
        return pltpu.make_async_remote_copy(
            src_ref=src, dst_ref=dst, send_sem=send, recv_sem=recv,
            device_id=to, device_id_type=pl.DeviceIdType.MESH,
        )

    line_copies = []
    for wave, ds in enumerate(([12, 13, 3, 14, 2, 15, 1], [8, 7, 9, 6, 10, 5, 11, 4])):
        for d in ds:
            at = wave * HALF + (NZ - d) % HALF
            line_copies.append(remote(
                stage.at[(z + d) % KVH], landed.at[at], z_send.at[d - 1], z_recv.at[wave], line[d]
            ))
            line_copies.append(remote(
                pos_own, pos_line.at[at], p_send.at[d - 1], p_recv.at[wave], line[d]
            ))
    for copy in line_copies:
        copy.start()
    landed[0] = stage[head]
    pos_line[0] = pos_own[...]

    q_copy.wait()
    q_over = remote(q_raw.at[0], q_raw.at[1], t_send.at[0], t_recv.at[0], twin)
    q_over.start()

    def turn(side):
        for cc in range(4):
            rows = jnp.concatenate(
                [
                    q_raw[side, cc * TOK:(cc + 1) * TOK, g * HD:(g + 1) * HD]
                    for g in range(GROUP)
                ],
                axis=0,
            )
            token = lax.broadcasted_iota(jnp.int32, (HD, 256), 0)
            lane = lax.broadcasted_iota(jnp.int32, (HD, 256), 1)
            q_t[side * 4 + cc, 0:HD] = rows.T
            q_t[side * 4 + cc, HD:] = jnp.where(
                token == side * QTOK + cc * TOK + lane % TOK, 1.0, 0.0
            ).astype(BF)

    turn(0)
    acc[...] = jnp.zeros_like(acc)
    top[...] = jnp.full_like(top, MASKED)

    lane16 = lax.broadcasted_iota(jnp.int32, (TOK, 128), 1)

    def collect(wave):
        first = 1 - wave
        got = pos_line.at[pl.ds(wave * HALF + first, HALF - first)]
        pltpu.make_async_copy(got, got, p_recv.at[wave]).wait()
        got = landed.at[pl.ds(wave * HALF + first, HALF - first)]
        pltpu.make_async_copy(got, got, z_recv.at[wave]).wait()
        slot = SLOT[(0, 0, wave)]
        places = [wave * HALF + d for d in range(HALF)]
        starts = jnp.concatenate([pos_line[d] for d in places * 2], axis=0)
        mine[slot, BKEYS + HD:] = jnp.where(
            lane16 < 64, starts // 128, starts % 128
        ).astype(F32).astype(BF)
        for d in range(HALF):
            mine[slot, d * TOK:(d + 1) * TOK] = landed[wave * HALF + d, 0]
        mine[slot, BKEYS:BKEYS + HD] = jnp.concatenate([landed[d, 1] for d in places], axis=0).T

    def route(n):
        slot, way, there = ROUTES[n]
        return remote(mine.at[slot], mine.at[there], f_send.at[n], m_recv.at[there], plane[way])

    def wait_mine(slot):
        pltpu.make_async_copy(mine.at[slot], mine.at[slot], m_recv.at[slot]).wait()

    def pass_on(slot):
        for n in range(len(ROUTES)):
            if ROUTES[n][0] == slot:
                route(n).start()

    collect(0)
    pass_on(0)

    lane1 = lax.broadcasted_iota(jnp.int32, (1, 128), 1)
    token_pos = jnp.zeros((1, 128), jnp.int32)
    for cc in range(4):
        token_pos = jnp.where(
            (lane1 % QTOK) // TOK == cc,
            pos_line[(cc - head + HALF) % HALF] + lane1 % TOK, token_pos,
        )
    q_pos[0] = token_pos
    pos_over = remote(q_pos.at[0], q_pos.at[1], t_send.at[1], t_recv.at[1], twin)
    pos_over.start()
    q_over.wait_recv()
    turn(1)
    pos_over.wait_recv()
    limit = (
        jnp.where(lane1 < QTOK, q_pos[0], q_pos[1]) - lax.broadcasted_iota(jnp.int32, (TOK, 128), 0)
    ).astype(F32)

    def augmented(slot):
        word = mine[slot, BKEYS + HD:].astype(F32)
        turned = pltpu.roll(word, 64, 1)
        start = jnp.where(lane16 < 64, word * 128.0 + turned, turned * 128.0 + word)
        bias = jnp.concatenate(
            [jnp.where(start[d:d + 1, :] <= limit, 0.0, MASKED).astype(BF) for d in range(HALF)],
            axis=0,
        )
        return jnp.concatenate([mine[slot, 0:BKEYS], bias], axis=1)

    def keys_of(s):
        return jnp.concatenate([augmented(2 * s), augmented(2 * s + 1)], axis=0)

    def values_of(s):
        parts = [mine[2 * s + k, BKEYS:BKEYS + HD] for k in (0, 1)]
        return jnp.concatenate(
            [jnp.concatenate(parts, axis=1), jnp.ones((TOK, KEYS), BF)], axis=0
        )

    def score(cc, keys, into, peak):
        scores = jnp.dot(keys, q_t[cc], preferred_element_type=F32)
        into[cc] = scores
        peak[cc] = jnp.max(scores, axis=0, keepdims=True)

    def absorb(cc, values, source, peak):
        old = top[cc]
        new = jnp.maximum(old, peak[cc])
        probs = jnp.exp2((source[cc] - new) * RATE).astype(BF)
        acc[cc] = acc[cc] * jnp.exp2((old - new) * RATE) + jnp.dot(
            values, probs, preferred_element_type=F32
        )
        top[cc] = new

    def step(s, source, peak, into, into_peak):
        keys = keys_of(s + 1)
        values = values_of(s)
        for cc in range(ROWS):
            score(cc, keys, into, into_peak)
            absorb(cc, values, source, peak)

    def receive(slot):
        if slot == SLOT[(0, 0, 1)]:
            collect(1)
        else:
            wait_mine(slot)
        pass_on(slot)

    due = {s: [] for s in range(-1, 15)}
    for slot in range(1, BLOCKS):
        passes = any(route_of[0] == slot for route_of in ROUTES)
        due[max(-1, slot // 2 - (2 if passes else 1))].append(slot)

    for slot in due[-1]:
        receive(slot)
    keys = keys_of(0)
    for cc in range(ROWS):
        score(cc, keys, even, peak_even)
    for slot in due[0]:
        receive(slot)
    step(0, even, peak_even, odd, peak_odd)

    def pair(i, carry):
        for k in range(2):
            for v in range(7):
                if due[2 * v + 1 + k]:
                    @pl.when(i == v)
                    def _():
                        for slot in due[2 * v + 1 + k]:
                            receive(slot)
            s = 2 * i + 1 + k
            if k == 0:
                step(s, odd, peak_odd, even, peak_even)
            else:
                step(s, even, peak_even, odd, peak_odd)
        return carry

    lax.fori_loop(0, 7, pair, 0)

    values = values_of(15)
    over = []
    for cc in range(4):
        absorb(4 + cc, values, odd, peak_odd)
        half_send[cc] = acc[4 + cc, 0:HD].astype(BF)
        stat_send[2 * cc] = acc[4 + cc, HD:HD + 1]
        stat_send[2 * cc + 1] = top[4 + cc]
        over.append((
            remote(half_send.at[cc], half_recv.at[cc], h_send.at[2 * cc], h_recv.at[2 * cc], twin),
            remote(
                stat_send.at[pl.ds(2 * cc, 2)], stat_recv.at[pl.ds(2 * cc, 2)],
                h_send.at[2 * cc + 1], h_recv.at[2 * cc + 1], twin,
            ),
        ))
        for copy in over[-1]:
            copy.start()
    for cc in range(4):
        absorb(cc, values, odd, peak_odd)
    for cc in range(4):
        for copy in over[cc]:
            copy.wait_recv()
        other = stat_recv[2 * cc + 1]
        new = jnp.maximum(top[cc], other)
        own_part = jnp.exp2((top[cc] - new) * RATE)
        other_part = jnp.exp2((other - new) * RATE)
        total = acc[cc, HD:HD + 1] * own_part + stat_recv[2 * cc] * other_part
        own_part = own_part / total
        other_part = other_part / total
        done = (acc[cc, 0:HD] * own_part + half_recv[cc].astype(F32) * other_part).T.astype(BF)
        for g in range(GROUP):
            out_stage[cc, :, g * HD:(g + 1) * HD] = done[g * TOK:(g + 1) * TOK, :]

    columns = pl.ds(pl.multiple_of(head * WIDTH, WIDTH), WIDTH)
    out_copies = []
    for j in (2, 1, 3, 0):
        cc = (head + j) % KVH
        if j == 0:
            out_copies.append(pltpu.make_async_copy(
                out_stage.at[cc], out_ref.at[:, columns], o_send.at[j]
            ))
        else:
            to = device(x, y, (z // KVH) * KVH + cc, core)
            out_copies.append(remote(
                out_stage.at[cc], out_ref.at[:, columns], o_send.at[j], o_recv.at[j], to
            ))
        out_copies[-1].start()
    for copy in line_copies:
        copy.wait_send()
    for n in range(len(ROUTES)):
        route(n).wait_send()
    q_over.wait_send()
    pos_over.wait_send()
    for copies in over:
        for copy in copies:
            copy.wait_send()
    for j in (1, 2, 3):
        source = (head - j + KVH) % KVH
        place = out_ref.at[:, pl.ds(pl.multiple_of(source * WIDTH, WIDTH), WIDTH)]
        pltpu.make_async_copy(place, place, o_recv.at[j]).wait()
    for copy in out_copies[:3]:
        copy.wait_send()
    out_copies[3].wait()


def shards(queries, keys, values, order):
    dma = pltpu.SemaphoreType.DMA
    return pl.pallas_call(
        kernel,
        out_shape=jax.ShapeDtypeStruct((TOK, KVH * WIDTH), BF),
        in_specs=[pl.BlockSpec(memory_space=pl.ANY)] * 4,
        out_specs=pl.BlockSpec(memory_space=pl.ANY),
        scratch_shapes=[
            pltpu.VMEM((BLOCKS, BLOCK, HD), BF),
            pltpu.VMEM((KVH, 2, TOK, HD), BF),
            pltpu.VMEM((NZ, 2, TOK, HD), BF),
            pltpu.SMEM((TOK,), jnp.int32),
            pltpu.VMEM((1, 128), jnp.int32),
            pltpu.VMEM((NZ, 1, 128), jnp.int32),
            pltpu.VMEM((2, QTOK, WIDTH), BF),
            pltpu.VMEM((2, 1, 128), jnp.int32),
            pltpu.VMEM((ROWS, 2 * HD, 256), BF),
            pltpu.VMEM((ROWS, KEYS, 256), F32),
            pltpu.VMEM((ROWS, KEYS, 256), F32),
            pltpu.VMEM((ROWS, 1, 256), F32),
            pltpu.VMEM((ROWS, 1, 256), F32),
            pltpu.VMEM((ROWS, HD + TOK, 256), F32),
            pltpu.VMEM((ROWS, 1, 256), F32),
            pltpu.VMEM((4, HD, 256), BF),
            pltpu.VMEM((4, HD, 256), BF),
            pltpu.VMEM((8, 1, 256), F32),
            pltpu.VMEM((8, 1, 256), F32),
            pltpu.VMEM((4, TOK, WIDTH), BF),
            dma, dma, dma,
            dma((NZ - 1,)), dma((2,)), dma((NZ - 1,)), dma((2,)),
            dma((len(ROUTES),)), dma((BLOCKS,)), dma((2,)), dma((2,)),
            dma((8,)), dma((8,)), dma((4,)), dma((4,)),
        ],
        compiler_params=pltpu.CompilerParams(
            collective_id=0, has_side_effects=True, vmem_limit_bytes=60 * 1024 * 1024
        ),
        cost_estimate=pl.CostEstimate(
            flops=4 * 1024 * 8192 * 128, bytes_accessed=1 << 20, transcendentals=1024 * 8192
        ),
    )(queries, keys, values, order)


def solution(mesh):
    return jax.shard_map(
        shards,
        mesh=mesh,
        in_specs=(
            P("row", None),
            P(("row", "col"), None),
            P(("row", "col"), None),
            P(("row", "col")),
        ),
        out_specs=P(("row", "col"), None),
        check_vma=False,
    )
```

```python
import math

import jax
import jax.numpy as jnp
from jax import lax
from jax.experimental import pallas as pl
from jax.experimental.pallas import tpu as pltpu
from jax.sharding import PartitionSpec as P

HD = 128
KVH = 4
GROUP = 16
TOK = 16
NX, NY, NZ, NLO = 4, 4, 16, 8
QTOK = 64
WIDTH = GROUP * HD
HALF = 8
BKEYS = HALF * TOK
BLOCK = BKEYS + HD + TOK
KEYS = 2 * BKEYS
ROWS = 8
BF = jnp.bfloat16
F32 = jnp.float32
MASKED = -1e30
RATE = math.log2(math.e) / math.sqrt(HD)

ORDER = [
    (0, 0, 0), (1, 0, 0), (3, 0, 0), (0, 3, 0), (0, 0, 1), (1, 3, 0), (0, 1, 0), (3, 3, 0),
    (2, 0, 0), (1, 1, 0), (3, 0, 1), (3, 1, 0), (0, 3, 1), (0, 1, 1), (1, 0, 1), (2, 3, 0),
    (0, 2, 0), (2, 0, 1), (3, 3, 1), (2, 1, 0), (0, 2, 1), (3, 1, 1), (1, 3, 1), (1, 2, 0),
    (3, 2, 0), (2, 3, 1), (1, 1, 1), (3, 2, 1), (2, 1, 1), (1, 2, 1), (2, 2, 0), (2, 2, 1),
]
HELD = [
    4, 4, 6, 6, 10, 10, 11, 11, 12, 12,
    14, 16, 16, 16, 18, 18, 20, 20, 24, 24,
    24, 26, 26, 26, 28, 28, 30, 30, 32, 32,
]
BLOCKS = len(ORDER)
SLOT = {place: index for index, place in enumerate(ORDER)}
STEP = {"A-": (1, 0), "A+": (-1, 0), "B-": (0, 1), "B+": (0, -1)}


def onward(a, b, wave):
    ways = []
    if b == 0:
        if a == 0:
            ways += ["A-", "A+"]
        if (a, wave) == (1, 0):
            ways.append("A-")
        if (a, wave) == (3, 1):
            ways.append("A+")
        ways += ["B-", "B+"]
    if (b, wave) == (1, 0):
        ways.append("B-")
    if (b, wave) == (3, 1):
        ways.append("B+")
    return ways


ROUTES = []
for place in ORDER:
    for way in onward(*place):
        da, db = STEP[way]
        there = ((place[0] + da) % 4, (place[1] + db) % 4, place[2])
        ROUTES.append((SLOT[place], way, SLOT[there]))


def kernel(
    q_hbm, k_hbm, v_hbm, order_hbm, out_ref,
    mine, stage, landed, order_own, pos_own, pos_line, q_raw, q_pos, q_t,
    even, odd, peak_even, peak_odd, acc, top, half_send, half_recv, stat_send, stat_recv, out_stage,
    q_sem, kv_sem, order_sem,
    z_send, z_recv, p_send, p_recv, f_send, m_recv, t_send, t_recv, h_send, h_recv, o_send, o_recv,
):
    row = lax.axis_index("row")
    col = lax.axis_index("col")
    core = row % 2
    x = (row // 2) % NX
    y = row // (4 * NX)
    z = ((row // (2 * NX)) % 2) * NLO + col
    head = col % KVH
    half = col // KVH

    order_copy = pltpu.make_async_copy(order_hbm, order_own, order_sem)
    order_copy.start()
    for g in range(KVH):
        columns = slice(g * HD, (g + 1) * HD)
        pltpu.make_async_copy(k_hbm.at[:, columns], stage.at[g, 0], kv_sem).start()
        pltpu.make_async_copy(v_hbm.at[:, columns], stage.at[g, 1], kv_sem).start()
    q_copy = pltpu.make_async_copy(
        q_hbm.at[pl.ds(half * QTOK, QTOK), pl.ds(pl.multiple_of(head * WIDTH, WIDTH), WIDTH)],
        q_raw.at[0], q_sem,
    )
    q_copy.start()

    def device(x_at, y_at, z_at, core_at):
        return (y_at * (4 * NX) + (z_at // NLO) * (2 * NX) + x_at * 2 + core_at, z_at % NLO)

    line = [None] + [device(x, y, (z + d) % NZ, core) for d in range(1, NZ)]
    plane = {}
    for way, (da, db) in STEP.items():
        sx = (1 - core) * da + core * db
        sy = core * da + (1 - core) * db
        plane[way] = device((x - sx + NX) % NX, (y - sy + NY) % NY, z, core)
    twin = device(x, y, z, 1 - core)

    barrier = pltpu.get_barrier_semaphore()
    others = line[1:] + list(plane.values()) + [twin]
    for other in others:
        pl.semaphore_signal(barrier, inc=1, device_id=other, device_id_type=pl.DeviceIdType.MESH)

    order_copy.wait()
    pos_own[...] = jnp.full((1, 128), order_own[0], jnp.int32)
    pltpu.make_async_copy(stage, stage, kv_sem).wait()
    pl.semaphore_wait(barrier, len(others))

    def remote(src, dst, send, recv, to):
        return pltpu.make_async_remote_copy(
            src_ref=src, dst_ref=dst, send_sem=send, recv_sem=recv,
            device_id=to, device_id_type=pl.DeviceIdType.MESH,
        )

    line_copies = []
    for wave, ds in enumerate(([12, 13, 3, 14, 2, 15, 1], [8, 7, 9, 6, 10, 5, 11, 4])):
        for d in ds:
            at = wave * HALF + (NZ - d) % HALF
            line_copies.append(remote(
                stage.at[(z + d) % KVH], landed.at[at], z_send.at[d - 1], z_recv.at[wave], line[d]
            ))
            line_copies.append(remote(
                pos_own, pos_line.at[at], p_send.at[d - 1], p_recv.at[wave], line[d]
            ))
    for copy in line_copies:
        copy.start()
    landed[0] = stage[head]
    pos_line[0] = pos_own[...]

    q_copy.wait()
    q_over = remote(q_raw.at[0], q_raw.at[1], t_send.at[0], t_recv.at[0], twin)
    q_over.start()

    def turn(side):
        for cc in range(4):
            rows = jnp.concatenate(
                [
                    q_raw[side, cc * TOK:(cc + 1) * TOK, g * HD:(g + 1) * HD]
                    for g in range(GROUP)
                ],
                axis=0,
            )
            token = lax.broadcasted_iota(jnp.int32, (HD, 256), 0)
            lane = lax.broadcasted_iota(jnp.int32, (HD, 256), 1)
            q_t[side * 4 + cc, 0:HD] = rows.T
            q_t[side * 4 + cc, HD:] = jnp.where(
                token == side * QTOK + cc * TOK + lane % TOK, 1.0, 0.0
            ).astype(BF)

    turn(0)
    q_over.wait_recv()
    turn(1)
    acc[...] = jnp.zeros_like(acc)
    top[...] = jnp.full_like(top, MASKED)

    lane16 = lax.broadcasted_iota(jnp.int32, (TOK, 128), 1)

    def collect(wave):
        first = 1 - wave
        got = pos_line.at[pl.ds(wave * HALF + first, HALF - first)]
        pltpu.make_async_copy(got, got, p_recv.at[wave]).wait()
        got = landed.at[pl.ds(wave * HALF + first, HALF - first)]
        pltpu.make_async_copy(got, got, z_recv.at[wave]).wait()
        slot = SLOT[(0, 0, wave)]
        places = [wave * HALF + d for d in range(HALF)]
        starts = jnp.concatenate([pos_line[d] for d in places * 2], axis=0)
        mine[slot, BKEYS + HD:] = jnp.where(
            lane16 < 64, starts // 128, starts % 128
        ).astype(F32).astype(BF)
        for d in range(HALF):
            mine[slot, d * TOK:(d + 1) * TOK] = landed[wave * HALF + d, 0]
        mine[slot, BKEYS:BKEYS + HD] = jnp.concatenate([landed[d, 1] for d in places], axis=0).T

    def route(n):
        slot, way, there = ROUTES[n]
        return remote(mine.at[slot], mine.at[there], f_send.at[n], m_recv.at[there], plane[way])

    def wait_mine(slot):
        pltpu.make_async_copy(mine.at[slot], mine.at[slot], m_recv.at[slot]).wait()

    def pass_on(slot):
        for n in range(len(ROUTES)):
            if ROUTES[n][0] == slot:
                route(n).start()

    collect(0)
    pass_on(0)

    lane1 = lax.broadcasted_iota(jnp.int32, (1, 128), 1)
    token_pos = jnp.zeros((1, 128), jnp.int32)
    for cc in range(4):
        token_pos = jnp.where(
            (lane1 % QTOK) // TOK == cc,
            pos_line[(cc - head + HALF) % HALF] + lane1 % TOK, token_pos,
        )
    q_pos[0] = token_pos
    pos_over = remote(q_pos.at[0], q_pos.at[1], t_send.at[1], t_recv.at[1], twin)
    pos_over.start()

    def receive(first, last):
        for slot in range(first, last):
            if slot == SLOT[(0, 0, 1)]:
                collect(1)
            else:
                wait_mine(slot)
            pass_on(slot)

    early = max(2, HELD[0] - 2)
    receive(1, early)
    pos_over.wait_recv()
    limit = (
        jnp.where(lane1 < QTOK, q_pos[0], q_pos[1]) - lax.broadcasted_iota(jnp.int32, (TOK, 128), 0)
    ).astype(F32)

    def augmented(slot):
        word = mine[slot, BKEYS + HD:].astype(F32)
        turned = pltpu.roll(word, 64, 1)
        start = jnp.where(lane16 < 64, word * 128.0 + turned, turned * 128.0 + word)
        bias = jnp.concatenate(
            [jnp.where(start[d:d + 1, :] <= limit, 0.0, MASKED).astype(BF) for d in range(HALF)],
            axis=0,
        )
        return jnp.concatenate([mine[slot, 0:BKEYS], bias], axis=1)

    def keys_of(s):
        return jnp.concatenate([augmented(2 * s), augmented(2 * s + 1)], axis=0)

    def values_of(s):
        parts = [mine[2 * s + k, BKEYS:BKEYS + HD] for k in (0, 1)]
        return jnp.concatenate(
            [jnp.concatenate(parts, axis=1), jnp.ones((TOK, KEYS), BF)], axis=0
        )

    def score(cc, keys, into, peak):
        scores = jnp.dot(keys, q_t[cc], preferred_element_type=F32)
        into[cc] = scores
        peak[cc] = jnp.max(scores, axis=0, keepdims=True)

    def absorb(cc, values, source, peak):
        old = top[cc]
        new = jnp.maximum(old, peak[cc])
        probs = jnp.exp2((source[cc] - new) * RATE).astype(BF)
        acc[cc] = acc[cc] * jnp.exp2((old - new) * RATE) + jnp.dot(
            values, probs, preferred_element_type=F32
        )
        top[cc] = new

    def step(s, source, peak, into, into_peak, between):
        for part in range(2):
            between(part)
            if part == 0:
                keys = keys_of(s + 1)
                values = values_of(s)
            for cc in range(4 * part, 4 * part + 4):
                score(cc, keys, into, into_peak)
                absorb(cc, values, source, peak)

    keys = keys_of(0)
    for cc in range(ROWS):
        score(cc, keys, even, peak_even)
    held = [early] + HELD
    step(
        0, even, peak_even, odd, peak_odd, lambda part: receive(held[part], held[part + 1])
    )

    def pair(i, carry):
        for k in range(2):
            def between(part):
                for v in range(7):
                    at = 2 * (2 * v + 1 + k) + part
                    if held[at] < held[at + 1]:
                        @pl.when(i == v)
                        def _():
                            receive(held[at], held[at + 1])

            s = 2 * i + 1 + k
            if k == 0:
                step(s, odd, peak_odd, even, peak_even, between)
            else:
                step(s, even, peak_even, odd, peak_odd, between)
        return carry

    lax.fori_loop(0, 7, pair, 0)

    values = values_of(15)
    over = []
    for cc in range(4):
        absorb(4 + cc, values, odd, peak_odd)
        half_send[cc] = acc[4 + cc, 0:HD].astype(BF)
        stat_send[2 * cc] = acc[4 + cc, HD:HD + 1]
        stat_send[2 * cc + 1] = top[4 + cc]
        over.append((
            remote(half_send.at[cc], half_recv.at[cc], h_send.at[2 * cc], h_recv.at[2 * cc], twin),
            remote(
                stat_send.at[pl.ds(2 * cc, 2)], stat_recv.at[pl.ds(2 * cc, 2)],
                h_send.at[2 * cc + 1], h_recv.at[2 * cc + 1], twin,
            ),
        ))
        for copy in over[-1]:
            copy.start()
    for cc in range(4):
        absorb(cc, values, odd, peak_odd)

    columns = pl.ds(pl.multiple_of(head * WIDTH, WIDTH), WIDTH)
    out_copies = []
    for j in (2, 1, 3, 0):
        cc = (head + j) % KVH
        for kind, (sent, got) in enumerate((
            (half_send.at[cc], half_recv.at[cc]),
            (stat_send.at[pl.ds(2 * cc, 2)], stat_recv.at[pl.ds(2 * cc, 2)]),
        )):
            remote(sent, got, h_send.at[2 * cc + kind], h_recv.at[2 * cc + kind], twin).wait_recv()
        own = top[cc]
        other = stat_recv[2 * cc + 1]
        new = jnp.maximum(own, other)
        own_part = jnp.exp2((own - new) * RATE)
        other_part = jnp.exp2((other - new) * RATE)
        total = acc[cc, HD:HD + 1] * own_part + stat_recv[2 * cc] * other_part
        own_part = own_part / total
        other_part = other_part / total
        done = (acc[cc, 0:HD] * own_part + half_recv[cc].astype(F32) * other_part).T.astype(BF)
        for g in range(GROUP):
            out_stage[j, :, g * HD:(g + 1) * HD] = done[g * TOK:(g + 1) * TOK, :]
        if j == 0:
            out_copies.append(pltpu.make_async_copy(
                out_stage.at[j], out_ref.at[:, columns], o_send.at[j]
            ))
        else:
            to = device(x, y, (z // KVH) * KVH + cc, core)
            out_copies.append(remote(
                out_stage.at[j], out_ref.at[:, columns], o_send.at[j], o_recv.at[j], to
            ))
        out_copies[-1].start()
    for copy in line_copies:
        copy.wait_send()
    for n in range(len(ROUTES)):
        route(n).wait_send()
    q_over.wait_send()
    pos_over.wait_send()
    for copies in over:
        for copy in copies:
            copy.wait_send()
    for j in (1, 2, 3):
        source = (head - j + KVH) % KVH
        place = out_ref.at[:, pl.ds(pl.multiple_of(source * WIDTH, WIDTH), WIDTH)]
        pltpu.make_async_copy(place, place, o_recv.at[j]).wait()
    for copy in out_copies[:3]:
        copy.wait_send()
    out_copies[3].wait()


def shards(queries, keys, values, order):
    dma = pltpu.SemaphoreType.DMA
    return pl.pallas_call(
        kernel,
        out_shape=jax.ShapeDtypeStruct((TOK, KVH * WIDTH), BF),
        in_specs=[pl.BlockSpec(memory_space=pl.ANY)] * 4,
        out_specs=pl.BlockSpec(memory_space=pl.ANY),
        scratch_shapes=[
            pltpu.VMEM((BLOCKS, BLOCK, HD), BF),
            pltpu.VMEM((KVH, 2, TOK, HD), BF),
            pltpu.VMEM((NZ, 2, TOK, HD), BF),
            pltpu.SMEM((TOK,), jnp.int32),
            pltpu.VMEM((1, 128), jnp.int32),
            pltpu.VMEM((NZ, 1, 128), jnp.int32),
            pltpu.VMEM((2, QTOK, WIDTH), BF),
            pltpu.VMEM((2, 1, 128), jnp.int32),
            pltpu.VMEM((ROWS, 2 * HD, 256), BF),
            pltpu.VMEM((ROWS, KEYS, 256), F32),
            pltpu.VMEM((ROWS, KEYS, 256), F32),
            pltpu.VMEM((ROWS, 1, 256), F32),
            pltpu.VMEM((ROWS, 1, 256), F32),
            pltpu.VMEM((ROWS, HD + TOK, 256), F32),
            pltpu.VMEM((ROWS, 1, 256), F32),
            pltpu.VMEM((4, HD, 256), BF),
            pltpu.VMEM((4, HD, 256), BF),
            pltpu.VMEM((8, 1, 256), F32),
            pltpu.VMEM((8, 1, 256), F32),
            pltpu.VMEM((4, TOK, WIDTH), BF),
            dma, dma, dma,
            dma((NZ - 1,)), dma((2,)), dma((NZ - 1,)), dma((2,)),
            dma((len(ROUTES),)), dma((BLOCKS,)), dma((2,)), dma((2,)),
            dma((8,)), dma((8,)), dma((4,)), dma((4,)),
        ],
        compiler_params=pltpu.CompilerParams(
            collective_id=0, has_side_effects=True, vmem_limit_bytes=60 * 1024 * 1024
        ),
        cost_estimate=pl.CostEstimate(
            flops=4 * 1024 * 8192 * 128, bytes_accessed=1 << 20, transcendentals=1024 * 8192
        ),
    )(queries, keys, values, order)


def solution(mesh):
    return jax.shard_map(
        shards,
        mesh=mesh,
        in_specs=(
            P("row", None),
            P(("row", "col"), None),
            P(("row", "col"), None),
            P(("row", "col")),
        ),
        out_specs=P(("row", "col"), None),
        check_vma=False,
    )
```

```python
import math

import jax
import jax.numpy as jnp
from jax import lax
from jax.experimental import pallas as pl
from jax.experimental.pallas import tpu as pltpu
from jax.sharding import PartitionSpec as P

HD = 128
KVH = 4
GROUP = 16
TOK = 16
NX, NY, NZ, NLO = 4, 4, 16, 8
QTOK = 64
WIDTH = GROUP * HD
HALF = 8
BKEYS = HALF * TOK
BLOCK = BKEYS + HD + TOK
KEYS = 2 * BKEYS
ROWS = 8
BF = jnp.bfloat16
F32 = jnp.float32
MASKED = -1e30
RATE = math.log2(math.e) / math.sqrt(HD)

ORDER = [
    (0, 0, 0), (1, 0, 0), (3, 0, 0), (0, 3, 0), (0, 0, 1), (1, 3, 0), (0, 1, 0), (3, 3, 0),
    (2, 0, 0), (1, 1, 0), (3, 0, 1), (3, 1, 0), (0, 3, 1), (0, 1, 1), (1, 0, 1), (2, 3, 0),
    (0, 2, 0), (2, 0, 1), (3, 3, 1), (2, 1, 0), (0, 2, 1), (3, 1, 1), (1, 3, 1), (1, 2, 0),
    (3, 2, 0), (2, 3, 1), (1, 1, 1), (3, 2, 1), (2, 1, 1), (1, 2, 1), (2, 2, 0), (2, 2, 1),
]
HELD = [
    4, 4, 6, 6, 10, 10, 11, 11, 12, 12,
    14, 16, 16, 16, 18, 18, 20, 20, 24, 24,
    24, 26, 26, 26, 28, 28, 30, 30, 32, 32,
]
BLOCKS = len(ORDER)
SLOT = {place: index for index, place in enumerate(ORDER)}
STEP = {"A-": (1, 0), "A+": (-1, 0), "B-": (0, 1), "B+": (0, -1)}


def onward(a, b, wave):
    ways = []
    if b == 0:
        if a == 0:
            ways += ["A-", "A+"]
        if (a, wave) == (1, 0):
            ways.append("A-")
        if (a, wave) == (3, 1):
            ways.append("A+")
        ways += ["B-", "B+"]
    if (b, wave) == (1, 0):
        ways.append("B-")
    if (b, wave) == (3, 1):
        ways.append("B+")
    return ways


ROUTES = []
for place in ORDER:
    for way in onward(*place):
        da, db = STEP[way]
        there = ((place[0] + da) % 4, (place[1] + db) % 4, place[2])
        ROUTES.append((SLOT[place], way, SLOT[there]))


def kernel(
    q_hbm, k_hbm, v_hbm, order_hbm, out_ref,
    mine, kv_own, stage, landed, order_own, pos_own, pos_line, q_raw, q_pos, q_t,
    even, odd, peak_even, peak_odd, acc, top, half_send, half_recv, stat_send, stat_recv, out_stage,
    q_sem, kv_sem, order_sem,
    z_send, z_recv, p_send, p_recv, f_send, m_recv, t_send, t_recv, h_send, h_recv, o_send, o_recv,
):
    row = lax.axis_index("row")
    col = lax.axis_index("col")
    core = row % 2
    x = (row // 2) % NX
    y = row // (4 * NX)
    z = ((row // (2 * NX)) % 2) * NLO + col
    head = col % KVH
    half = col // KVH

    order_copy = pltpu.make_async_copy(order_hbm, order_own, order_sem)
    order_copy.start()
    fetches = [
        pltpu.make_async_copy(array, kv_own.at[n], kv_sem.at[n])
        for n, array in enumerate((k_hbm, v_hbm))
    ]
    for fetch in fetches:
        fetch.start()
    q_copy = pltpu.make_async_copy(
        q_hbm.at[pl.ds(half * QTOK, QTOK), pl.ds(pl.multiple_of(head * WIDTH, WIDTH), WIDTH)],
        q_raw.at[0], q_sem,
    )
    q_copy.start()

    def device(x_at, y_at, z_at, core_at):
        return (y_at * (4 * NX) + (z_at // NLO) * (2 * NX) + x_at * 2 + core_at, z_at % NLO)

    line = [None] + [device(x, y, (z + d) % NZ, core) for d in range(1, NZ)]
    plane = {}
    for way, (da, db) in STEP.items():
        sx = (1 - core) * da + core * db
        sy = core * da + (1 - core) * db
        plane[way] = device((x - sx + NX) % NX, (y - sy + NY) % NY, z, core)
    twin = device(x, y, z, 1 - core)

    barrier = pltpu.get_barrier_semaphore()
    others = line[1:] + list(plane.values()) + [twin]
    for other in others:
        pl.semaphore_signal(barrier, inc=1, device_id=other, device_id_type=pl.DeviceIdType.MESH)

    order_copy.wait()
    pos_own[...] = jnp.full((1, 128), order_own[0], jnp.int32)
    for n, fetch in enumerate(fetches):
        fetch.wait()
        for g in range(KVH):
            stage[g, n] = kv_own[n, :, g * HD:(g + 1) * HD]
    pl.semaphore_wait(barrier, len(others))

    def remote(src, dst, send, recv, to):
        return pltpu.make_async_remote_copy(
            src_ref=src, dst_ref=dst, send_sem=send, recv_sem=recv,
            device_id=to, device_id_type=pl.DeviceIdType.MESH,
        )

    waves = ([12, 13, 3, 14, 2, 15, 1], [8, 7, 9, 6, 10, 5, 11, 4])

    def blocks_to_line(wave):
        return [
            remote(
                stage.at[(z + d) % KVH], landed.at[wave * HALF + (NZ - d) % HALF],
                z_send.at[d - 1], z_recv.at[wave], line[d],
            )
            for d in waves[wave]
        ]

    def positions_to_line(wave):
        return [
            remote(
                pos_own, pos_line.at[wave * HALF + (NZ - d) % HALF],
                p_send.at[d - 1], p_recv.at[wave], line[d],
            )
            for d in waves[wave]
        ]

    line_copies = (
        blocks_to_line(0) + positions_to_line(0) + positions_to_line(1) + blocks_to_line(1)
    )
    for copy in line_copies:
        copy.start()
    landed[0] = stage[head]
    pos_line[0] = pos_own[...]

    q_copy.wait()
    q_over = remote(q_raw.at[0], q_raw.at[1], t_send.at[0], t_recv.at[0], twin)
    q_over.start()

    def turn(side):
        for cc in range(4):
            rows = jnp.concatenate(
                [
                    q_raw[side, cc * TOK:(cc + 1) * TOK, g * HD:(g + 1) * HD]
                    for g in range(GROUP)
                ],
                axis=0,
            )
            token = lax.broadcasted_iota(jnp.int32, (HD, 256), 0)
            lane = lax.broadcasted_iota(jnp.int32, (HD, 256), 1)
            q_t[side * 4 + cc, 0:HD] = rows.T
            q_t[side * 4 + cc, HD:] = jnp.where(
                token == side * QTOK + cc * TOK + lane % TOK, 1.0, 0.0
            ).astype(BF)

    turn(0)
    q_over.wait_recv()
    turn(1)
    acc[...] = jnp.zeros_like(acc)
    top[...] = jnp.full_like(top, MASKED)

    lane16 = lax.broadcasted_iota(jnp.int32, (TOK, 128), 1)

    def collect(wave):
        first = 1 - wave
        got = pos_line.at[pl.ds(wave * HALF + first, HALF - first)]
        pltpu.make_async_copy(got, got, p_recv.at[wave]).wait()
        got = landed.at[pl.ds(wave * HALF + first, HALF - first)]
        pltpu.make_async_copy(got, got, z_recv.at[wave]).wait()
        slot = SLOT[(0, 0, wave)]
        places = [wave * HALF + d for d in range(HALF)]
        starts = jnp.concatenate([pos_line[d] for d in places * 2], axis=0)
        mine[slot, BKEYS + HD:] = jnp.where(
            lane16 < 64, starts // 128, starts % 128
        ).astype(F32).astype(BF)
        for d in range(HALF):
            mine[slot, d * TOK:(d + 1) * TOK] = landed[wave * HALF + d, 0]
        mine[slot, BKEYS:BKEYS + HD] = jnp.concatenate([landed[d, 1] for d in places], axis=0).T

    def route(n):
        slot, way, there = ROUTES[n]
        return remote(mine.at[slot], mine.at[there], f_send.at[n], m_recv.at[there], plane[way])

    def wait_mine(slot):
        pltpu.make_async_copy(mine.at[slot], mine.at[slot], m_recv.at[slot]).wait()

    def pass_on(slot):
        for n in range(len(ROUTES)):
            if ROUTES[n][0] == slot:
                route(n).start()

    collect(0)
    pass_on(0)

    lane1 = lax.broadcasted_iota(jnp.int32, (1, 128), 1)
    token_pos = jnp.zeros((1, 128), jnp.int32)
    for cc in range(4):
        token_pos = jnp.where(
            (lane1 % QTOK) // TOK == cc,
            pos_line[(cc - head + HALF) % HALF] + lane1 % TOK, token_pos,
        )
    q_pos[0] = token_pos
    pos_over = remote(q_pos.at[0], q_pos.at[1], t_send.at[1], t_recv.at[1], twin)
    pos_over.start()

    def receive(first, last):
        for slot in range(first, last):
            if slot == SLOT[(0, 0, 1)]:
                collect(1)
            else:
                wait_mine(slot)
            pass_on(slot)

    early = max(2, HELD[0] - 2)
    receive(1, early)
    pos_over.wait_recv()
    limit = (
        jnp.where(lane1 < QTOK, q_pos[0], q_pos[1]) - lax.broadcasted_iota(jnp.int32, (TOK, 128), 0)
    ).astype(F32)

    def augmented(slot):
        word = mine[slot, BKEYS + HD:].astype(F32)
        turned = pltpu.roll(word, 64, 1)
        start = jnp.where(lane16 < 64, word * 128.0 + turned, turned * 128.0 + word)
        bias = jnp.concatenate(
            [jnp.where(start[d:d + 1, :] <= limit, 0.0, MASKED).astype(BF) for d in range(HALF)],
            axis=0,
        )
        return jnp.concatenate([mine[slot, 0:BKEYS], bias], axis=1)

    def keys_of(s):
        return jnp.concatenate([augmented(2 * s), augmented(2 * s + 1)], axis=0)

    def values_of(s):
        parts = [mine[2 * s + k, BKEYS:BKEYS + HD] for k in (0, 1)]
        return jnp.concatenate(
            [jnp.concatenate(parts, axis=1), jnp.ones((TOK, KEYS), BF)], axis=0
        )

    def score(cc, keys, into, peak):
        scores = jnp.dot(keys, q_t[cc], preferred_element_type=F32)
        into[cc] = scores
        peak[cc] = jnp.max(scores, axis=0, keepdims=True)

    def absorb(cc, values, source, peak):
        old = top[cc]
        new = jnp.maximum(old, peak[cc])
        probs = jnp.exp2((source[cc] - new) * RATE).astype(BF)
        acc[cc] = acc[cc] * jnp.exp2((old - new) * RATE) + jnp.dot(
            values, probs, preferred_element_type=F32
        )
        top[cc] = new

    def step(s, source, peak, into, into_peak, between):
        for part in range(2):
            between(part)
            if part == 0:
                keys = keys_of(s + 1)
                values = values_of(s)
            for cc in range(4 * part, 4 * part + 4):
                score(cc, keys, into, into_peak)
                absorb(cc, values, source, peak)

    keys = keys_of(0)
    for cc in range(ROWS):
        score(cc, keys, even, peak_even)
    held = [early] + HELD
    step(
        0, even, peak_even, odd, peak_odd, lambda part: receive(held[part], held[part + 1])
    )

    def pair(i, carry):
        for k in range(2):
            def between(part):
                for v in range(7):
                    at = 2 * (2 * v + 1 + k) + part
                    if held[at] < held[at + 1]:
                        @pl.when(i == v)
                        def _():
                            receive(held[at], held[at + 1])

            s = 2 * i + 1 + k
            if k == 0:
                step(s, odd, peak_odd, even, peak_even, between)
            else:
                step(s, even, peak_even, odd, peak_odd, between)
        return carry

    lax.fori_loop(0, 7, pair, 0)

    values = values_of(15)
    over = []
    for cc in range(4):
        absorb(4 + cc, values, odd, peak_odd)
        half_send[cc] = acc[4 + cc, 0:HD].astype(BF)
        stat_send[2 * cc] = acc[4 + cc, HD:HD + 1]
        stat_send[2 * cc + 1] = top[4 + cc]
        over.append((
            remote(half_send.at[cc], half_recv.at[cc], h_send.at[2 * cc], h_recv.at[2 * cc], twin),
            remote(
                stat_send.at[pl.ds(2 * cc, 2)], stat_recv.at[pl.ds(2 * cc, 2)],
                h_send.at[2 * cc + 1], h_recv.at[2 * cc + 1], twin,
            ),
        ))
        for copy in over[-1]:
            copy.start()
    for cc in range(4):
        absorb(cc, values, odd, peak_odd)

    columns = pl.ds(pl.multiple_of(head * WIDTH, WIDTH), WIDTH)
    out_copies = []
    for j in (2, 1, 3, 0):
        cc = (head + j) % KVH
        for kind, (sent, got) in enumerate((
            (half_send.at[cc], half_recv.at[cc]),
            (stat_send.at[pl.ds(2 * cc, 2)], stat_recv.at[pl.ds(2 * cc, 2)]),
        )):
            remote(sent, got, h_send.at[2 * cc + kind], h_recv.at[2 * cc + kind], twin).wait_recv()
        own = top[cc]
        other = stat_recv[2 * cc + 1]
        new = jnp.maximum(own, other)
        own_part = jnp.exp2((own - new) * RATE)
        other_part = jnp.exp2((other - new) * RATE)
        total = acc[cc, HD:HD + 1] * own_part + stat_recv[2 * cc] * other_part
        own_part = own_part / total
        other_part = other_part / total
        done = (acc[cc, 0:HD] * own_part + half_recv[cc].astype(F32) * other_part).T.astype(BF)
        for g in range(GROUP):
            out_stage[j, :, g * HD:(g + 1) * HD] = done[g * TOK:(g + 1) * TOK, :]
        if j == 0:
            out_copies.append(pltpu.make_async_copy(
                out_stage.at[j], out_ref.at[:, columns], o_send.at[j]
            ))
        else:
            to = device(x, y, (z // KVH) * KVH + cc, core)
            out_copies.append(remote(
                out_stage.at[j], out_ref.at[:, columns], o_send.at[j], o_recv.at[j], to
            ))
        out_copies[-1].start()
    for copy in line_copies:
        copy.wait_send()
    for n in range(len(ROUTES)):
        route(n).wait_send()
    q_over.wait_send()
    pos_over.wait_send()
    for copies in over:
        for copy in copies:
            copy.wait_send()
    for j in (1, 2, 3):
        source = (head - j + KVH) % KVH
        place = out_ref.at[:, pl.ds(pl.multiple_of(source * WIDTH, WIDTH), WIDTH)]
        pltpu.make_async_copy(place, place, o_recv.at[j]).wait()
    for copy in out_copies[:3]:
        copy.wait_send()
    out_copies[3].wait()


def settle(source, target, sems):
    copies = [
        pltpu.make_async_copy(
            source.at[:, pl.ds(n * WIDTH, WIDTH)], target.at[:, pl.ds(n * WIDTH, WIDTH)], sems.at[n]
        )
        for n in range(KVH)
    ]
    for copy in copies:
        copy.start()
    for copy in copies:
        copy.wait()


def shards(queries, keys, values, order):
    dma = pltpu.SemaphoreType.DMA
    attended = pl.pallas_call(
        kernel,
        out_shape=jax.ShapeDtypeStruct((TOK, KVH * WIDTH), BF),
        in_specs=[pl.BlockSpec(memory_space=pl.ANY)] * 4,
        out_specs=pl.BlockSpec(memory_space=pl.ANY),
        scratch_shapes=[
            pltpu.VMEM((BLOCKS, BLOCK, HD), BF),
            pltpu.VMEM((2, TOK, KVH * HD), BF),
            pltpu.VMEM((KVH, 2, TOK, HD), BF),
            pltpu.VMEM((NZ, 2, TOK, HD), BF),
            pltpu.SMEM((TOK,), jnp.int32),
            pltpu.VMEM((1, 128), jnp.int32),
            pltpu.VMEM((NZ, 1, 128), jnp.int32),
            pltpu.VMEM((2, QTOK, WIDTH), BF),
            pltpu.VMEM((2, 1, 128), jnp.int32),
            pltpu.VMEM((ROWS, 2 * HD, 256), BF),
            pltpu.VMEM((ROWS, KEYS, 256), F32),
            pltpu.VMEM((ROWS, KEYS, 256), F32),
            pltpu.VMEM((ROWS, 1, 256), F32),
            pltpu.VMEM((ROWS, 1, 256), F32),
            pltpu.VMEM((ROWS, HD + TOK, 256), F32),
            pltpu.VMEM((ROWS, 1, 256), F32),
            pltpu.VMEM((4, HD, 256), BF),
            pltpu.VMEM((4, HD, 256), BF),
            pltpu.VMEM((8, 1, 256), F32),
            pltpu.VMEM((8, 1, 256), F32),
            pltpu.VMEM((4, TOK, WIDTH), BF),
            dma, dma((2,)), dma,
            dma((NZ - 1,)), dma((2,)), dma((NZ - 1,)), dma((2,)),
            dma((len(ROUTES),)), dma((BLOCKS,)), dma((2,)), dma((2,)),
            dma((8,)), dma((8,)), dma((4,)), dma((4,)),
        ],
        compiler_params=pltpu.CompilerParams(
            collective_id=0, has_side_effects=True, vmem_limit_bytes=60 * 1024 * 1024
        ),
        cost_estimate=pl.CostEstimate(
            flops=4 * 1024 * 8192 * 128, bytes_accessed=1 << 20, transcendentals=1024 * 8192
        ),
    )(queries, keys, values, order)
    return pl.pallas_call(
        settle,
        out_shape=jax.ShapeDtypeStruct((TOK, KVH * WIDTH), BF),
        in_specs=[pl.BlockSpec(memory_space=pl.ANY)],
        out_specs=pl.BlockSpec(memory_space=pl.ANY),
        scratch_shapes=[dma((KVH,))],
        compiler_params=pltpu.CompilerParams(vmem_limit_bytes=60 * 1024 * 1024),
    )(attended)


def solution(mesh):
    return jax.shard_map(
        shards,
        mesh=mesh,
        in_specs=(
            P("row", None),
            P(("row", "col"), None),
            P(("row", "col"), None),
            P(("row", "col")),
        ),
        out_specs=P(("row", "col"), None),
        check_vma=False,
    )
```

```python
import math

import jax
import jax.numpy as jnp
from jax import lax
from jax.experimental import pallas as pl
from jax.experimental.pallas import tpu as pltpu
from jax.sharding import PartitionSpec as P

HD = 128
KVH = 4
GROUP = 16
TOK = 16
NX, NY, NZ, NLO = 4, 4, 16, 8
QTOK = 64
WIDTH = GROUP * HD
HALF = 8
BKEYS = HALF * TOK
BLOCK = BKEYS + HD + TOK
KEYS = 2 * BKEYS
ROWS = 8
BF = jnp.bfloat16
F32 = jnp.float32
MASKED = -1e30
RATE = math.log2(math.e) / math.sqrt(HD)

ORDER = [
    (0, 0, 0), (1, 0, 0), (3, 0, 0), (0, 3, 0), (0, 1, 0), (0, 0, 1), (3, 3, 0), (1, 3, 0),
    (2, 0, 0), (1, 1, 0), (3, 0, 1), (0, 2, 0), (3, 1, 0), (1, 0, 1), (0, 1, 1), (2, 3, 0),
    (0, 3, 1), (2, 0, 1), (2, 1, 0), (3, 3, 1), (3, 1, 1), (1, 2, 0), (1, 3, 1), (0, 2, 1),
    (2, 3, 1), (1, 1, 1), (3, 2, 0), (2, 1, 1), (3, 2, 1), (1, 2, 1), (2, 2, 0), (2, 2, 1),
]
HELD = [
    4, 4, 6, 7, 8, 8, 10, 11, 12, 12,
    14, 17, 17, 17, 18, 19, 21, 21, 23, 23,
    24, 26, 27, 27, 28, 29, 30, 31, 32, 32,
]
BLOCKS = len(ORDER)
SLOT = {place: index for index, place in enumerate(ORDER)}
STEP = {"A-": (1, 0), "A+": (-1, 0), "B-": (0, 1), "B+": (0, -1)}


def onward(a, b, wave):
    ways = []
    if b == 0:
        if a == 0:
            ways += ["A-", "A+"]
        if (a, wave) == (1, 0):
            ways.append("A-")
        if (a, wave) == (3, 1):
            ways.append("A+")
        ways += ["B-", "B+"]
    if (b, wave) == (1, 0):
        ways.append("B-")
    if (b, wave) == (3, 1):
        ways.append("B+")
    return ways


ROUTES = []
for place in ORDER:
    for way in onward(*place):
        da, db = STEP[way]
        there = ((place[0] + da) % 4, (place[1] + db) % 4, place[2])
        ROUTES.append((SLOT[place], way, SLOT[there]))


def kernel(
    q_hbm, k_hbm, v_hbm, order_hbm, out_ref,
    mine, stage, landed, order_own, pos_own, pos_line, q_raw, q_pos, q_t,
    even, odd, peak_even, peak_odd, acc, top, half_send, half_recv, stat_send, stat_recv, out_stage,
    q_sem, kv_sem, order_sem,
    z_send, z_recv, p_send, p_recv, f_send, m_recv, t_send, t_recv, h_send, h_recv, o_send, o_recv,
):
    row = lax.axis_index("row")
    col = lax.axis_index("col")
    core = row % 2
    x = (row // 2) % NX
    y = row // (4 * NX)
    z = ((row // (2 * NX)) % 2) * NLO + col
    head = col % KVH
    half = col // KVH

    order_copy = pltpu.make_async_copy(order_hbm, order_own, order_sem)
    order_copy.start()
    for g in range(KVH):
        columns = slice(g * HD, (g + 1) * HD)
        pltpu.make_async_copy(k_hbm.at[:, columns], stage.at[g, 0], kv_sem).start()
        pltpu.make_async_copy(v_hbm.at[:, columns], stage.at[g, 1], kv_sem).start()
    q_copy = pltpu.make_async_copy(
        q_hbm.at[pl.ds(half * QTOK, QTOK), pl.ds(pl.multiple_of(head * WIDTH, WIDTH), WIDTH)],
        q_raw.at[0], q_sem,
    )
    q_copy.start()

    def device(x_at, y_at, z_at, core_at):
        return (y_at * (4 * NX) + (z_at // NLO) * (2 * NX) + x_at * 2 + core_at, z_at % NLO)

    line = [None] + [device(x, y, (z + d) % NZ, core) for d in range(1, NZ)]
    plane = {}
    for way, (da, db) in STEP.items():
        sx = (1 - core) * da + core * db
        sy = core * da + (1 - core) * db
        plane[way] = device((x - sx + NX) % NX, (y - sy + NY) % NY, z, core)
    twin = device(x, y, z, 1 - core)

    barrier = pltpu.get_barrier_semaphore()
    others = line[1:] + list(plane.values()) + [twin]
    for other in others:
        pl.semaphore_signal(barrier, inc=1, device_id=other, device_id_type=pl.DeviceIdType.MESH)

    order_copy.wait()
    pos_own[...] = jnp.full((1, 128), order_own[0], jnp.int32)
    pltpu.make_async_copy(stage, stage, kv_sem).wait()
    pl.semaphore_wait(barrier, len(others))

    def remote(src, dst, send, recv, to):
        return pltpu.make_async_remote_copy(
            src_ref=src, dst_ref=dst, send_sem=send, recv_sem=recv,
            device_id=to, device_id_type=pl.DeviceIdType.MESH,
        )

    waves = ([12, 13, 3, 14, 2, 15, 1], [8, 7, 9, 6, 10, 5, 11, 4])

    def blocks_to_line(wave):
        return [
            remote(
                stage.at[(z + d) % KVH], landed.at[wave * HALF + (NZ - d) % HALF],
                z_send.at[d - 1], z_recv.at[wave], line[d],
            )
            for d in waves[wave]
        ]

    def positions_to_line(wave):
        return [
            remote(
                pos_own, pos_line.at[wave * HALF + (NZ - d) % HALF],
                p_send.at[d - 1], p_recv.at[wave], line[d],
            )
            for d in waves[wave]
        ]

    line_copies = (
        blocks_to_line(1) + blocks_to_line(0) + positions_to_line(0) + positions_to_line(1)
    )
    for copy in line_copies:
        copy.start()
    landed[0] = stage[head]
    pos_line[0] = pos_own[...]

    q_copy.wait()
    q_over = remote(q_raw.at[0], q_raw.at[1], t_send.at[0], t_recv.at[0], twin)
    q_over.start()

    def turn(side):
        for cc in range(4):
            rows = jnp.concatenate(
                [
                    q_raw[side, cc * TOK:(cc + 1) * TOK, g * HD:(g + 1) * HD]
                    for g in range(GROUP)
                ],
                axis=0,
            )
            token = lax.broadcasted_iota(jnp.int32, (HD, 256), 0)
            lane = lax.broadcasted_iota(jnp.int32, (HD, 256), 1)
            q_t[side * 4 + cc, 0:HD] = rows.T
            q_t[side * 4 + cc, HD:] = jnp.where(
                token == side * QTOK + cc * TOK + lane % TOK, 1.0, 0.0
            ).astype(BF)

    turn(0)
    q_over.wait_recv()
    turn(1)
    acc[...] = jnp.zeros_like(acc)
    top[...] = jnp.full_like(top, MASKED)

    lane16 = lax.broadcasted_iota(jnp.int32, (TOK, 128), 1)

    def collect(wave):
        first = 1 - wave
        got = pos_line.at[pl.ds(wave * HALF + first, HALF - first)]
        pltpu.make_async_copy(got, got, p_recv.at[wave]).wait()
        got = landed.at[pl.ds(wave * HALF + first, HALF - first)]
        pltpu.make_async_copy(got, got, z_recv.at[wave]).wait()
        slot = SLOT[(0, 0, wave)]
        places = [wave * HALF + d for d in range(HALF)]
        starts = jnp.concatenate([pos_line[d] for d in places * 2], axis=0)
        mine[slot, BKEYS + HD:] = jnp.where(
            lane16 < 64, starts // 128, starts % 128
        ).astype(F32).astype(BF)
        for d in range(HALF):
            mine[slot, d * TOK:(d + 1) * TOK] = landed[wave * HALF + d, 0]
        mine[slot, BKEYS:BKEYS + HD] = jnp.concatenate([landed[d, 1] for d in places], axis=0).T

    def route(n):
        slot, way, there = ROUTES[n]
        return remote(mine.at[slot], mine.at[there], f_send.at[n], m_recv.at[there], plane[way])

    def wait_mine(slot):
        pltpu.make_async_copy(mine.at[slot], mine.at[slot], m_recv.at[slot]).wait()

    def pass_on(slot):
        for n in range(len(ROUTES)):
            if ROUTES[n][0] == slot:
                route(n).start()

    collect(0)
    pass_on(0)

    lane1 = lax.broadcasted_iota(jnp.int32, (1, 128), 1)
    token_pos = jnp.zeros((1, 128), jnp.int32)
    for cc in range(4):
        token_pos = jnp.where(
            (lane1 % QTOK) // TOK == cc,
            pos_line[(cc - head + HALF) % HALF] + lane1 % TOK, token_pos,
        )
    q_pos[0] = token_pos
    pos_over = remote(q_pos.at[0], q_pos.at[1], t_send.at[1], t_recv.at[1], twin)
    pos_over.start()

    def receive(first, last):
        for slot in range(first, last):
            if slot == SLOT[(0, 0, 1)]:
                collect(1)
            else:
                wait_mine(slot)
            pass_on(slot)

    early = max(2, HELD[0] - 2)
    receive(1, early)
    pos_over.wait_recv()
    limit = (
        jnp.where(lane1 < QTOK, q_pos[0], q_pos[1]) - lax.broadcasted_iota(jnp.int32, (TOK, 128), 0)
    ).astype(F32)

    def augmented(slot):
        word = mine[slot, BKEYS + HD:].astype(F32)
        turned = pltpu.roll(word, 64, 1)
        start = jnp.where(lane16 < 64, word * 128.0 + turned, turned * 128.0 + word)
        bias = jnp.concatenate(
            [jnp.where(start[d:d + 1, :] <= limit, 0.0, MASKED).astype(BF) for d in range(HALF)],
            axis=0,
        )
        return jnp.concatenate([mine[slot, 0:BKEYS], bias], axis=1)

    def keys_of(s):
        return jnp.concatenate([augmented(2 * s), augmented(2 * s + 1)], axis=0)

    def values_of(s):
        parts = [mine[2 * s + k, BKEYS:BKEYS + HD] for k in (0, 1)]
        return jnp.concatenate(
            [jnp.concatenate(parts, axis=1), jnp.ones((TOK, KEYS), BF)], axis=0
        )

    def score(cc, keys, into, peak):
        scores = jnp.dot(keys, q_t[cc], preferred_element_type=F32)
        into[cc] = scores
        peak[cc] = jnp.max(scores, axis=0, keepdims=True)

    def absorb(cc, values, source, peak):
        old = top[cc]
        new = jnp.maximum(old, peak[cc])
        probs = jnp.exp2((source[cc] - new) * RATE).astype(BF)
        acc[cc] = acc[cc] * jnp.exp2((old - new) * RATE) + jnp.dot(
            values, probs, preferred_element_type=F32
        )
        top[cc] = new

    def step(s, source, peak, into, into_peak, between):
        for part in range(2):
            between(part)
            if part == 0:
                keys = keys_of(s + 1)
                values = values_of(s)
            for cc in range(4 * part, 4 * part + 4):
                score(cc, keys, into, into_peak)
                absorb(cc, values, source, peak)

    keys = keys_of(0)
    for cc in range(ROWS):
        score(cc, keys, even, peak_even)
    held = [early] + HELD
    step(
        0, even, peak_even, odd, peak_odd, lambda part: receive(held[part], held[part + 1])
    )

    def pair(i, carry):
        for k in range(2):
            def between(part):
                for v in range(7):
                    at = 2 * (2 * v + 1 + k) + part
                    if held[at] < held[at + 1]:
                        @pl.when(i == v)
                        def _():
                            receive(held[at], held[at + 1])

            s = 2 * i + 1 + k
            if k == 0:
                step(s, odd, peak_odd, even, peak_even, between)
            else:
                step(s, even, peak_even, odd, peak_odd, between)
        return carry

    lax.fori_loop(0, 7, pair, 0)

    values = values_of(15)
    over = []
    for cc in range(4):
        absorb(4 + cc, values, odd, peak_odd)
        half_send[cc] = acc[4 + cc, 0:HD].astype(BF)
        stat_send[2 * cc] = acc[4 + cc, HD:HD + 1]
        stat_send[2 * cc + 1] = top[4 + cc]
        over.append((
            remote(half_send.at[cc], half_recv.at[cc], h_send.at[2 * cc], h_recv.at[2 * cc], twin),
            remote(
                stat_send.at[pl.ds(2 * cc, 2)], stat_recv.at[pl.ds(2 * cc, 2)],
                h_send.at[2 * cc + 1], h_recv.at[2 * cc + 1], twin,
            ),
        ))
        for copy in over[-1]:
            copy.start()
    for cc in range(4):
        absorb(cc, values, odd, peak_odd)

    columns = pl.ds(pl.multiple_of(head * WIDTH, WIDTH), WIDTH)
    out_copies = []
    for j in (2, 1, 3, 0):
        cc = (head + j) % KVH
        for kind, (sent, got) in enumerate((
            (half_send.at[cc], half_recv.at[cc]),
            (stat_send.at[pl.ds(2 * cc, 2)], stat_recv.at[pl.ds(2 * cc, 2)]),
        )):
            remote(sent, got, h_send.at[2 * cc + kind], h_recv.at[2 * cc + kind], twin).wait_recv()
        own = top[cc]
        other = stat_recv[2 * cc + 1]
        new = jnp.maximum(own, other)
        own_part = jnp.exp2((own - new) * RATE)
        other_part = jnp.exp2((other - new) * RATE)
        total = acc[cc, HD:HD + 1] * own_part + stat_recv[2 * cc] * other_part
        own_part = own_part / total
        other_part = other_part / total
        done = (acc[cc, 0:HD] * own_part + half_recv[cc].astype(F32) * other_part).T.astype(BF)
        for g in range(GROUP):
            out_stage[j, :, g * HD:(g + 1) * HD] = done[g * TOK:(g + 1) * TOK, :]
        if j == 0:
            out_copies.append(pltpu.make_async_copy(
                out_stage.at[j], out_ref.at[:, columns], o_send.at[j]
            ))
        else:
            to = device(x, y, (z // KVH) * KVH + cc, core)
            out_copies.append(remote(
                out_stage.at[j], out_ref.at[:, columns], o_send.at[j], o_recv.at[j], to
            ))
        out_copies[-1].start()
    for copy in line_copies:
        copy.wait_send()
    for n in range(len(ROUTES)):
        route(n).wait_send()
    q_over.wait_send()
    pos_over.wait_send()
    for copies in over:
        for copy in copies:
            copy.wait_send()
    for j in (1, 2, 3):
        source = (head - j + KVH) % KVH
        place = out_ref.at[:, pl.ds(pl.multiple_of(source * WIDTH, WIDTH), WIDTH)]
        pltpu.make_async_copy(place, place, o_recv.at[j]).wait()
    for copy in out_copies[:3]:
        copy.wait_send()
    out_copies[3].wait()


def shards(queries, keys, values, order):
    dma = pltpu.SemaphoreType.DMA
    return pl.pallas_call(
        kernel,
        out_shape=jax.ShapeDtypeStruct((TOK, KVH * WIDTH), BF),
        in_specs=[pl.BlockSpec(memory_space=pl.ANY)] * 4,
        out_specs=pl.BlockSpec(memory_space=pl.ANY),
        scratch_shapes=[
            pltpu.VMEM((BLOCKS, BLOCK, HD), BF),
            pltpu.VMEM((KVH, 2, TOK, HD), BF),
            pltpu.VMEM((NZ, 2, TOK, HD), BF),
            pltpu.SMEM((TOK,), jnp.int32),
            pltpu.VMEM((1, 128), jnp.int32),
            pltpu.VMEM((NZ, 1, 128), jnp.int32),
            pltpu.VMEM((2, QTOK, WIDTH), BF),
            pltpu.VMEM((2, 1, 128), jnp.int32),
            pltpu.VMEM((ROWS, 2 * HD, 256), BF),
            pltpu.VMEM((ROWS, KEYS, 256), F32),
            pltpu.VMEM((ROWS, KEYS, 256), F32),
            pltpu.VMEM((ROWS, 1, 256), F32),
            pltpu.VMEM((ROWS, 1, 256), F32),
            pltpu.VMEM((ROWS, HD + TOK, 256), F32),
            pltpu.VMEM((ROWS, 1, 256), F32),
            pltpu.VMEM((4, HD, 256), BF),
            pltpu.VMEM((4, HD, 256), BF),
            pltpu.VMEM((8, 1, 256), F32),
            pltpu.VMEM((8, 1, 256), F32),
            pltpu.VMEM((4, TOK, WIDTH), BF),
            dma, dma, dma,
            dma((NZ - 1,)), dma((2,)), dma((NZ - 1,)), dma((2,)),
            dma((len(ROUTES),)), dma((BLOCKS,)), dma((2,)), dma((2,)),
            dma((8,)), dma((8,)), dma((4,)), dma((4,)),
        ],
        compiler_params=pltpu.CompilerParams(
            collective_id=0, has_side_effects=True, vmem_limit_bytes=60 * 1024 * 1024
        ),
        cost_estimate=pl.CostEstimate(
            flops=4 * 1024 * 8192 * 128, bytes_accessed=1 << 20, transcendentals=1024 * 8192
        ),
    )(queries, keys, values, order)


def solution(mesh):
    return jax.shard_map(
        shards,
        mesh=mesh,
        in_specs=(
            P("row", None),
            P(("row", "col"), None),
            P(("row", "col"), None),
            P(("row", "col")),
        ),
        out_specs=P(("row", "col"), None),
        check_vma=False,
    )
```

```python
import math

import jax
import jax.numpy as jnp
from jax import lax
from jax.experimental import pallas as pl
from jax.experimental.pallas import tpu as pltpu
from jax.sharding import PartitionSpec as P

HD = 128
KVH = 4
GROUP = 16
TOK = 16
NX, NY, NZ, NLO = 4, 4, 16, 8
QTOK = 64
WIDTH = GROUP * HD
HALF = 8
BKEYS = HALF * TOK
BLOCK = BKEYS + HD + TOK
KEYS = 2 * BKEYS
ROWS = 8
BF = jnp.bfloat16
F32 = jnp.float32
MASKED = -1e30
RATE = math.log2(math.e) / math.sqrt(HD)

ORDER = [
    (0, 0, 0), (1, 0, 0), (3, 0, 0), (0, 3, 0), (0, 0, 1), (1, 3, 0), (0, 1, 0), (3, 3, 0),
    (2, 0, 0), (1, 1, 0), (3, 0, 1), (3, 1, 0), (0, 3, 1), (0, 1, 1), (1, 0, 1), (2, 3, 0),
    (0, 2, 0), (2, 0, 1), (3, 3, 1), (2, 1, 0), (0, 2, 1), (3, 1, 1), (1, 3, 1), (1, 2, 0),
    (3, 2, 0), (2, 3, 1), (1, 1, 1), (3, 2, 1), (2, 1, 1), (1, 2, 1), (2, 2, 0), (2, 2, 1),
]
HELD = [
    4, 4, 6, 6, 10, 10, 11, 11, 12, 12,
    14, 16, 16, 16, 18, 18, 20, 20, 24, 24,
    24, 26, 26, 26, 28, 28, 30, 30, 32, 32,
]
BLOCKS = len(ORDER)
SLOT = {place: index for index, place in enumerate(ORDER)}
STEP = {"A-": (1, 0), "A+": (-1, 0), "B-": (0, 1), "B+": (0, -1)}


def onward(a, b, wave):
    ways = []
    if b == 0:
        if a == 0:
            ways += ["A-", "A+"]
        if (a, wave) == (1, 0):
            ways.append("A-")
        if (a, wave) == (3, 1):
            ways.append("A+")
        ways += ["B-", "B+"]
    if (b, wave) == (1, 0):
        ways.append("B-")
    if (b, wave) == (3, 1):
        ways.append("B+")
    return ways


ROUTES = []
for place in ORDER:
    for way in onward(*place):
        da, db = STEP[way]
        there = ((place[0] + da) % 4, (place[1] + db) % 4, place[2])
        ROUTES.append((SLOT[place], way, SLOT[there]))


def kernel(
    q_hbm, k_hbm, v_hbm, order_hbm, out_ref,
    mine, stage, landed, order_own, q_raw, q_pos, q_t,
    even, odd, peak_even, peak_odd, acc, top, half_send, half_recv, stat_send, stat_recv, out_stage,
    q_sem, kv_sem, order_sem,
    z_send, z_recv, f_send, m_recv, t_send, t_recv, h_send, h_recv, o_send, o_recv,
):
    row = lax.axis_index("row")
    col = lax.axis_index("col")
    core = row % 2
    x = (row // 2) % NX
    y = row // (4 * NX)
    z = ((row // (2 * NX)) % 2) * NLO + col
    head = col % KVH
    half = col // KVH

    order_copy = pltpu.make_async_copy(order_hbm, order_own, order_sem)
    order_copy.start()
    for g in range(KVH):
        columns = slice(g * HD, (g + 1) * HD)
        pltpu.make_async_copy(k_hbm.at[:, columns], stage.at[g, 0], kv_sem).start()
        pltpu.make_async_copy(v_hbm.at[:, columns], stage.at[g, 1], kv_sem).start()
    q_copy = pltpu.make_async_copy(
        q_hbm.at[pl.ds(half * QTOK, QTOK), pl.ds(pl.multiple_of(head * WIDTH, WIDTH), WIDTH)],
        q_raw.at[0], q_sem,
    )
    q_copy.start()

    def device(x_at, y_at, z_at, core_at):
        return (y_at * (4 * NX) + (z_at // NLO) * (2 * NX) + x_at * 2 + core_at, z_at % NLO)

    line = [None] + [device(x, y, (z + d) % NZ, core) for d in range(1, NZ)]
    plane = {}
    for way, (da, db) in STEP.items():
        sx = (1 - core) * da + core * db
        sy = core * da + (1 - core) * db
        plane[way] = device((x - sx + NX) % NX, (y - sy + NY) % NY, z, core)
    twin = device(x, y, z, 1 - core)

    barrier = pltpu.get_barrier_semaphore()
    others = line[1:] + list(plane.values()) + [twin]
    for other in others:
        pl.semaphore_signal(barrier, inc=1, device_id=other, device_id_type=pl.DeviceIdType.MESH)

    order_copy.wait()
    lane16 = lax.broadcasted_iota(jnp.int32, (TOK, 128), 1)
    start_own = jnp.full((TOK, 128), order_own[0], jnp.int32)
    start_own = jnp.where(lane16 < 64, start_own // 128, start_own % 128).astype(F32).astype(BF)
    for g in range(KVH):
        stage[g, 2] = start_own
    fetched = stage.at[:, pl.ds(0, 2)]
    pltpu.make_async_copy(fetched, fetched, kv_sem).wait()
    pl.semaphore_wait(barrier, len(others))

    def remote(src, dst, send, recv, to):
        return pltpu.make_async_remote_copy(
            src_ref=src, dst_ref=dst, send_sem=send, recv_sem=recv,
            device_id=to, device_id_type=pl.DeviceIdType.MESH,
        )

    line_copies = []
    for wave, ds in enumerate(([12, 13, 3, 14, 2, 15, 1], [8, 7, 9, 6, 10, 5, 11, 4])):
        for d in ds:
            at = wave * HALF + (NZ - d) % HALF
            line_copies.append(remote(
                stage.at[(z + d) % KVH], landed.at[at], z_send.at[d - 1], z_recv.at[wave], line[d]
            ))
    for copy in line_copies:
        copy.start()
    landed[0] = stage[head]

    q_copy.wait()
    q_over = remote(q_raw.at[0], q_raw.at[1], t_send.at[0], t_recv.at[0], twin)
    q_over.start()

    def turn(side):
        for cc in range(4):
            rows = jnp.concatenate(
                [
                    q_raw[side, cc * TOK:(cc + 1) * TOK, g * HD:(g + 1) * HD]
                    for g in range(GROUP)
                ],
                axis=0,
            )
            token = lax.broadcasted_iota(jnp.int32, (HD, 256), 0)
            lane = lax.broadcasted_iota(jnp.int32, (HD, 256), 1)
            q_t[side * 4 + cc, 0:HD] = rows.T
            q_t[side * 4 + cc, HD:] = jnp.where(
                token == side * QTOK + cc * TOK + lane % TOK, 1.0, 0.0
            ).astype(BF)

    turn(0)
    q_over.wait_recv()
    turn(1)
    acc[...] = jnp.zeros_like(acc)
    top[...] = jnp.full_like(top, MASKED)

    def collect(wave):
        first = 1 - wave
        got = landed.at[pl.ds(wave * HALF + first, HALF - first)]
        pltpu.make_async_copy(got, got, z_recv.at[wave]).wait()
        slot = SLOT[(0, 0, wave)]
        places = [wave * HALF + d for d in range(HALF)]
        mine[slot, BKEYS + HD:] = jnp.concatenate(
            [landed[d, 2].astype(F32)[0:1] for d in places * 2], axis=0
        ).astype(BF)
        for d in range(HALF):
            mine[slot, d * TOK:(d + 1) * TOK] = landed[wave * HALF + d, 0]
        mine[slot, BKEYS:BKEYS + HD] = jnp.concatenate([landed[d, 1] for d in places], axis=0).T

    def route(n):
        slot, way, there = ROUTES[n]
        return remote(mine.at[slot], mine.at[there], f_send.at[n], m_recv.at[there], plane[way])

    def wait_mine(slot):
        pltpu.make_async_copy(mine.at[slot], mine.at[slot], m_recv.at[slot]).wait()

    def pass_on(slot):
        for n in range(len(ROUTES)):
            if ROUTES[n][0] == slot:
                route(n).start()

    collect(0)
    pass_on(0)

    def decode(word):
        turned = pltpu.roll(word, 64, 1)
        return jnp.where(lane16 < 64, word * 128.0 + turned, turned * 128.0 + word)

    lane1 = lax.broadcasted_iota(jnp.int32, (1, 128), 1)
    token_pos = jnp.zeros((1, 128), F32)
    for cc in range(4):
        start = decode(landed[(cc - head + HALF) % HALF, 2].astype(F32))[0:1]
        token_pos = jnp.where(
            (lane1 % QTOK) // TOK == cc, start + (lane1 % TOK).astype(F32), token_pos
        )
    q_pos[0] = token_pos
    pos_over = remote(q_pos.at[0], q_pos.at[1], t_send.at[1], t_recv.at[1], twin)
    pos_over.start()

    def receive(first, last):
        for slot in range(first, last):
            if slot == SLOT[(0, 0, 1)]:
                collect(1)
            else:
                wait_mine(slot)
            pass_on(slot)

    early = max(2, HELD[0] - 2)
    receive(1, early)
    pos_over.wait_recv()
    offset = lax.broadcasted_iota(jnp.int32, (TOK, 128), 0).astype(F32)
    limit = jnp.where(lane1 < QTOK, q_pos[0], q_pos[1]) - offset

    def augmented(slot):
        start = decode(mine[slot, BKEYS + HD:].astype(F32))
        bias = jnp.concatenate(
            [jnp.where(start[d:d + 1, :] <= limit, 0.0, MASKED).astype(BF) for d in range(HALF)],
            axis=0,
        )
        return jnp.concatenate([mine[slot, 0:BKEYS], bias], axis=1)

    def keys_of(s):
        return jnp.concatenate([augmented(2 * s), augmented(2 * s + 1)], axis=0)

    def values_of(s):
        parts = [mine[2 * s + k, BKEYS:BKEYS + HD] for k in (0, 1)]
        return jnp.concatenate(
            [jnp.concatenate(parts, axis=1), jnp.ones((TOK, KEYS), BF)], axis=0
        )

    def score(cc, keys, into, peak):
        scores = jnp.dot(keys, q_t[cc], preferred_element_type=F32)
        into[cc] = scores
        peak[cc] = jnp.max(scores, axis=0, keepdims=True)

    def absorb(cc, values, source, peak):
        old = top[cc]
        new = jnp.maximum(old, peak[cc])
        probs = jnp.exp2((source[cc] - new) * RATE).astype(BF)
        acc[cc] = acc[cc] * jnp.exp2((old - new) * RATE) + jnp.dot(
            values, probs, preferred_element_type=F32
        )
        top[cc] = new

    def step(s, source, peak, into, into_peak, between):
        for part in range(2):
            between(part)
            if part == 0:
                keys = keys_of(s + 1)
                values = values_of(s)
            for cc in range(4 * part, 4 * part + 4):
                score(cc, keys, into, into_peak)
                absorb(cc, values, source, peak)

    keys = keys_of(0)
    for cc in range(ROWS):
        score(cc, keys, even, peak_even)
    held = [early] + HELD
    step(
        0, even, peak_even, odd, peak_odd, lambda part: receive(held[part], held[part + 1])
    )

    def pair(i, carry):
        for k in range(2):
            def between(part):
                for v in range(7):
                    at = 2 * (2 * v + 1 + k) + part
                    if held[at] < held[at + 1]:
                        @pl.when(i == v)
                        def _():
                            receive(held[at], held[at + 1])

            s = 2 * i + 1 + k
            if k == 0:
                step(s, odd, peak_odd, even, peak_even, between)
            else:
                step(s, even, peak_even, odd, peak_odd, between)
        return carry

    lax.fori_loop(0, 7, pair, 0)

    values = values_of(15)
    over = []
    for cc in range(4):
        absorb(4 + cc, values, odd, peak_odd)
        half_send[cc] = acc[4 + cc, 0:HD].astype(BF)
        stat_send[2 * cc] = acc[4 + cc, HD:HD + 1]
        stat_send[2 * cc + 1] = top[4 + cc]
        over.append((
            remote(half_send.at[cc], half_recv.at[cc], h_send.at[2 * cc], h_recv.at[2 * cc], twin),
            remote(
                stat_send.at[pl.ds(2 * cc, 2)], stat_recv.at[pl.ds(2 * cc, 2)],
                h_send.at[2 * cc + 1], h_recv.at[2 * cc + 1], twin,
            ),
        ))
        for copy in over[-1]:
            copy.start()
    for cc in range(4):
        absorb(cc, values, odd, peak_odd)

    columns = pl.ds(pl.multiple_of(head * WIDTH, WIDTH), WIDTH)
    out_copies = []
    for j in (2, 1, 3, 0):
        cc = (head + j) % KVH
        for kind, (sent, got) in enumerate((
            (half_send.at[cc], half_recv.at[cc]),
            (stat_send.at[pl.ds(2 * cc, 2)], stat_recv.at[pl.ds(2 * cc, 2)]),
        )):
            remote(sent, got, h_send.at[2 * cc + kind], h_recv.at[2 * cc + kind], twin).wait_recv()
        own = top[cc]
        other = stat_recv[2 * cc + 1]
        new = jnp.maximum(own, other)
        own_part = jnp.exp2((own - new) * RATE)
        other_part = jnp.exp2((other - new) * RATE)
        total = acc[cc, HD:HD + 1] * own_part + stat_recv[2 * cc] * other_part
        own_part = own_part / total
        other_part = other_part / total
        done = (acc[cc, 0:HD] * own_part + half_recv[cc].astype(F32) * other_part).T.astype(BF)
        for g in range(GROUP):
            out_stage[j, :, g * HD:(g + 1) * HD] = done[g * TOK:(g + 1) * TOK, :]
        if j == 0:
            out_copies.append(pltpu.make_async_copy(
                out_stage.at[j], out_ref.at[:, columns], o_send.at[j]
            ))
        else:
            to = device(x, y, (z // KVH) * KVH + cc, core)
            out_copies.append(remote(
                out_stage.at[j], out_ref.at[:, columns], o_send.at[j], o_recv.at[j], to
            ))
        out_copies[-1].start()
    for copy in line_copies:
        copy.wait_send()
    for n in range(len(ROUTES)):
        route(n).wait_send()
    q_over.wait_send()
    pos_over.wait_send()
    for copies in over:
        for copy in copies:
            copy.wait_send()
    for j in (1, 2, 3):
        source = (head - j + KVH) % KVH
        place = out_ref.at[:, pl.ds(pl.multiple_of(source * WIDTH, WIDTH), WIDTH)]
        pltpu.make_async_copy(place, place, o_recv.at[j]).wait()
    for copy in out_copies[:3]:
        copy.wait_send()
    out_copies[3].wait()


def shards(queries, keys, values, order):
    dma = pltpu.SemaphoreType.DMA
    return pl.pallas_call(
        kernel,
        out_shape=jax.ShapeDtypeStruct((TOK, KVH * WIDTH), BF),
        in_specs=[pl.BlockSpec(memory_space=pl.ANY)] * 4,
        out_specs=pl.BlockSpec(memory_space=pl.ANY),
        scratch_shapes=[
            pltpu.VMEM((BLOCKS, BLOCK, HD), BF),
            pltpu.VMEM((KVH, 3, TOK, HD), BF),
            pltpu.VMEM((NZ, 3, TOK, HD), BF),
            pltpu.SMEM((TOK,), jnp.int32),
            pltpu.VMEM((2, QTOK, WIDTH), BF),
            pltpu.VMEM((2, 1, 128), F32),
            pltpu.VMEM((ROWS, 2 * HD, 256), BF),
            pltpu.VMEM((ROWS, KEYS, 256), F32),
            pltpu.VMEM((ROWS, KEYS, 256), F32),
            pltpu.VMEM((ROWS, 1, 256), F32),
            pltpu.VMEM((ROWS, 1, 256), F32),
            pltpu.VMEM((ROWS, HD + TOK, 256), F32),
            pltpu.VMEM((ROWS, 1, 256), F32),
            pltpu.VMEM((4, HD, 256), BF),
            pltpu.VMEM((4, HD, 256), BF),
            pltpu.VMEM((8, 1, 256), F32),
            pltpu.VMEM((8, 1, 256), F32),
            pltpu.VMEM((4, TOK, WIDTH), BF),
            dma, dma, dma,
            dma((NZ - 1,)), dma((2,)),
            dma((len(ROUTES),)), dma((BLOCKS,)), dma((2,)), dma((2,)),
            dma((8,)), dma((8,)), dma((4,)), dma((4,)),
        ],
        compiler_params=pltpu.CompilerParams(
            collective_id=0, has_side_effects=True, vmem_limit_bytes=60 * 1024 * 1024
        ),
        cost_estimate=pl.CostEstimate(
            flops=4 * 1024 * 8192 * 128, bytes_accessed=1 << 20, transcendentals=1024 * 8192
        ),
    )(queries, keys, values, order)


def solution(mesh):
    return jax.shard_map(
        shards,
        mesh=mesh,
        in_specs=(
            P("row", None),
            P(("row", "col"), None),
            P(("row", "col"), None),
            P(("row", "col")),
        ),
        out_specs=P(("row", "col"), None),
        check_vma=False,
    )
```

```python
import math

import jax
import jax.numpy as jnp
from jax import lax
from jax.experimental import pallas as pl
from jax.experimental.pallas import tpu as pltpu
from jax.sharding import PartitionSpec as P

HD = 128
KVH = 4
GROUP = 16
TOK = 16
NX, NY, NZ, NLO = 4, 4, 16, 8
QTOK = 64
WIDTH = GROUP * HD
HALF = 8
BKEYS = HALF * TOK
BLOCK = BKEYS + HD + TOK
KEYS = 2 * BKEYS
ROWS = 8
BF = jnp.bfloat16
F32 = jnp.float32
MASKED = -1e30
RATE = math.log2(math.e) / math.sqrt(HD)

ORDER = [
    (0, 0, 0), (1, 0, 0), (3, 0, 0), (0, 3, 0), (0, 0, 1), (1, 3, 0), (0, 1, 0), (3, 3, 0),
    (2, 0, 0), (1, 1, 0), (3, 0, 1), (3, 1, 0), (0, 3, 1), (0, 1, 1), (1, 0, 1), (2, 3, 0),
    (0, 2, 0), (2, 0, 1), (3, 3, 1), (2, 1, 0), (0, 2, 1), (3, 1, 1), (1, 3, 1), (1, 2, 0),
    (3, 2, 0), (2, 3, 1), (1, 1, 1), (3, 2, 1), (2, 1, 1), (1, 2, 1), (2, 2, 0), (2, 2, 1),
]
HELD = [
    4, 4, 6, 6, 10, 10, 11, 11, 12, 12,
    14, 16, 16, 16, 18, 18, 20, 20, 24, 24,
    24, 26, 26, 26, 28, 28, 30, 30, 32, 32,
]
BLOCKS = len(ORDER)
SLOT = {place: index for index, place in enumerate(ORDER)}
STEP = {"A-": (1, 0), "A+": (-1, 0), "B-": (0, 1), "B+": (0, -1)}


def onward(a, b, wave):
    ways = []
    if b == 0:
        if a == 0:
            ways += ["A-", "A+"]
        if (a, wave) == (1, 0):
            ways.append("A-")
        if (a, wave) == (3, 1):
            ways.append("A+")
        ways += ["B-", "B+"]
    if (b, wave) == (1, 0):
        ways.append("B-")
    if (b, wave) == (3, 1):
        ways.append("B+")
    return ways


ROUTES = []
for place in ORDER:
    for way in onward(*place):
        da, db = STEP[way]
        there = ((place[0] + da) % 4, (place[1] + db) % 4, place[2])
        ROUTES.append((SLOT[place], way, SLOT[there]))


def kernel(
    q_hbm, k_hbm, v_hbm, order_hbm, out_ref,
    mine, stage, landed, order_own, pos_own, pos_line, q_raw, q_pos, q_t,
    even, odd, peak_even, peak_odd, acc, top, half_send, half_recv, stat_send, stat_recv, out_stage,
    q_sem, kv_sem, order_sem,
    z_send, z_recv, p_send, p_recv, f_send, m_recv, t_send, t_recv, h_send, h_recv, o_send, o_recv,
):
    row = lax.axis_index("row")
    col = lax.axis_index("col")
    core = row % 2
    x = (row // 2) % NX
    y = row // (4 * NX)
    z = ((row // (2 * NX)) % 2) * NLO + col
    head = col % KVH
    half = col // KVH

    order_copy = pltpu.make_async_copy(order_hbm, order_own, order_sem)
    order_copy.start()
    for g in range(KVH):
        columns = slice(g * HD, (g + 1) * HD)
        pltpu.make_async_copy(k_hbm.at[:, columns], stage.at[g, 0], kv_sem).start()
        pltpu.make_async_copy(v_hbm.at[:, columns], stage.at[g, 1], kv_sem).start()
    q_copy = pltpu.make_async_copy(
        q_hbm.at[pl.ds(half * QTOK, QTOK), pl.ds(pl.multiple_of(head * WIDTH, WIDTH), WIDTH)],
        q_raw.at[0], q_sem,
    )
    q_copy.start()

    def device(x_at, y_at, z_at, core_at):
        return (y_at * (4 * NX) + (z_at // NLO) * (2 * NX) + x_at * 2 + core_at, z_at % NLO)

    line = [None] + [device(x, y, (z + d) % NZ, core) for d in range(1, NZ)]
    plane = {}
    for way, (da, db) in STEP.items():
        sx = (1 - core) * da + core * db
        sy = core * da + (1 - core) * db
        plane[way] = device((x - sx + NX) % NX, (y - sy + NY) % NY, z, core)
    twin = device(x, y, z, 1 - core)

    barrier = pltpu.get_barrier_semaphore()
    others = [line[d] for d in (1, 2, 3, 4, 12, 13, 14, 15)] + list(plane.values()) + [twin]
    for other in others:
        pl.semaphore_signal(barrier, inc=1, device_id=other, device_id_type=pl.DeviceIdType.MESH)

    order_copy.wait()
    pos_own[...] = jnp.full((1, 128), order_own[0], jnp.int32)
    pltpu.make_async_copy(stage, stage, kv_sem).wait()
    pl.semaphore_wait(barrier, len(others))

    def remote(src, dst, send, recv, to):
        return pltpu.make_async_remote_copy(
            src_ref=src, dst_ref=dst, send_sem=send, recv_sem=recv,
            device_id=to, device_id_type=pl.DeviceIdType.MESH,
        )

    line_copies = []
    for d in (-4, -3, 3, -2, 2, -1, 1):
        at = 3 - d
        line_copies.append(remote(
            stage.at[(z + d + NZ) % KVH], landed.at[at], z_send.at[at], z_recv.at[at], line[d % NZ]
        ))
        line_copies.append(remote(
            pos_own, pos_line.at[at], p_send.at[at], p_recv.at[at], line[d % NZ]
        ))
    near_copies = list(line_copies)
    for copy in near_copies:
        copy.start()
    landed[3] = stage[head]
    pos_line[3] = pos_own[...]

    for first, there, to in ((0, HALF + 4, line[4]), (4, HALF, line[NZ - 4])):
        line_copies.append(remote(
            landed.at[pl.ds(first, 4)], landed.at[pl.ds(there, 4)],
            z_send.at[HALF + first], z_recv.at[there], to,
        ))
        line_copies.append(remote(
            pos_line.at[pl.ds(first, 4)], pos_line.at[pl.ds(there, 4)],
            p_send.at[HALF + first], p_recv.at[there], to,
        ))
    far_copies = line_copies[len(near_copies):]

    q_copy.wait()
    q_over = remote(q_raw.at[0], q_raw.at[1], t_send.at[0], t_recv.at[0], twin)
    q_over.start()

    def turn(side):
        for cc in range(4):
            rows = jnp.concatenate(
                [
                    q_raw[side, cc * TOK:(cc + 1) * TOK, g * HD:(g + 1) * HD]
                    for g in range(GROUP)
                ],
                axis=0,
            )
            token = lax.broadcasted_iota(jnp.int32, (HD, 256), 0)
            lane = lax.broadcasted_iota(jnp.int32, (HD, 256), 1)
            q_t[side * 4 + cc, 0:HD] = rows.T
            q_t[side * 4 + cc, HD:] = jnp.where(
                token == side * QTOK + cc * TOK + lane % TOK, 1.0, 0.0
            ).astype(BF)

    turn(0)
    q_over.wait_recv()
    turn(1)
    acc[...] = jnp.zeros_like(acc)
    top[...] = jnp.full_like(top, MASKED)

    lane16 = lax.broadcasted_iota(jnp.int32, (TOK, 128), 1)

    def collect(wave):
        for copy in (near_copies, far_copies)[wave]:
            copy.wait_recv()
        if wave == 0:
            for copy in far_copies:
                copy.start()
        slot = SLOT[(0, 0, wave)]
        places = [wave * HALF + d for d in range(HALF)]
        starts = jnp.concatenate([pos_line[d] for d in places * 2], axis=0)
        mine[slot, BKEYS + HD:] = jnp.where(
            lane16 < 64, starts // 128, starts % 128
        ).astype(F32).astype(BF)
        for d in range(HALF):
            mine[slot, d * TOK:(d + 1) * TOK] = landed[wave * HALF + d, 0]
        mine[slot, BKEYS:BKEYS + HD] = jnp.concatenate([landed[d, 1] for d in places], axis=0).T

    def route(n):
        slot, way, there = ROUTES[n]
        return remote(mine.at[slot], mine.at[there], f_send.at[n], m_recv.at[there], plane[way])

    def wait_mine(slot):
        pltpu.make_async_copy(mine.at[slot], mine.at[slot], m_recv.at[slot]).wait()

    def pass_on(slot):
        for n in range(len(ROUTES)):
            if ROUTES[n][0] == slot:
                route(n).start()

    collect(0)
    pass_on(0)

    lane1 = lax.broadcasted_iota(jnp.int32, (1, 128), 1)
    token_pos = jnp.zeros((1, 128), jnp.int32)
    for cc in range(4):
        token_pos = jnp.where(
            (lane1 % QTOK) // TOK == cc,
            pos_line[cc - head + 3] + lane1 % TOK, token_pos,
        )
    q_pos[0] = token_pos
    pos_over = remote(q_pos.at[0], q_pos.at[1], t_send.at[1], t_recv.at[1], twin)
    pos_over.start()

    def receive(first, last):
        for slot in range(first, last):
            if slot == SLOT[(0, 0, 1)]:
                collect(1)
            else:
                wait_mine(slot)
            pass_on(slot)

    early = max(2, HELD[0] - 2)
    receive(1, early)
    pos_over.wait_recv()
    limit = (
        jnp.where(lane1 < QTOK, q_pos[0], q_pos[1]) - lax.broadcasted_iota(jnp.int32, (TOK, 128), 0)
    ).astype(F32)

    def augmented(slot):
        word = mine[slot, BKEYS + HD:].astype(F32)
        turned = pltpu.roll(word, 64, 1)
        start = jnp.where(lane16 < 64, word * 128.0 + turned, turned * 128.0 + word)
        bias = jnp.concatenate(
            [jnp.where(start[d:d + 1, :] <= limit, 0.0, MASKED).astype(BF) for d in range(HALF)],
            axis=0,
        )
        return jnp.concatenate([mine[slot, 0:BKEYS], bias], axis=1)

    def keys_of(s):
        return jnp.concatenate([augmented(2 * s), augmented(2 * s + 1)], axis=0)

    def values_of(s):
        parts = [mine[2 * s + k, BKEYS:BKEYS + HD] for k in (0, 1)]
        return jnp.concatenate(
            [jnp.concatenate(parts, axis=1), jnp.ones((TOK, KEYS), BF)], axis=0
        )

    def score(cc, keys, into, peak):
        scores = jnp.dot(keys, q_t[cc], preferred_element_type=F32)
        into[cc] = scores
        peak[cc] = jnp.max(scores, axis=0, keepdims=True)

    def absorb(cc, values, source, peak):
        old = top[cc]
        new = jnp.maximum(old, peak[cc])
        probs = jnp.exp2((source[cc] - new) * RATE).astype(BF)
        acc[cc] = acc[cc] * jnp.exp2((old - new) * RATE) + jnp.dot(
            values, probs, preferred_element_type=F32
        )
        top[cc] = new

    def step(s, source, peak, into, into_peak, between):
        for part in range(2):
            between(part)
            if part == 0:
                keys = keys_of(s + 1)
                values = values_of(s)
            for cc in range(4 * part, 4 * part + 4):
                score(cc, keys, into, into_peak)
                absorb(cc, values, source, peak)

    keys = keys_of(0)
    for cc in range(ROWS):
        score(cc, keys, even, peak_even)
    held = [early] + HELD
    step(
        0, even, peak_even, odd, peak_odd, lambda part: receive(held[part], held[part + 1])
    )

    def pair(i, carry):
        for k in range(2):
            def between(part):
                for v in range(7):
                    at = 2 * (2 * v + 1 + k) + part
                    if held[at] < held[at + 1]:
                        @pl.when(i == v)
                        def _():
                            receive(held[at], held[at + 1])

            s = 2 * i + 1 + k
            if k == 0:
                step(s, odd, peak_odd, even, peak_even, between)
            else:
                step(s, even, peak_even, odd, peak_odd, between)
        return carry

    lax.fori_loop(0, 7, pair, 0)

    values = values_of(15)
    over = []
    for cc in range(4):
        absorb(4 + cc, values, odd, peak_odd)
        half_send[cc] = acc[4 + cc, 0:HD].astype(BF)
        stat_send[2 * cc] = acc[4 + cc, HD:HD + 1]
        stat_send[2 * cc + 1] = top[4 + cc]
        over.append((
            remote(half_send.at[cc], half_recv.at[cc], h_send.at[2 * cc], h_recv.at[2 * cc], twin),
            remote(
                stat_send.at[pl.ds(2 * cc, 2)], stat_recv.at[pl.ds(2 * cc, 2)],
                h_send.at[2 * cc + 1], h_recv.at[2 * cc + 1], twin,
            ),
        ))
        for copy in over[-1]:
            copy.start()
    for cc in range(4):
        absorb(cc, values, odd, peak_odd)

    columns = pl.ds(pl.multiple_of(head * WIDTH, WIDTH), WIDTH)
    out_copies = []
    for j in (2, 1, 3, 0):
        cc = (head + j) % KVH
        for kind, (sent, got) in enumerate((
            (half_send.at[cc], half_recv.at[cc]),
            (stat_send.at[pl.ds(2 * cc, 2)], stat_recv.at[pl.ds(2 * cc, 2)]),
        )):
            remote(sent, got, h_send.at[2 * cc + kind], h_recv.at[2 * cc + kind], twin).wait_recv()
        own = top[cc]
        other = stat_recv[2 * cc + 1]
        new = jnp.maximum(own, other)
        own_part = jnp.exp2((own - new) * RATE)
        other_part = jnp.exp2((other - new) * RATE)
        total = acc[cc, HD:HD + 1] * own_part + stat_recv[2 * cc] * other_part
        own_part = own_part / total
        other_part = other_part / total
        done = (acc[cc, 0:HD] * own_part + half_recv[cc].astype(F32) * other_part).T.astype(BF)
        for g in range(GROUP):
            out_stage[j, :, g * HD:(g + 1) * HD] = done[g * TOK:(g + 1) * TOK, :]
        if j == 0:
            out_copies.append(pltpu.make_async_copy(
                out_stage.at[j], out_ref.at[:, columns], o_send.at[j]
            ))
        else:
            to = device(x, y, (z // KVH) * KVH + cc, core)
            out_copies.append(remote(
                out_stage.at[j], out_ref.at[:, columns], o_send.at[j], o_recv.at[j], to
            ))
        out_copies[-1].start()
    for copy in line_copies:
        copy.wait_send()
    for n in range(len(ROUTES)):
        route(n).wait_send()
    q_over.wait_send()
    pos_over.wait_send()
    for copies in over:
        for copy in copies:
            copy.wait_send()
    for j in (1, 2, 3):
        source = (head - j + KVH) % KVH
        place = out_ref.at[:, pl.ds(pl.multiple_of(source * WIDTH, WIDTH), WIDTH)]
        pltpu.make_async_copy(place, place, o_recv.at[j]).wait()
    for copy in out_copies[:3]:
        copy.wait_send()
    out_copies[3].wait()


def shards(queries, keys, values, order):
    dma = pltpu.SemaphoreType.DMA
    return pl.pallas_call(
        kernel,
        out_shape=jax.ShapeDtypeStruct((TOK, KVH * WIDTH), BF),
        in_specs=[pl.BlockSpec(memory_space=pl.ANY)] * 4,
        out_specs=pl.BlockSpec(memory_space=pl.ANY),
        scratch_shapes=[
            pltpu.VMEM((BLOCKS, BLOCK, HD), BF),
            pltpu.VMEM((KVH, 2, TOK, HD), BF),
            pltpu.VMEM((NZ, 2, TOK, HD), BF),
            pltpu.SMEM((TOK,), jnp.int32),
            pltpu.VMEM((1, 128), jnp.int32),
            pltpu.VMEM((NZ, 1, 128), jnp.int32),
            pltpu.VMEM((2, QTOK, WIDTH), BF),
            pltpu.VMEM((2, 1, 128), jnp.int32),
            pltpu.VMEM((ROWS, 2 * HD, 256), BF),
            pltpu.VMEM((ROWS, KEYS, 256), F32),
            pltpu.VMEM((ROWS, KEYS, 256), F32),
            pltpu.VMEM((ROWS, 1, 256), F32),
            pltpu.VMEM((ROWS, 1, 256), F32),
            pltpu.VMEM((ROWS, HD + TOK, 256), F32),
            pltpu.VMEM((ROWS, 1, 256), F32),
            pltpu.VMEM((4, HD, 256), BF),
            pltpu.VMEM((4, HD, 256), BF),
            pltpu.VMEM((8, 1, 256), F32),
            pltpu.VMEM((8, 1, 256), F32),
            pltpu.VMEM((4, TOK, WIDTH), BF),
            dma, dma, dma,
            dma((NZ,)), dma((NZ,)), dma((NZ,)), dma((NZ,)),
            dma((len(ROUTES),)), dma((BLOCKS,)), dma((2,)), dma((2,)),
            dma((8,)), dma((8,)), dma((4,)), dma((4,)),
        ],
        compiler_params=pltpu.CompilerParams(
            collective_id=0, has_side_effects=True, vmem_limit_bytes=60 * 1024 * 1024
        ),
        cost_estimate=pl.CostEstimate(
            flops=4 * 1024 * 8192 * 128, bytes_accessed=1 << 20, transcendentals=1024 * 8192
        ),
    )(queries, keys, values, order)


def solution(mesh):
    return jax.shard_map(
        shards,
        mesh=mesh,
        in_specs=(
            P("row", None),
            P(("row", "col"), None),
            P(("row", "col"), None),
            P(("row", "col")),
        ),
        out_specs=P(("row", "col"), None),
        check_vma=False,
    )
```

```python
import math

import jax
import jax.numpy as jnp
from jax import lax
from jax.experimental import pallas as pl
from jax.experimental.pallas import tpu as pltpu
from jax.sharding import PartitionSpec as P

HD = 128
KVH = 4
GROUP = 16
TOK = 16
NX, NY, NZ, NLO = 4, 4, 16, 8
QTOK = 64
WIDTH = GROUP * HD
HALF = 8
BKEYS = HALF * TOK
BLOCK = BKEYS + HD + TOK
KEYS = 2 * BKEYS
ROWS = 8
BF = jnp.bfloat16
F32 = jnp.float32
MASKED = -1e30
RATE = math.log2(math.e) / math.sqrt(HD)

ORDER = [
    (0, 0, 0), (1, 0, 0), (3, 0, 0), (0, 3, 0), (0, 0, 1), (1, 3, 0), (0, 1, 0), (3, 3, 0),
    (2, 0, 0), (1, 1, 0), (3, 0, 1), (3, 1, 0), (0, 3, 1), (0, 1, 1), (1, 0, 1), (2, 3, 0),
    (0, 2, 0), (2, 0, 1), (3, 3, 1), (2, 1, 0), (0, 2, 1), (3, 1, 1), (1, 3, 1), (1, 2, 0),
    (3, 2, 0), (2, 3, 1), (1, 1, 1), (3, 2, 1), (2, 1, 1), (1, 2, 1), (2, 2, 0), (2, 2, 1),
]
HELD = [
    4, 4, 6, 6, 10, 10, 11, 11, 12, 12,
    14, 16, 16, 16, 18, 18, 20, 20, 24, 24,
    24, 26, 26, 26, 28, 28, 30, 30, 32, 32,
]
BLOCKS = len(ORDER)
SLOT = {place: index for index, place in enumerate(ORDER)}
STEP = {"A-": (1, 0), "A+": (-1, 0), "B-": (0, 1), "B+": (0, -1)}


def onward(a, b, wave):
    ways = []
    if b == 0:
        if a == 0:
            ways += ["A-", "A+"]
        if (a, wave) == (1, 0):
            ways.append("A-")
        if (a, wave) == (3, 1):
            ways.append("A+")
        ways += ["B-", "B+"]
    if (b, wave) == (1, 0):
        ways.append("B-")
    if (b, wave) == (3, 1):
        ways.append("B+")
    return ways


ROUTES = []
for place in ORDER:
    for way in onward(*place):
        da, db = STEP[way]
        there = ((place[0] + da) % 4, (place[1] + db) % 4, place[2])
        ROUTES.append((SLOT[place], way, SLOT[there]))


def kernel(
    q_hbm, k_hbm, v_hbm, order_hbm, out_ref,
    mine, stage, landed, order_own, pos_own, pos_line, q_raw, q_pos, q_t,
    even, odd, peak_even, peak_odd, acc, top, half_send, half_recv, stat_send, stat_recv, out_stage,
    q_sem, kv_sem, order_sem,
    z_send, z_recv, p_send, p_recv, f_send, m_recv, t_send, t_recv, h_send, h_recv, o_send, o_recv,
):
    row = lax.axis_index("row")
    col = lax.axis_index("col")
    core = row % 2
    x = (row // 2) % NX
    y = row // (4 * NX)
    z = ((row // (2 * NX)) % 2) * NLO + col
    head = col % KVH
    half = col // KVH

    order_copy = pltpu.make_async_copy(order_hbm, order_own, order_sem)
    order_copy.start()
    for g in range(KVH):
        columns = slice(g * HD, (g + 1) * HD)
        pltpu.make_async_copy(k_hbm.at[:, columns], stage.at[g, 0], kv_sem).start()
        pltpu.make_async_copy(v_hbm.at[:, columns], stage.at[g, 1], kv_sem).start()
    q_copy = pltpu.make_async_copy(
        q_hbm.at[pl.ds(half * QTOK, QTOK), pl.ds(pl.multiple_of(head * WIDTH, WIDTH), WIDTH)],
        q_raw.at[0], q_sem,
    )
    q_copy.start()

    def device(x_at, y_at, z_at, core_at):
        return (y_at * (4 * NX) + (z_at // NLO) * (2 * NX) + x_at * 2 + core_at, z_at % NLO)

    line = [None] + [device(x, y, (z + d) % NZ, core) for d in range(1, NZ)]
    plane = {}
    for way, (da, db) in STEP.items():
        sx = (1 - core) * da + core * db
        sy = core * da + (1 - core) * db
        plane[way] = device((x - sx + NX) % NX, (y - sy + NY) % NY, z, core)
    twin = device(x, y, z, 1 - core)

    barrier = pltpu.get_barrier_semaphore()
    others = [line[d] for d in (1, 2, 3, 4, 12, 13, 14, 15)] + list(plane.values()) + [twin]
    for other in others:
        pl.semaphore_signal(barrier, inc=1, device_id=other, device_id_type=pl.DeviceIdType.MESH)

    order_copy.wait()
    pos_own[...] = jnp.full((1, 128), order_own[0], jnp.int32)
    pltpu.make_async_copy(stage, stage, kv_sem).wait()
    pl.semaphore_wait(barrier, len(others))

    def remote(src, dst, send, recv, to):
        return pltpu.make_async_remote_copy(
            src_ref=src, dst_ref=dst, send_sem=send, recv_sem=recv,
            device_id=to, device_id_type=pl.DeviceIdType.MESH,
        )

    line_copies = []
    for d in (-4, -3, 3, -2, 2, -1, 1):
        at = 3 - d
        line_copies.append(remote(
            stage.at[(z + d + NZ) % KVH], landed.at[at], z_send.at[at], z_recv.at[at], line[d % NZ]
        ))
        line_copies.append(remote(
            pos_own, pos_line.at[at], p_send.at[at], p_recv.at[at], line[d % NZ]
        ))
    near_copies = list(line_copies)
    for copy in near_copies:
        copy.start()
    landed[3] = stage[head]
    pos_line[3] = pos_own[...]

    for first, there, to in ((0, HALF + 4, line[4]), (4, HALF, line[NZ - 4])):
        line_copies.append(remote(
            landed.at[pl.ds(first, 4)], landed.at[pl.ds(there, 4)],
            z_send.at[HALF + first], z_recv.at[there], to,
        ))
        line_copies.append(remote(
            pos_line.at[pl.ds(first, 4)], pos_line.at[pl.ds(there, 4)],
            p_send.at[HALF + first], p_recv.at[there], to,
        ))
    far_copies = line_copies[len(near_copies):]

    q_copy.wait()
    q_over = remote(q_raw.at[0], q_raw.at[1], t_send.at[0], t_recv.at[0], twin)
    q_over.start()

    def turn(side):
        for cc in range(4):
            rows = jnp.concatenate(
                [
                    q_raw[side, cc * TOK:(cc + 1) * TOK, g * HD:(g + 1) * HD]
                    for g in range(GROUP)
                ],
                axis=0,
            )
            token = lax.broadcasted_iota(jnp.int32, (HD, 256), 0)
            lane = lax.broadcasted_iota(jnp.int32, (HD, 256), 1)
            q_t[side * 4 + cc, 0:HD] = rows.T
            q_t[side * 4 + cc, HD:] = jnp.where(
                token == side * QTOK + cc * TOK + lane % TOK, 1.0, 0.0
            ).astype(BF)

    turn(0)
    acc[...] = jnp.zeros_like(acc)
    top[...] = jnp.full_like(top, MASKED)

    lane16 = lax.broadcasted_iota(jnp.int32, (TOK, 128), 1)

    def collect(wave):
        if wave == 0:
            for first, pairs in ((0, (2, 4, 6)), (2, (5, 3, 1, 0))):
                for n in pairs:
                    near_copies[2 * n].wait_recv()
                    near_copies[2 * n + 1].wait_recv()
                far_copies[first].start()
                far_copies[first + 1].start()
        else:
            for copy in far_copies:
                copy.wait_recv()
        slot = SLOT[(0, 0, wave)]
        places = [wave * HALF + d for d in range(HALF)]
        starts = jnp.concatenate([pos_line[d] for d in places * 2], axis=0)
        mine[slot, BKEYS + HD:] = jnp.where(
            lane16 < 64, starts // 128, starts % 128
        ).astype(F32).astype(BF)
        for d in range(HALF):
            mine[slot, d * TOK:(d + 1) * TOK] = landed[wave * HALF + d, 0]
        mine[slot, BKEYS:BKEYS + HD] = jnp.concatenate([landed[d, 1] for d in places], axis=0).T

    def route(n):
        slot, way, there = ROUTES[n]
        return remote(mine.at[slot], mine.at[there], f_send.at[n], m_recv.at[there], plane[way])

    def wait_mine(slot):
        pltpu.make_async_copy(mine.at[slot], mine.at[slot], m_recv.at[slot]).wait()

    def pass_on(slot):
        for n in range(len(ROUTES)):
            if ROUTES[n][0] == slot:
                route(n).start()

    collect(0)
    pass_on(0)

    lane1 = lax.broadcasted_iota(jnp.int32, (1, 128), 1)
    token_pos = jnp.zeros((1, 128), jnp.int32)
    for cc in range(4):
        token_pos = jnp.where(
            (lane1 % QTOK) // TOK == cc,
            pos_line[cc - head + 3] + lane1 % TOK, token_pos,
        )
    q_pos[0] = token_pos
    pos_over = remote(q_pos.at[0], q_pos.at[1], t_send.at[1], t_recv.at[1], twin)
    pos_over.start()
    q_over.wait_recv()
    turn(1)

    def receive(first, last):
        for slot in range(first, last):
            if slot == SLOT[(0, 0, 1)]:
                collect(1)
            else:
                wait_mine(slot)
            pass_on(slot)

    early = max(2, HELD[0] - 2)
    receive(1, early)
    pos_over.wait_recv()
    limit = (
        jnp.where(lane1 < QTOK, q_pos[0], q_pos[1]) - lax.broadcasted_iota(jnp.int32, (TOK, 128), 0)
    ).astype(F32)

    def augmented(slot):
        word = mine[slot, BKEYS + HD:].astype(F32)
        turned = pltpu.roll(word, 64, 1)
        start = jnp.where(lane16 < 64, word * 128.0 + turned, turned * 128.0 + word)
        bias = jnp.concatenate(
            [jnp.where(start[d:d + 1, :] <= limit, 0.0, MASKED).astype(BF) for d in range(HALF)],
            axis=0,
        )
        return jnp.concatenate([mine[slot, 0:BKEYS], bias], axis=1)

    def keys_of(s):
        return jnp.concatenate([augmented(2 * s), augmented(2 * s + 1)], axis=0)

    def values_of(s):
        parts = [mine[2 * s + k, BKEYS:BKEYS + HD] for k in (0, 1)]
        return jnp.concatenate(
            [jnp.concatenate(parts, axis=1), jnp.ones((TOK, KEYS), BF)], axis=0
        )

    def score(cc, keys, into, peak):
        scores = jnp.dot(keys, q_t[cc], preferred_element_type=F32)
        into[cc] = scores
        peak[cc] = jnp.max(scores, axis=0, keepdims=True)

    def absorb(cc, values, source, peak):
        old = top[cc]
        new = jnp.maximum(old, peak[cc])
        probs = jnp.exp2((source[cc] - new) * RATE).astype(BF)
        acc[cc] = acc[cc] * jnp.exp2((old - new) * RATE) + jnp.dot(
            values, probs, preferred_element_type=F32
        )
        top[cc] = new

    def step(s, source, peak, into, into_peak, between):
        for part in range(2):
            between(part)
            if part == 0:
                keys = keys_of(s + 1)
                values = values_of(s)
            for cc in range(4 * part, 4 * part + 4):
                score(cc, keys, into, into_peak)
                absorb(cc, values, source, peak)

    keys = keys_of(0)
    for cc in range(ROWS):
        score(cc, keys, even, peak_even)
    held = [early] + HELD
    step(
        0, even, peak_even, odd, peak_odd, lambda part: receive(held[part], held[part + 1])
    )

    def pair(i, carry):
        for k in range(2):
            def between(part):
                for v in range(7):
                    at = 2 * (2 * v + 1 + k) + part
                    if held[at] < held[at + 1]:
                        @pl.when(i == v)
                        def _():
                            receive(held[at], held[at + 1])

            s = 2 * i + 1 + k
            if k == 0:
                step(s, odd, peak_odd, even, peak_even, between)
            else:
                step(s, even, peak_even, odd, peak_odd, between)
        return carry

    lax.fori_loop(0, 7, pair, 0)

    values = values_of(15)
    over = []
    for cc in range(4):
        absorb(4 + cc, values, odd, peak_odd)
        half_send[cc] = acc[4 + cc, 0:HD].astype(BF)
        stat_send[2 * cc] = acc[4 + cc, HD:HD + 1]
        stat_send[2 * cc + 1] = top[4 + cc]
        over.append((
            remote(half_send.at[cc], half_recv.at[cc], h_send.at[2 * cc], h_recv.at[2 * cc], twin),
            remote(
                stat_send.at[pl.ds(2 * cc, 2)], stat_recv.at[pl.ds(2 * cc, 2)],
                h_send.at[2 * cc + 1], h_recv.at[2 * cc + 1], twin,
            ),
        ))
        for copy in over[-1]:
            copy.start()
    for cc in range(4):
        absorb(cc, values, odd, peak_odd)

    columns = pl.ds(pl.multiple_of(head * WIDTH, WIDTH), WIDTH)
    out_copies = []
    for j in (2, 1, 3, 0):
        cc = (head + j) % KVH
        for kind, (sent, got) in enumerate((
            (half_send.at[cc], half_recv.at[cc]),
            (stat_send.at[pl.ds(2 * cc, 2)], stat_recv.at[pl.ds(2 * cc, 2)]),
        )):
            remote(sent, got, h_send.at[2 * cc + kind], h_recv.at[2 * cc + kind], twin).wait_recv()
        own = top[cc]
        other = stat_recv[2 * cc + 1]
        new = jnp.maximum(own, other)
        own_part = jnp.exp2((own - new) * RATE)
        other_part = jnp.exp2((other - new) * RATE)
        total = acc[cc, HD:HD + 1] * own_part + stat_recv[2 * cc] * other_part
        own_part = own_part / total
        other_part = other_part / total
        done = (acc[cc, 0:HD] * own_part + half_recv[cc].astype(F32) * other_part).T.astype(BF)
        for g in range(GROUP):
            out_stage[j, :, g * HD:(g + 1) * HD] = done[g * TOK:(g + 1) * TOK, :]
        if j == 0:
            out_copies.append(pltpu.make_async_copy(
                out_stage.at[j], out_ref.at[:, columns], o_send.at[j]
            ))
        else:
            to = device(x, y, (z // KVH) * KVH + cc, core)
            out_copies.append(remote(
                out_stage.at[j], out_ref.at[:, columns], o_send.at[j], o_recv.at[j], to
            ))
        out_copies[-1].start()
    for copy in line_copies:
        copy.wait_send()
    for n in range(len(ROUTES)):
        route(n).wait_send()
    q_over.wait_send()
    pos_over.wait_send()
    for copies in over:
        for copy in copies:
            copy.wait_send()
    for j in (1, 2, 3):
        source = (head - j + KVH) % KVH
        place = out_ref.at[:, pl.ds(pl.multiple_of(source * WIDTH, WIDTH), WIDTH)]
        pltpu.make_async_copy(place, place, o_recv.at[j]).wait()
    for copy in out_copies[:3]:
        copy.wait_send()
    out_copies[3].wait()


def shards(queries, keys, values, order):
    dma = pltpu.SemaphoreType.DMA
    return pl.pallas_call(
        kernel,
        out_shape=jax.ShapeDtypeStruct((TOK, KVH * WIDTH), BF),
        in_specs=[pl.BlockSpec(memory_space=pl.ANY)] * 4,
        out_specs=pl.BlockSpec(memory_space=pl.ANY),
        scratch_shapes=[
            pltpu.VMEM((BLOCKS, BLOCK, HD), BF),
            pltpu.VMEM((KVH, 2, TOK, HD), BF),
            pltpu.VMEM((NZ, 2, TOK, HD), BF),
            pltpu.SMEM((TOK,), jnp.int32),
            pltpu.VMEM((1, 128), jnp.int32),
            pltpu.VMEM((NZ, 1, 128), jnp.int32),
            pltpu.VMEM((2, QTOK, WIDTH), BF),
            pltpu.VMEM((2, 1, 128), jnp.int32),
            pltpu.VMEM((ROWS, 2 * HD, 256), BF),
            pltpu.VMEM((ROWS, KEYS, 256), F32),
            pltpu.VMEM((ROWS, KEYS, 256), F32),
            pltpu.VMEM((ROWS, 1, 256), F32),
            pltpu.VMEM((ROWS, 1, 256), F32),
            pltpu.VMEM((ROWS, HD + TOK, 256), F32),
            pltpu.VMEM((ROWS, 1, 256), F32),
            pltpu.VMEM((4, HD, 256), BF),
            pltpu.VMEM((4, HD, 256), BF),
            pltpu.VMEM((8, 1, 256), F32),
            pltpu.VMEM((8, 1, 256), F32),
            pltpu.VMEM((4, TOK, WIDTH), BF),
            dma, dma, dma,
            dma((NZ,)), dma((NZ,)), dma((NZ,)), dma((NZ,)),
            dma((len(ROUTES),)), dma((BLOCKS,)), dma((2,)), dma((2,)),
            dma((8,)), dma((8,)), dma((4,)), dma((4,)),
        ],
        compiler_params=pltpu.CompilerParams(
            collective_id=0, has_side_effects=True, vmem_limit_bytes=60 * 1024 * 1024
        ),
        cost_estimate=pl.CostEstimate(
            flops=4 * 1024 * 8192 * 128, bytes_accessed=1 << 20, transcendentals=1024 * 8192
        ),
    )(queries, keys, values, order)


def solution(mesh):
    return jax.shard_map(
        shards,
        mesh=mesh,
        in_specs=(
            P("row", None),
            P(("row", "col"), None),
            P(("row", "col"), None),
            P(("row", "col")),
        ),
        out_specs=P(("row", "col"), None),
        check_vma=False,
    )
```

```python
import math

import jax
import jax.numpy as jnp
from jax import lax
from jax.experimental import pallas as pl
from jax.experimental.pallas import tpu as pltpu
from jax.sharding import PartitionSpec as P

HD = 128
KVH = 4
GROUP = 16
TOK = 16
NX, NY, NZ, NLO = 4, 4, 16, 8
QTOK = 64
WIDTH = GROUP * HD
HALF = 8
BKEYS = HALF * TOK
BLOCK = BKEYS + HD + TOK
KEYS = 2 * BKEYS
ROWS = 8
BF = jnp.bfloat16
F32 = jnp.float32
MASKED = -1e30
RATE = math.log2(math.e) / math.sqrt(HD)

ORDER = [
    (0, 0, 0), (1, 0, 0), (3, 0, 0), (0, 3, 0), (0, 0, 1), (1, 3, 0), (0, 1, 0), (3, 3, 0),
    (2, 0, 0), (1, 1, 0), (3, 0, 1), (3, 1, 0), (0, 3, 1), (0, 1, 1), (1, 0, 1), (2, 3, 0),
    (0, 2, 0), (2, 0, 1), (3, 3, 1), (2, 1, 0), (0, 2, 1), (3, 1, 1), (1, 3, 1), (1, 2, 0),
    (3, 2, 0), (2, 3, 1), (1, 1, 1), (3, 2, 1), (2, 1, 1), (1, 2, 1), (2, 2, 0), (2, 2, 1),
]
HELD = [
    4, 4, 6, 6, 10, 10, 11, 11, 12, 12,
    14, 16, 16, 16, 18, 18, 20, 20, 24, 24,
    24, 26, 26, 26, 28, 28, 30, 30, 32, 32,
]
BLOCKS = len(ORDER)
SLOT = {place: index for index, place in enumerate(ORDER)}
STEP = {"A-": (1, 0), "A+": (-1, 0), "B-": (0, 1), "B+": (0, -1)}


def onward(a, b, wave):
    ways = []
    if b == 0:
        if a == 0:
            ways += ["A-", "A+"]
        if (a, wave) == (1, 0):
            ways.append("A-")
        if (a, wave) == (3, 1):
            ways.append("A+")
        ways += ["B-", "B+"]
    if (b, wave) == (1, 0):
        ways.append("B-")
    if (b, wave) == (3, 1):
        ways.append("B+")
    return ways


ROUTES = []
for place in ORDER:
    for way in onward(*place):
        da, db = STEP[way]
        there = ((place[0] + da) % 4, (place[1] + db) % 4, place[2])
        ROUTES.append((SLOT[place], way, SLOT[there]))


def kernel(
    q_hbm, k_hbm, v_hbm, order_hbm, out_ref,
    mine, stage, landed, order_own, pos_own, pos_line, q_raw, q_pos, q_t,
    even, odd, peak_even, peak_odd, acc, top, half_send, half_recv, stat_send, stat_recv, out_stage,
    q_sem, kv_sem, order_sem,
    z_send, z_recv, p_send, p_recv, f_send, m_recv, t_send, t_recv, h_send, h_recv, o_send, o_recv,
):
    row = lax.axis_index("row")
    col = lax.axis_index("col")
    core = row % 2
    x = (row // 2) % NX
    y = row // (4 * NX)
    z = ((row // (2 * NX)) % 2) * NLO + col
    head = col % KVH
    half = col // KVH

    order_copy = pltpu.make_async_copy(order_hbm, order_own, order_sem)
    order_copy.start()
    for g in range(KVH):
        columns = slice(g * HD, (g + 1) * HD)
        pltpu.make_async_copy(k_hbm.at[:, columns], stage.at[g, 0], kv_sem).start()
        pltpu.make_async_copy(v_hbm.at[:, columns], stage.at[g, 1], kv_sem).start()
    q_copy = pltpu.make_async_copy(
        q_hbm.at[pl.ds(half * QTOK, QTOK), pl.ds(pl.multiple_of(head * WIDTH, WIDTH), WIDTH)],
        q_raw.at[0], q_sem,
    )
    q_copy.start()

    def device(x_at, y_at, z_at, core_at):
        return (y_at * (4 * NX) + (z_at // NLO) * (2 * NX) + x_at * 2 + core_at, z_at % NLO)

    line = [None] + [device(x, y, (z + d) % NZ, core) for d in range(1, NZ)]
    plane = {}
    for way, (da, db) in STEP.items():
        sx = (1 - core) * da + core * db
        sy = core * da + (1 - core) * db
        plane[way] = device((x - sx + NX) % NX, (y - sy + NY) % NY, z, core)
    twin = device(x, y, z, 1 - core)

    barrier = pltpu.get_barrier_semaphore()
    others = [line[d] for d in (1, 2, 3, 4, 12, 13, 14, 15)] + list(plane.values()) + [twin]
    for other in others:
        pl.semaphore_signal(barrier, inc=1, device_id=other, device_id_type=pl.DeviceIdType.MESH)

    order_copy.wait()
    pos_own[...] = jnp.full((1, 128), order_own[0], jnp.int32)
    pltpu.make_async_copy(stage, stage, kv_sem).wait()
    pl.semaphore_wait(barrier, len(others))

    def remote(src, dst, send, recv, to):
        return pltpu.make_async_remote_copy(
            src_ref=src, dst_ref=dst, send_sem=send, recv_sem=recv,
            device_id=to, device_id_type=pl.DeviceIdType.MESH,
        )

    line_copies = []
    for d in (-4, -3, 3, -2, 2, -1, 1):
        at = 3 - d
        line_copies.append(remote(
            stage.at[(z + d + NZ) % KVH], landed.at[at], z_send.at[at], z_recv.at[at], line[d % NZ]
        ))
        line_copies.append(remote(
            pos_own, pos_line.at[at], p_send.at[at], p_recv.at[at], line[d % NZ]
        ))
    near_copies = list(line_copies)
    for copy in near_copies:
        copy.start()
    landed[3] = stage[head]
    pos_line[3] = pos_own[...]

    for first, there, to in ((0, HALF + 4, line[4]), (4, HALF, line[NZ - 4])):
        line_copies.append(remote(
            landed.at[pl.ds(first, 4)], landed.at[pl.ds(there, 4)],
            z_send.at[HALF + first], z_recv.at[there], to,
        ))
        line_copies.append(remote(
            pos_line.at[pl.ds(first, 4)], pos_line.at[pl.ds(there, 4)],
            p_send.at[HALF + first], p_recv.at[there], to,
        ))
    far_copies = line_copies[len(near_copies):]

    q_copy.wait()
    q_over = remote(q_raw.at[0], q_raw.at[1], t_send.at[0], t_recv.at[0], twin)
    q_over.start()

    def turn(side):
        for cc in range(4):
            rows = jnp.concatenate(
                [
                    q_raw[side, cc * TOK:(cc + 1) * TOK, g * HD:(g + 1) * HD]
                    for g in range(GROUP)
                ],
                axis=0,
            )
            token = lax.broadcasted_iota(jnp.int32, (HD, 256), 0)
            lane = lax.broadcasted_iota(jnp.int32, (HD, 256), 1)
            q_t[side * 4 + cc, 0:HD] = rows.T
            q_t[side * 4 + cc, HD:] = jnp.where(
                token == side * QTOK + cc * TOK + lane % TOK, 1.0, 0.0
            ).astype(BF)

    turn(0)
    q_over.wait_recv()
    turn(1)
    acc[...] = jnp.zeros_like(acc)
    top[...] = jnp.full_like(top, MASKED)

    lane16 = lax.broadcasted_iota(jnp.int32, (TOK, 128), 1)

    def collect(wave):
        for copy in (near_copies, far_copies)[wave]:
            copy.wait_recv()
        if wave == 0:
            for copy in far_copies:
                copy.start()
        slot = SLOT[(0, 0, wave)]
        places = [wave * HALF + d for d in range(HALF)]
        starts = jnp.concatenate([pos_line[d] for d in places * 2], axis=0)
        mine[slot, BKEYS + HD:] = jnp.where(
            lane16 < 64, starts // 128, starts % 128
        ).astype(F32).astype(BF)
        for d in range(HALF):
            mine[slot, d * TOK:(d + 1) * TOK] = landed[wave * HALF + d, 0]
        mine[slot, BKEYS:BKEYS + HD] = jnp.concatenate([landed[d, 1] for d in places], axis=0).T

    def route(n):
        slot, way, there = ROUTES[n]
        return remote(mine.at[slot], mine.at[there], f_send.at[n], m_recv.at[there], plane[way])

    def wait_mine(slot):
        pltpu.make_async_copy(mine.at[slot], mine.at[slot], m_recv.at[slot]).wait()

    def pass_on(slot):
        for n in range(len(ROUTES)):
            if ROUTES[n][0] == slot:
                route(n).start()

    collect(0)
    pass_on(0)

    lane1 = lax.broadcasted_iota(jnp.int32, (1, 128), 1)
    token_pos = jnp.zeros((1, 128), jnp.int32)
    for cc in range(4):
        token_pos = jnp.where(
            (lane1 % QTOK) // TOK == cc,
            pos_line[cc - head + 3] + lane1 % TOK, token_pos,
        )
    q_pos[0] = token_pos
    pos_over = remote(q_pos.at[0], q_pos.at[1], t_send.at[1], t_recv.at[1], twin)
    pos_over.start()

    def receive(first, last):
        for slot in range(first, last):
            if slot == SLOT[(0, 0, 1)]:
                collect(1)
            else:
                wait_mine(slot)
            pass_on(slot)

    early = max(2, HELD[0] - 2)
    receive(1, early)
    pos_over.wait_recv()
    limit = (
        jnp.where(lane1 < QTOK, q_pos[0], q_pos[1]) - lax.broadcasted_iota(jnp.int32, (TOK, 128), 0)
    ).astype(F32)

    def augmented(slot):
        word = mine[slot, BKEYS + HD:].astype(F32)
        turned = pltpu.roll(word, 64, 1)
        start = jnp.where(lane16 < 64, word * 128.0 + turned, turned * 128.0 + word)
        bias = jnp.concatenate(
            [jnp.where(start[d:d + 1, :] <= limit, 0.0, MASKED).astype(BF) for d in range(HALF)],
            axis=0,
        )
        return jnp.concatenate([mine[slot, 0:BKEYS], bias], axis=1)

    def keys_of(s):
        return jnp.concatenate([augmented(2 * s), augmented(2 * s + 1)], axis=0)

    def values_of(s):
        parts = [mine[2 * s + k, BKEYS:BKEYS + HD] for k in (0, 1)]
        return jnp.concatenate(
            [jnp.concatenate(parts, axis=1), jnp.ones((TOK, KEYS), BF)], axis=0
        )

    def score(cc, keys, into, peak):
        scores = jnp.dot(keys, q_t[cc], preferred_element_type=F32)
        into[cc] = scores
        peak[cc] = jnp.max(scores, axis=0, keepdims=True)

    def absorb(cc, values, source, peak):
        old = top[cc]
        new = jnp.maximum(old, peak[cc])
        probs = jnp.exp2((source[cc] - new) * RATE).astype(BF)
        acc[cc] = acc[cc] * jnp.exp2((old - new) * RATE) + jnp.dot(
            values, probs, preferred_element_type=F32
        )
        top[cc] = new

    def step(s, source, peak, into, into_peak, between):
        for part in range(2):
            between(part)
            if part == 0:
                keys = keys_of(s + 1)
                values = values_of(s)
            for cc in range(4 * part, 4 * part + 4):
                score(cc, keys, into, into_peak)
                absorb(cc, values, source, peak)

    keys = keys_of(0)
    for cc in range(ROWS):
        score(cc, keys, even, peak_even)
    held = [early] + HELD
    step(
        0, even, peak_even, odd, peak_odd, lambda part: receive(held[part], held[part + 1])
    )

    def pair(i, carry):
        for k in range(2):
            def between(part):
                for v in range(7):
                    at = 2 * (2 * v + 1 + k) + part
                    if held[at] < held[at + 1]:
                        @pl.when(i == v)
                        def _():
                            receive(held[at], held[at + 1])

            s = 2 * i + 1 + k
            if k == 0:
                step(s, odd, peak_odd, even, peak_even, between)
            else:
                step(s, even, peak_even, odd, peak_odd, between)
        return carry

    lax.fori_loop(0, 7, pair, 0)

    values = values_of(15)
    over = []
    for cc in range(4):
        absorb(4 + cc, values, odd, peak_odd)
        half_send[cc] = acc[4 + cc, 0:HD].astype(BF)
        stat_send[2 * cc] = acc[4 + cc, HD:HD + 1]
        stat_send[2 * cc + 1] = top[4 + cc]
        over.append((
            remote(half_send.at[cc], half_recv.at[cc], h_send.at[2 * cc], h_recv.at[2 * cc], twin),
            remote(
                stat_send.at[pl.ds(2 * cc, 2)], stat_recv.at[pl.ds(2 * cc, 2)],
                h_send.at[2 * cc + 1], h_recv.at[2 * cc + 1], twin,
            ),
        ))
        for copy in over[-1]:
            copy.start()
    for cc in range(4):
        absorb(cc, values, odd, peak_odd)

    columns = pl.ds(pl.multiple_of(head * WIDTH, WIDTH), WIDTH)
    out_copies = []
    for j in (2, 1, 3, 0):
        cc = (head + j) % KVH
        for kind, (sent, got) in enumerate((
            (half_send.at[cc], half_recv.at[cc]),
            (stat_send.at[pl.ds(2 * cc, 2)], stat_recv.at[pl.ds(2 * cc, 2)]),
        )):
            remote(sent, got, h_send.at[2 * cc + kind], h_recv.at[2 * cc + kind], twin).wait_recv()
        own = top[cc]
        other = stat_recv[2 * cc + 1]
        new = jnp.maximum(own, other)
        own_part = jnp.exp2((own - new) * RATE)
        other_part = jnp.exp2((other - new) * RATE)
        total = acc[cc, HD:HD + 1] * own_part + stat_recv[2 * cc] * other_part
        own_part = own_part / total
        other_part = other_part / total
        done = (acc[cc, 0:HD] * own_part + half_recv[cc].astype(F32) * other_part).T.astype(BF)
        for g in range(GROUP):
            out_stage[j, :, g * HD:(g + 1) * HD] = done[g * TOK:(g + 1) * TOK, :]
        if j == 0:
            out_copies.append(pltpu.make_async_copy(
                out_stage.at[j], out_ref.at[:, columns], o_send.at[j]
            ))
        else:
            to = device(x, y, (z // KVH) * KVH + cc, core)
            out_copies.append(remote(
                out_stage.at[j], out_ref.at[:, columns], o_send.at[j], o_recv.at[j], to
            ))
        out_copies[-1].start()
    for copy in line_copies:
        copy.wait_send()
    for n in range(len(ROUTES)):
        route(n).wait_send()
    q_over.wait_send()
    pos_over.wait_send()
    for copies in over:
        for copy in copies:
            copy.wait_send()
    for j in (1, 2, 3):
        source = (head - j + KVH) % KVH
        place = out_ref.at[:, pl.ds(pl.multiple_of(source * WIDTH, WIDTH), WIDTH)]
        pltpu.make_async_copy(place, place, o_recv.at[j]).wait()
    for copy in out_copies[:3]:
        copy.wait_send()
    out_copies[3].wait()


def shards(queries, keys, values, order):
    dma = pltpu.SemaphoreType.DMA
    return pl.pallas_call(
        kernel,
        out_shape=jax.ShapeDtypeStruct((TOK, KVH * WIDTH), BF),
        in_specs=[pl.BlockSpec(memory_space=pl.ANY)] * 4,
        out_specs=pl.BlockSpec(memory_space=pltpu.VMEM),
        scratch_shapes=[
            pltpu.VMEM((BLOCKS, BLOCK, HD), BF),
            pltpu.VMEM((KVH, 2, TOK, HD), BF),
            pltpu.VMEM((NZ, 2, TOK, HD), BF),
            pltpu.SMEM((TOK,), jnp.int32),
            pltpu.VMEM((1, 128), jnp.int32),
            pltpu.VMEM((NZ, 1, 128), jnp.int32),
            pltpu.VMEM((2, QTOK, WIDTH), BF),
            pltpu.VMEM((2, 1, 128), jnp.int32),
            pltpu.VMEM((ROWS, 2 * HD, 256), BF),
            pltpu.VMEM((ROWS, KEYS, 256), F32),
            pltpu.VMEM((ROWS, KEYS, 256), F32),
            pltpu.VMEM((ROWS, 1, 256), F32),
            pltpu.VMEM((ROWS, 1, 256), F32),
            pltpu.VMEM((ROWS, HD + TOK, 256), F32),
            pltpu.VMEM((ROWS, 1, 256), F32),
            pltpu.VMEM((4, HD, 256), BF),
            pltpu.VMEM((4, HD, 256), BF),
            pltpu.VMEM((8, 1, 256), F32),
            pltpu.VMEM((8, 1, 256), F32),
            pltpu.VMEM((4, TOK, WIDTH), BF),
            dma, dma, dma,
            dma((NZ,)), dma((NZ,)), dma((NZ,)), dma((NZ,)),
            dma((len(ROUTES),)), dma((BLOCKS,)), dma((2,)), dma((2,)),
            dma((8,)), dma((8,)), dma((4,)), dma((4,)),
        ],
        compiler_params=pltpu.CompilerParams(
            collective_id=0, has_side_effects=True, vmem_limit_bytes=60 * 1024 * 1024
        ),
        cost_estimate=pl.CostEstimate(
            flops=4 * 1024 * 8192 * 128, bytes_accessed=1 << 20, transcendentals=1024 * 8192
        ),
    )(queries, keys, values, order)


def solution(mesh):
    return jax.shard_map(
        shards,
        mesh=mesh,
        in_specs=(
            P("row", None),
            P(("row", "col"), None),
            P(("row", "col"), None),
            P(("row", "col")),
        ),
        out_specs=P(("row", "col"), None),
        check_vma=False,
    )
```
